128 devices in a mesh: ia: 16 (over z, x_hi, core), ja: 8 (over y, x_lo).
Axes of the slice: x: 4 (x_hi: 2, x_lo: 2; x = x_hi * 2 + x_lo), y: 4, z: 4, core: 2. Of those that a mesh axis runs over, the one named last changes fastest.
Arguments:
- pair: bfloat16 [512, 512, 128], P('ia', 'ja'), may hold values from -9 to 9
- cotangent: bfloat16 [512, 512, 128], P('ia', 'ja'), may hold values from -6 to 6
- norm_gain: float32 [128], replicated, may hold values from 0.25 to 1.75
- norm_shift: float32 [128], replicated, may hold values from -3 to 3
- query_weight: bfloat16 [128, 128], replicated, may hold values from -2 to 2
- key_weight: bfloat16 [128, 128], replicated, may hold values from -2 to 2
- value_weight: bfloat16 [128, 128], replicated, may hold values from -0.5 to 0.5
- gate_weight: bfloat16 [128, 128], replicated, may hold values from -0.5 to 0.5
- bias_weight: bfloat16 [128, 4], replicated, may hold values from -0.5 to 0.5
- out_weight: bfloat16 [128, 128], replicated, may hold values from -0.5 to 0.5
Outputs:
- update: bfloat16 [512, 512, 128], P('ia', 'ja')
- pair_grad: float32 [512, 512, 128], P('ia', 'ja')
The draws below stay inside these ranges and needn't reach their ends.
All inputs are finite; a program needn't handle non-finite values.
Results may differ from the reference program's by a relative error of at most 0.04.
The reference program's roundings to bfloat16 on the way (of `normed`, `bias`, `probs_b`, `gated`, `d_scores`, `grad_query` and `grad_bias`) count: a program that leaves them out, or rounds other values in their place, can miss the bound.
Values may be sent and summed in bfloat16 or wider, within the bound.
No kernel may reach another device: no remote copies, remote signals or barrier semaphores. Data moves between devices by JAX's collectives and lax.ppermute only.
A program may use at most 128 MiB of HBM per device.

```python
import math
import jax
import jax.numpy as jnp
from jax import lax

C = 128
HEADS = 4
HEAD_DIM = 32
N = 512
ROWS_J = 64
N_JA = 8


def draw_pair(key, part):
    key = jax.random.fold_in(key, 3)
    noise_key = jax.random.fold_in(key, 0)
    noise = jax.random.truncated_normal(noise_key, -6.0, 6.0, (N, N, C), jnp.float32)
    values = noise
    return values.astype(jnp.bfloat16)


def projection_draw(key):
    base = jax.random.truncated_normal(key, -4.0, 4.0, (C, HEADS * HEAD_DIM), jnp.float32) / math.sqrt(C)
    return base.astype(jnp.bfloat16)


def draw_query_weight(key, part):
    key = jax.random.fold_in(key, 5)
    return projection_draw(key)


def draw_key_weight(key, part):
    key = jax.random.fold_in(key, 7)
    return projection_draw(key)


def block_scale(own_key, extent, shards, smallest, top_value):
    loudness = 1.0
    for axis_at, shards_of in shards:
        draws = jax.random.uniform(jax.random.fold_in(jax.random.fold_in(own_key, 6), axis_at), (shards_of,), jnp.float32, smallest / len(shards), top_value / len(shards))
        loudness = loudness * jnp.repeat(jnp.exp(draws), extent[axis_at] // shards_of).reshape((-1,) + (1,) * (len(extent) - 1 - axis_at))
    return loudness


def normal_values(key, dims, scale, most, shards=(), kind=jnp.bfloat16):
    loudness = block_scale(key, dims, shards, -0.22, 0.18) if shards else 1.0
    entries = jax.random.normal(key, dims, jnp.float32) * scale * loudness
    return jnp.minimum(jnp.maximum(entries, -most), most).astype(kind)


def setup_inputs(seed: int = 0) -> dict:
    splits = jax.random.split(jax.random.key(seed), 11)
    return {
        "pair": draw_pair(jax.random.fold_in(splits[10], 71), 0),
        "cotangent": normal_values(splits[1], (N, N, C), 1.0, 6.0, ((0, 16), (1, 8))),
        "norm_gain": jnp.clip(1.0 + 0.15 * jax.random.normal(splits[2], (C,), jnp.float32), 0.25, 1.75),
        "norm_shift": normal_values(splits[3], (C,), 0.5, 3.0, (), jnp.float32),
        "query_weight": draw_query_weight(jax.random.fold_in(splits[10], 71), 0),
        "key_weight": draw_key_weight(jax.random.fold_in(splits[10], 71), 0),
        "value_weight": normal_values(splits[6], (C, HEADS * HEAD_DIM), C ** -0.5, 0.5),
        "gate_weight": normal_values(splits[7], (C, HEADS * HEAD_DIM), C ** -0.5, 0.5),
        "bias_weight": normal_values(splits[8], (C, HEADS), C ** -0.5, 0.5),
        "out_weight": normal_values(splits[9], (HEADS * HEAD_DIM, C), (HEADS * HEAD_DIM) ** -0.5, 0.5),
    }


EPSILON = 1e-05

def normalize(values, norm_gain, norm_shift):
    mean_val = lax.optimization_barrier(jnp.mean(values, axis=-1, keepdims=True))
    centred = values - mean_val
    variance = lax.optimization_barrier(jnp.mean(centred * centred, axis=-1, keepdims=True))
    return centred * lax.rsqrt(variance + EPSILON) * norm_gain + norm_shift

def reference(pair, cotangent, norm_gain, norm_shift, query_weight, key_weight, value_weight, gate_weight, bias_weight, out_weight):
    inner_width = HEADS * HEAD_DIM
    score_scale = 1.0 / math.sqrt(HEAD_DIM)
    flat_pair = pair.astype(jnp.float32).reshape(N * N, C)
    normed, norm_back = jax.vjp(lambda rows: normalize(rows, norm_gain, norm_shift), flat_pair)
    normed_b = normed.astype(jnp.bfloat16)

    def project(weight):
        return jnp.dot(normed_b, weight, preferred_element_type=jnp.float32)
    queries = project(query_weight).astype(jnp.bfloat16).reshape(N, N, HEADS, HEAD_DIM)
    keys = project(key_weight).astype(jnp.bfloat16).reshape(N, N, HEADS, HEAD_DIM)
    values = project(value_weight).astype(jnp.bfloat16).reshape(N, N, HEADS, HEAD_DIM)
    gate_act = jax.nn.sigmoid(project(gate_weight)).reshape(N, N, inner_width)
    bias = project(bias_weight).astype(jnp.bfloat16).reshape(N, N, HEADS).transpose(0, 2, 1)
    bias_f = bias.astype(jnp.float32)

    def one_row(state, inputs):
        query_row, key_row, value_row, gate_row, cot_row = inputs
        query_f = query_row.astype(jnp.float32)
        key_f = key_row.astype(jnp.float32)
        value_f = value_row.astype(jnp.float32)
        scores = jnp.einsum('jhd,khd->jhk', query_f, key_f) * score_scale + bias_f
        log_total = jax.nn.logsumexp(scores, axis=-1)
        probs = jnp.exp(scores - log_total[..., None])
        probs_b = probs.astype(jnp.bfloat16)
        attended = jnp.einsum('jhk,khd->jhd', probs_b.astype(jnp.float32), value_f).reshape(N, inner_width)
        gated = (gate_row * attended).astype(jnp.bfloat16)
        update_row = jnp.dot(gated, out_weight, preferred_element_type=jnp.float32).astype(jnp.bfloat16)
        d_gated = jnp.dot(cot_row, out_weight.T, preferred_element_type=jnp.float32)
        d_att = (d_gated * gate_row).astype(jnp.bfloat16)
        d_gate_pre = (d_gated * attended * gate_row * (1.0 - gate_row)).astype(jnp.bfloat16)
        d_att_f = d_att.astype(jnp.float32).reshape(N, HEADS, HEAD_DIM)
        diag_term = lax.optimization_barrier(jnp.sum(d_att_f * attended.reshape(N, HEADS, HEAD_DIM), axis=-1))
        d_probs = jnp.einsum('jhd,khd->jhk', d_att_f, value_f)
        d_scores = (probs * (d_probs - diag_term[..., None])).astype(jnp.bfloat16)
        d_scores_f = d_scores.astype(jnp.float32)
        grad_query = (jnp.einsum('jhk,khd->jhd', d_scores_f, key_f) * score_scale).astype(jnp.bfloat16).reshape(N, inner_width)
        score_blocks = d_scores_f.reshape(N_JA, ROWS_J, HEADS, N)
        key_parts = jnp.einsum('bjhk,bjhd->bkhd', score_blocks, query_f.reshape(N_JA, ROWS_J, HEADS, HEAD_DIM)) * score_scale
        key_parts = lax.optimization_barrier(key_parts.astype(jnp.bfloat16)).astype(jnp.float32)
        grad_key = lax.optimization_barrier(jnp.sum(key_parts, axis=0)).astype(jnp.bfloat16).reshape(N, inner_width)
        prob_blocks = probs_b.astype(jnp.float32).reshape(N_JA, ROWS_J, HEADS, N)
        value_parts = jnp.einsum('bjhk,bjhd->bkhd', prob_blocks, d_att_f.reshape(N_JA, ROWS_J, HEADS, HEAD_DIM))
        value_parts = lax.optimization_barrier(value_parts.astype(jnp.bfloat16)).astype(jnp.float32)
        grad_value = lax.optimization_barrier(jnp.sum(value_parts, axis=0)).astype(jnp.bfloat16).reshape(N, inner_width)
        d_normed_row = jnp.dot(grad_query, query_weight.T, preferred_element_type=jnp.float32)
        d_normed_row = d_normed_row + jnp.dot(grad_key, key_weight.T, preferred_element_type=jnp.float32)
        d_normed_row = d_normed_row + jnp.dot(grad_value, value_weight.T, preferred_element_type=jnp.float32)
        d_normed_row = d_normed_row + jnp.dot(d_gate_pre, gate_weight.T, preferred_element_type=jnp.float32)
        return (state + d_scores_f, (update_row, d_normed_row))
    zero_bias = jnp.zeros((N, HEADS, N), jnp.float32)
    bias_sum, outputs = lax.scan(one_row, zero_bias, (queries, keys, values, gate_act, cotangent))
    update, d_normed = outputs
    grad_bias = lax.optimization_barrier(bias_sum.astype(jnp.bfloat16)).astype(jnp.float32)
    bias_term = jnp.einsum('jhk,ch->jkc', grad_bias, bias_weight.astype(jnp.float32))
    d_normed = d_normed.reshape(N * N, C) + bias_term.reshape(N * N, C)
    pair_grad = norm_back(d_normed)[0]
    return (update, pair_grad.reshape(N, N, C))
```

```python
import math

import jax
import jax.numpy as jnp
from jax import lax
from jax.experimental import pallas as pl
from jax.experimental.pallas import tpu as pltpu
from jax.sharding import Mesh, PartitionSpec as P

EPSILON = 1e-05
LOG2E = math.log2(math.e)
IA = ("z", "xh", "core")
JA = ("y", "xl")
F32 = jnp.float32
BF16 = jnp.bfloat16


def normalize(values, norm_gain, norm_shift):
    mean_val = jnp.mean(values, axis=-1, keepdims=True)
    centred = values - mean_val
    variance = jnp.mean(centred * centred, axis=-1, keepdims=True)
    return centred * lax.rsqrt(variance + EPSILON) * norm_gain + norm_shift


def mm(a, b):
    return lax.dot_general(a, b, (((1,), (0,)), ((), ())), preferred_element_type=F32)


def mm_nt(a, b):
    return lax.dot_general(a, b, (((1,), (1,)), ((), ())), preferred_element_type=F32)


def mm_tn(a, b):
    return lax.dot_general(a, b, (((0,), (0,)), ((), ())), preferred_element_type=F32)


def attention_kernel(
    heads,
    pair_ref,
    cot_ref,
    gain_ref,
    shift_ref,
    w_n_ref,
    w_t_ref,
    w_o_ref,
    bias0_ref,
    bias1_ref,
    update_ref,
    dn_ref,
    gb0_ref,
    gb1_ref,
    bias_s,
    gb_s,
    s_s,
    dp_s,
    p_s,
    ds_s,
    qt_s,
    kt_s,
    vt_s,
    dat_s,
    att_s,
    dq_s,
    dk_s,
    dv_s,
):
    row = pl.program_id(0)
    n_blocks, _, block, channels = pair_ref.shape
    n = n_blocks * block
    inner = w_o_ref.shape[0]
    head_dim = inner // heads
    scale = 1.0 / math.sqrt(head_dim)
    lanes = 128
    chunks = n // lanes
    half = heads // 2

    @pl.when(row == 0)
    def _():
        for h in range(heads):
            src = bias0_ref if h < half else bias1_ref
            hh = h % half
            for z in range(chunks):
                for b in range(n_blocks):
                    tile = src[z, b, hh * block : (hh + 1) * block, :].astype(F32)
                    bias_s[h, b * block : (b + 1) * block, z * lanes : (z + 1) * lanes] = (
                        tile * LOG2E
                    )

    x = pair_ref[...].reshape(n, channels).astype(F32)
    normed = normalize(x, gain_ref[...], shift_ref[...]).astype(BF16)
    proj = mm(normed, w_n_ref[...])
    q_n = proj[:, :inner].astype(BF16)
    k_n = proj[:, inner : 2 * inner].astype(BF16)
    v_n = proj[:, 2 * inner :].astype(BF16)
    proj_t = mm_nt(w_t_ref[...], normed)
    qt_s[...] = proj_t[:inner].astype(BF16)
    gate = jax.nn.sigmoid(proj_t[inner : 2 * inner])
    kt_s[...] = proj_t[2 * inner : 3 * inner].astype(BF16)
    vt_s[...] = proj_t[3 * inner :].astype(BF16)
    d_gated = mm_nt(w_o_ref[...], cot_ref[...].reshape(n, channels))
    dat = (d_gated * gate).astype(BF16)
    dat_s[...] = dat
    da_n = dat.T
    dk_s[...] = jnp.zeros_like(dk_s)
    dv_s[...] = jnp.zeros_like(dv_s)
    row_head = lax.broadcasted_iota(jnp.int32, (inner, n), 0) // head_dim
    lane_head = lax.broadcasted_iota(jnp.int32, (n, inner), 1) // head_dim
    step = 16

    def head_body(h, carry):
        rows = pl.ds(pl.multiple_of(h * head_dim, head_dim), head_dim)
        q_mask = jnp.where(row_head == h, qt_s[...], jnp.zeros((), BF16))
        a_mask = jnp.where(row_head == h, dat_s[...], jnp.zeros((), BF16))
        s_s[...] = mm(k_n, q_mask)
        top = jnp.full((8, n), -jnp.inf, F32)
        for k in range(0, n, step):
            t = s_s[k : k + step, :] * (scale * LOG2E) + bias_s[h, k : k + step, :]
            s_s[k : k + step, :] = t
            top = jnp.maximum(top, jnp.maximum(t[:8], t[8:]))
        top = jnp.max(top, axis=0, keepdims=True)
        total = jnp.zeros((8, n), F32)
        for k in range(0, n, step):
            p = jnp.exp2(s_s[k : k + step, :] - top)
            s_s[k : k + step, :] = p
            total = total + (p[:8] + p[8:])
        inv = 1.0 / jnp.sum(total, axis=0, keepdims=True)
        for k in range(0, n, step):
            p_s[k : k + step, :] = (s_s[k : k + step, :] * inv).astype(BF16)
        att = mm(vt_s[rows, :], p_s[...])
        att_s[rows, :] = att
        diag = jnp.sum(dat_s[rows, :].astype(F32) * att, axis=0, keepdims=True)
        dp_s[...] = mm(v_n, a_mask)
        for k in range(0, n, step):
            ds = (s_s[k : k + step, :] * inv) * (dp_s[k : k + step, :] - diag)
            gb_s[h, k : k + step, :] += ds
            ds_s[k : k + step, :] = ds.astype(BF16)
        dq_s[rows, :] = mm(kt_s[rows, :], ds_s[...])
        dk_s[...] += mm(ds_s[...], jnp.where(lane_head == h, q_n, jnp.zeros((), BF16)))
        dv_s[...] += mm(p_s[...], jnp.where(lane_head == h, da_n, jnp.zeros((), BF16)))
        return carry

    @pl.when(row == 0)
    def _():
        gb_s[...] = jnp.zeros_like(gb_s)

    lax.fori_loop(0, heads, head_body, 0)

    att = att_s[...]
    gated = (gate * att).astype(BF16)
    update = mm_tn(gated, w_o_ref[...])
    update_ref[...] = update.astype(BF16).reshape(update_ref.shape)
    d_gate = (d_gated * att * gate * (1.0 - gate)).astype(BF16)
    left_t = jnp.concatenate([(dq_s[...] * scale).astype(BF16), d_gate], axis=0)
    left = jnp.concatenate(
        [(dk_s[...] * scale).astype(BF16), dv_s[...].astype(BF16)], axis=1
    )
    dn = mm_tn(left_t, w_t_ref[: 2 * inner]) + mm(left, w_t_ref[2 * inner :])
    dn_ref[...] = dn.astype(BF16).reshape(dn_ref.shape)

    @pl.when(row == pl.num_programs(0) - 1)
    def _():
        for h in range(heads):
            dst = gb0_ref if h < half else gb1_ref
            hh = h % half
            for z in range(chunks):
                for b in range(n_blocks):
                    dst[z, b, hh * block : (hh + 1) * block, :] = gb_s[
                        h, b * block : (b + 1) * block, z * lanes : (z + 1) * lanes
                    ].astype(BF16)


def attention(heads, pair, cot, gain, shift, w_n, w_t, w_o, bias0, bias1):
    n_blocks, rows, block, channels = pair.shape
    n = n_blocks * block
    inner = w_o.shape[0]
    row_spec = pl.BlockSpec((n_blocks, 1, block, channels), lambda i: (0, i, 0, 0))

    def whole(a):
        return pl.BlockSpec(a.shape, lambda i: (0,) * len(a.shape))

    flops = 2 * 6 * rows * n * n * inner
    return pl.pallas_call(
        lambda *refs: attention_kernel(heads, *refs),
        grid=(rows,),
        in_specs=[row_spec, row_spec]
        + [whole(a) for a in (gain, shift, w_n, w_t, w_o, bias0, bias1)],
        out_specs=[row_spec, row_spec, whole(bias0), whole(bias1)],
        out_shape=[
            jax.ShapeDtypeStruct(pair.shape, BF16),
            jax.ShapeDtypeStruct(pair.shape, BF16),
            jax.ShapeDtypeStruct(bias0.shape, BF16),
            jax.ShapeDtypeStruct(bias1.shape, BF16),
        ],
        scratch_shapes=[
            pltpu.VMEM((heads, n, n), F32),
            pltpu.VMEM((heads, n, n), F32),
            pltpu.VMEM((n, n), F32),
            pltpu.VMEM((n, n), F32),
            pltpu.VMEM((n, n), BF16),
            pltpu.VMEM((n, n), BF16),
            pltpu.VMEM((inner, n), BF16),
            pltpu.VMEM((inner, n), BF16),
            pltpu.VMEM((inner, n), BF16),
            pltpu.VMEM((inner, n), BF16),
            pltpu.VMEM((inner, n), F32),
            pltpu.VMEM((inner, n), F32),
            pltpu.VMEM((n, inner), F32),
            pltpu.VMEM((n, inner), F32),
        ],
        compiler_params=pltpu.CompilerParams(vmem_limit_bytes=48 * 1024 * 1024),
        cost_estimate=pl.CostEstimate(
            flops=flops, bytes_accessed=8 * 2**20, transcendentals=rows * n * n * heads
        ),
    )(pair, cot, gain, shift, w_n, w_t, w_o, bias0, bias1)


def swap(a):
    return lax.ppermute(a, "core", [(0, 1), (1, 0)])


def shards(
    pair,
    cotangent,
    norm_gain,
    norm_shift,
    query_weight,
    key_weight,
    value_weight,
    gate_weight,
    bias_weight,
    out_weight,
):
    rows_i, rows_j, channels = pair.shape
    heads = bias_weight.shape[1]
    inner = query_weight.shape[1]
    n_ja = lax.axis_size(JA)
    n_z = lax.axis_size("z")
    n_xh = lax.axis_size("xh")
    n_core = lax.axis_size("core")
    own_i = rows_i // n_ja
    core = lax.axis_index("core")
    width = (heads // n_core) * rows_j

    pair_rows = lax.all_to_all(
        pair.reshape(n_ja, own_i, rows_j, channels), JA, 0, 0, tiled=True
    )
    cot_rows = lax.all_to_all(
        cotangent.reshape(n_ja, own_i, rows_j, channels), JA, 0, 0, tiled=True
    )

    flat_pair = pair.astype(F32).reshape(rows_i * rows_j, channels)
    normed, norm_back = jax.vjp(lambda rows: normalize(rows, norm_gain, norm_shift), flat_pair)
    bias_tile = (
        jnp.dot(normed.astype(BF16), bias_weight, preferred_element_type=F32)
        .astype(BF16)
        .reshape(rows_i, rows_j, heads)
        .transpose(0, 2, 1)
        .reshape(rows_i, n_core, width)
        .transpose(1, 0, 2)
    )
    near = lax.all_to_all(
        jnp.broadcast_to(
            bias_tile[None, :, None], (n_xh, n_core, n_ja, rows_i, width)
        ).reshape(n_xh * n_core * n_ja, rows_i, width),
        ("xh", "core", "y", "xl"),
        0,
        0,
        tiled=True,
    )
    near = (
        near.reshape(n_xh * n_core, n_ja, rows_i, width)
        .transpose(1, 3, 0, 2)
        .reshape(n_ja, width, n_xh * n_core * rows_i)
    )
    bias_own = lax.all_to_all(
        jnp.broadcast_to(near[None], (n_z,) + near.shape), "z", 0, 0, tiled=True
    )
    bias_other = swap(bias_own)

    turn = core * (inner // n_core)

    def turned(w, axis):
        return jnp.where(core == 0, w, jnp.roll(w, inner // n_core, axis))

    del turn
    w_q, w_k, w_v, w_g = (
        turned(w, 1) for w in (query_weight, key_weight, value_weight, gate_weight)
    )
    w_o = turned(out_weight, 0)
    w_n = jnp.concatenate([w_q, w_k, w_v], axis=1)
    w_t = jnp.concatenate([w_q.T, w_g.T, w_k.T, w_v.T], axis=0)

    update_rows, dn_rows, gb_own, gb_other = attention(
        heads,
        pair_rows,
        cot_rows,
        norm_gain.reshape(1, channels),
        norm_shift.reshape(1, channels),
        w_n,
        w_t,
        w_o,
        bias_own,
        bias_other,
    )

    update = lax.all_to_all(update_rows, JA, 0, 0, tiled=True).reshape(pair.shape)
    dn = lax.all_to_all(dn_rows, JA, 0, 0, tiled=True).reshape(rows_i * rows_j, channels)

    gb = (gb_own.astype(F32) + swap(gb_other).astype(F32)).astype(BF16)
    gb = lax.all_to_all(gb, "z", 0, 0, tiled=True)
    gb = jnp.sum(gb.astype(F32), axis=0).astype(BF16)
    gb = (
        gb.transpose(2, 0, 1)
        .reshape(n_xh * n_core, rows_i, n_ja, width)
        .transpose(0, 2, 1, 3)
        .reshape(n_xh * n_core * n_ja, rows_i, width)
    )
    gb = lax.all_to_all(gb, ("xh", "core", "y", "xl"), 0, 0, tiled=True)
    gb = jnp.sum(
        gb.reshape(n_xh, n_core, n_ja, rows_i, width).astype(F32), axis=(0, 2)
    ).astype(BF16)
    gb = gb.transpose(1, 0, 2).reshape(rows_i, heads, rows_j)
    bias_back = jnp.einsum("ihj,ch->ijc", gb, bias_weight, preferred_element_type=F32)
    d_normed = dn.astype(F32) + bias_back.reshape(rows_i * rows_j, channels)
    pair_grad = norm_back(d_normed)[0].reshape(rows_i, rows_j, channels)
    return (update, pair_grad)


def solution(mesh):
    fine = Mesh(mesh.devices.reshape(4, 2, 2, 4, 2), IA + JA)
    spec = P(IA, JA, None)
    in_specs = (spec, spec) + (P(),) * 8
    return jax.shard_map(
        shards, mesh=fine, in_specs=in_specs, out_specs=(spec, spec), check_vma=False
    )
```

```python
import math

import jax
import jax.numpy as jnp
from jax import lax
from jax.experimental import pallas as pl
from jax.experimental.pallas import tpu as pltpu
from jax.sharding import Mesh, PartitionSpec as P

EPSILON = 1e-05
LOG2E = math.log2(math.e)
IA = ("z", "xh", "core")
JA = ("y", "xl")
F32 = jnp.float32
BF16 = jnp.bfloat16


def normalize(values, norm_gain, norm_shift):
    mean_val = jnp.mean(values, axis=-1, keepdims=True)
    centred = values - mean_val
    variance = jnp.mean(centred * centred, axis=-1, keepdims=True)
    return centred * lax.rsqrt(variance + EPSILON) * norm_gain + norm_shift


def mm(a, b):
    return lax.dot_general(a, b, (((1,), (0,)), ((), ())), preferred_element_type=F32)


def mm_nt(a, b):
    return lax.dot_general(a, b, (((1,), (1,)), ((), ())), preferred_element_type=F32)


def mm_tn(a, b):
    return lax.dot_general(a, b, (((0,), (0,)), ((), ())), preferred_element_type=F32)


def swap(a):
    return lax.ppermute(a, "core", [(0, 1), (1, 0)])


def cross(a, bits):
    return lax.ppermute(a, ("xh", "core"), [(s, s ^ bits) for s in range(4)])


def shift(a, axis, by):
    size = lax.axis_size(axis)
    return lax.ppermute(a, axis, [(s, (s + by) % size) for s in range(size)])


def prep_kernel(pair_ref, gain_ref, shift_ref, w_ref, mine_ref, theirs_ref, tile_s):
    rows, block, channels = pair_ref.shape
    x = pair_ref[...].reshape(rows * block, channels).astype(F32)
    normed = normalize(x, gain_ref[...], shift_ref[...]).astype(BF16)
    every = mm(normed, w_ref[...])
    width = every.shape[1]
    half = width // 2
    sub = block // 2
    lane = lax.broadcasted_iota(jnp.int32, (block, width), 1)
    column = lane // half * sub + lane % sub
    keep = lax.broadcasted_iota(jnp.int32, (block, width), 0) == column
    lines = []
    for i in range(rows):
        part = jnp.where(keep, every[i * block : (i + 1) * block], 0.0)
        lines.append(jnp.sum(part, axis=0, keepdims=True))
    tile = jnp.concatenate(lines, axis=0).astype(BF16)
    tile_s[0] = tile[:, :half]
    tile_s[1] = tile[:, half:]
    core = lax.axis_index("core")
    mine_ref[...] = tile_s[core]
    theirs_ref[...] = tile_s[1 - core]


def prep(pair, gain, shift_row, w_spread):
    rows = pair.shape[0]
    half = w_spread.shape[1] // 2
    tile = jax.ShapeDtypeStruct((rows, half), BF16)
    return pl.pallas_call(
        prep_kernel,
        out_shape=[tile, tile],
        scratch_shapes=[pltpu.VMEM((2, rows, half), BF16)],
        compiler_params=pltpu.CompilerParams(vmem_limit_bytes=32 * 1024 * 1024),
        cost_estimate=pl.CostEstimate(
            flops=2**27, bytes_accessed=2**19, transcendentals=2**12
        ),
    )(pair, gain, shift_row, w_spread)


def assemble_kernel(own_ref, core_ref, far_ref, both_ref, out_ref, rows_s):
    rows = own_ref.shape[0]
    me = lax.axis_index("xh") * 2 + lax.axis_index("core")
    for bits, ref in enumerate((own_ref, core_ref, far_ref, both_ref)):
        start = pl.multiple_of((me ^ bits) * rows, rows)
        rows_s[pl.ds(start, rows), :] = ref[...]
    out_ref[...] = rows_s[...].astype(F32).T.astype(BF16)


def assemble(own, core, far, both):
    rows, width = own.shape
    return pl.pallas_call(
        assemble_kernel,
        out_shape=jax.ShapeDtypeStruct((width, 4 * rows), BF16),
        scratch_shapes=[pltpu.VMEM((4 * rows, width), BF16)],
        cost_estimate=pl.CostEstimate(flops=2**16, bytes_accessed=2**16, transcendentals=0),
    )(own, core, far, both)


def final_kernel(
    pair_ref, dn_ref, gain_ref, shift_ref, w_ref, g0_ref, g1_ref, g2_ref, g3_ref, out_ref, tile_s
):
    rows, block, channels = pair_ref.shape
    core = lax.axis_index("core")
    tile_s[core] = g0_ref[...].astype(F32) + g2_ref[...].astype(F32)
    tile_s[1 - core] = g1_ref[...].astype(F32) + g3_ref[...].astype(F32)
    tile = jnp.concatenate([tile_s[0], tile_s[1]], axis=1)
    width = tile.shape[1]
    half = width // 2
    sub = block // 2
    lane = lax.broadcasted_iota(jnp.int32, (block, width), 1)
    column = lane // half * sub + lane % sub
    keep = lax.broadcasted_iota(jnp.int32, (block, width), 0) == column
    spread = jnp.concatenate(
        [
            jnp.where(keep, jnp.broadcast_to(tile[i : i + 1], keep.shape), 0.0).astype(BF16)
            for i in range(rows)
        ],
        axis=0,
    )
    dn = dn_ref[...].reshape(rows * block, channels).astype(F32) + mm(spread, w_ref[...])
    x = pair_ref[...].reshape(rows * block, channels).astype(F32)
    centred = x - jnp.mean(x, axis=-1, keepdims=True)
    rstd = lax.rsqrt(jnp.mean(centred * centred, axis=-1, keepdims=True) + EPSILON)
    unit = centred * rstd
    push = dn * gain_ref[...]
    along = jnp.mean(push * unit, axis=-1, keepdims=True)
    level = jnp.mean(push, axis=-1, keepdims=True)
    out_ref[...] = ((push - level - unit * along) * rstd).reshape(out_ref.shape)


def final(pair, dn, gain, shift_row, w_spread, tiles):
    rows, half = tiles[0].shape
    return pl.pallas_call(
        final_kernel,
        out_shape=jax.ShapeDtypeStruct(pair.shape, F32),
        scratch_shapes=[pltpu.VMEM((2, rows, half), F32)],
        compiler_params=pltpu.CompilerParams(vmem_limit_bytes=32 * 1024 * 1024),
        cost_estimate=pl.CostEstimate(
            flops=2**27, bytes_accessed=2**21, transcendentals=2**12
        ),
    )(pair, dn, gain, shift_row, w_spread, *tiles)


def attention_kernel(
    heads,
    pair_ref,
    cot_ref,
    gain_ref,
    shift_ref,
    w_n_ref,
    w_t_ref,
    w_o_ref,
    own_ref,
    prev_ref,
    next_ref,
    opp0_ref,
    opp1_ref,
    own_ref2,
    prev_ref2,
    next_ref2,
    opp0_ref2,
    opp1_ref2,
    update_ref,
    dn_ref,
    gb_own_ref,
    gb_next_ref,
    gb_prev_ref,
    gb_opp_ref,
    gb_own_ref2,
    gb_next_ref2,
    gb_prev_ref2,
    gb_opp_ref2,
    bias_s,
    gb_s,
    s_s,
    dp_s,
    p_s,
    ds_s,
    qt_s,
    kt_s,
    vt_s,
    dat_s,
    att_s,
    dq_s,
    dk_s,
    dv_s,
):
    row = pl.program_id(0)
    n_blocks, _, block, channels = pair_ref.shape
    n = n_blocks * block
    inner = w_o_ref.shape[0]
    head_dim = inner // heads
    scale = 1.0 / math.sqrt(head_dim)
    lanes = 128
    chunks = n // lanes
    sub = block // 2
    core = lax.axis_index("core")
    z = lax.axis_index("z")
    y = lax.axis_index("y")
    xl = lax.axis_index("xl")

    def lanes_of(ahead):
        start = lax.rem(z + ahead, chunks) * lanes
        return pl.ds(pl.multiple_of(start, lanes), lanes)

    def rows_of(owner, which):
        return pl.ds(pl.multiple_of(owner * block + which * sub, sub), sub)

    @pl.when(row == 0)
    def _():
        gb_s[...] = jnp.zeros_like(gb_s)
        for which, refs in (
            (core, (own_ref, prev_ref, next_ref, opp0_ref, opp1_ref)),
            (1 - core, (own_ref2, prev_ref2, next_ref2, opp0_ref2, opp1_ref2)),
        ):
            for ahead, ref in ((0, refs[0]), (3, refs[1]), (1, refs[2]), (2, None)):
                for far in range(2):
                    for back in range(4):
                        owner = lax.rem(y + 4 - back, 4) * 2 + (xl ^ far)
                        tile = refs[3 + far][back] if ref is None else ref[far, back]
                        tile = tile.astype(F32) * LOG2E
                        for h in range(heads):
                            bias_s[h, rows_of(owner, which), lanes_of(ahead)] = tile[
                                h * sub : (h + 1) * sub
                            ]

    x = pair_ref[...].reshape(n, channels).astype(F32)
    normed = normalize(x, gain_ref[...], shift_ref[...]).astype(BF16)
    proj = mm(normed, w_n_ref[...])
    q_n = proj[:, :inner].astype(BF16)
    k_n = proj[:, inner : 2 * inner].astype(BF16)
    v_n = proj[:, 2 * inner :].astype(BF16)
    proj_t = mm_nt(w_t_ref[...], normed)
    qt_s[...] = proj_t[:inner].astype(BF16)
    gate = jax.nn.sigmoid(proj_t[inner : 2 * inner])
    kt_s[...] = proj_t[2 * inner : 3 * inner].astype(BF16)
    vt_s[...] = proj_t[3 * inner :].astype(BF16)
    d_gated = mm_nt(w_o_ref[...], cot_ref[...].reshape(n, channels))
    dat = (d_gated * gate).astype(BF16)
    dat_s[...] = dat
    da_n = dat.T
    dk_s[...] = jnp.zeros_like(dk_s)
    dv_s[...] = jnp.zeros_like(dv_s)
    row_head = lax.broadcasted_iota(jnp.int32, (inner, n), 0) // head_dim
    lane_head = lax.broadcasted_iota(jnp.int32, (n, inner), 1) // head_dim
    step = 16

    def head_body(h, carry):
        rows = pl.ds(pl.multiple_of(h * head_dim, head_dim), head_dim)
        q_mask = jnp.where(row_head == h, qt_s[...], jnp.zeros((), BF16))
        a_mask = jnp.where(row_head == h, dat_s[...], jnp.zeros((), BF16))
        s_s[...] = mm(k_n, q_mask)
        top = jnp.full((8, n), -jnp.inf, F32)
        for k in range(0, n, step):
            t = s_s[k : k + step, :] * (scale * LOG2E) + bias_s[h, k : k + step, :]
            s_s[k : k + step, :] = t
            top = jnp.maximum(top, jnp.maximum(t[:8], t[8:]))
        top = jnp.max(top, axis=0, keepdims=True)
        total = jnp.zeros((8, n), F32)
        for k in range(0, n, step):
            p = jnp.exp2(s_s[k : k + step, :] - top)
            s_s[k : k + step, :] = p
            total = total + (p[:8] + p[8:])
        inv = 1.0 / jnp.sum(total, axis=0, keepdims=True)
        for k in range(0, n, step):
            p_s[k : k + step, :] = (s_s[k : k + step, :] * inv).astype(BF16)
        att = mm(vt_s[rows, :], p_s[...])
        att_s[rows, :] = att
        diag = jnp.sum(dat_s[rows, :].astype(F32) * att, axis=0, keepdims=True)
        dp_s[...] = mm(v_n, a_mask)
        for k in range(0, n, step):
            ds = (s_s[k : k + step, :] * inv) * (dp_s[k : k + step, :] - diag)
            gb_s[h, k : k + step, :] += ds
            ds_s[k : k + step, :] = ds.astype(BF16)
        dq_s[rows, :] = mm(kt_s[rows, :], ds_s[...])
        dk_s[...] += mm(ds_s[...], jnp.where(lane_head == h, q_n, jnp.zeros((), BF16)))
        dv_s[...] += mm(p_s[...], jnp.where(lane_head == h, da_n, jnp.zeros((), BF16)))
        return carry

    lax.fori_loop(0, heads, head_body, 0)

    att = att_s[...]
    gated = (gate * att).astype(BF16)
    update = mm_tn(gated, w_o_ref[...])
    update_ref[...] = update.astype(BF16).reshape(update_ref.shape)
    d_gate = (d_gated * att * gate * (1.0 - gate)).astype(BF16)
    left_t = jnp.concatenate([(dq_s[...] * scale).astype(BF16), d_gate], axis=0)
    left = jnp.concatenate(
        [(dk_s[...] * scale).astype(BF16), dv_s[...].astype(BF16)], axis=1
    )
    dn = mm_tn(left_t, w_t_ref[: 2 * inner]) + mm(left, w_t_ref[2 * inner :])
    dn_ref[...] = dn.astype(BF16).reshape(dn_ref.shape)

    @pl.when(row == pl.num_programs(0) - 1)
    def _():
        for which, refs in (
            (core, (gb_own_ref, gb_next_ref, gb_opp_ref, gb_prev_ref)),
            (1 - core, (gb_own_ref2, gb_next_ref2, gb_opp_ref2, gb_prev_ref2)),
        ):
            for ahead, ref in enumerate(refs):
                for owner in range(n_blocks):
                    for h in range(heads):
                        ref[owner, h * sub : (h + 1) * sub, :] = gb_s[
                            h, rows_of(owner, which), lanes_of(ahead)
                        ].astype(BF16)


def attention(heads, pair, cot, gain, shift_row, w_n, w_t, w_o, bias):
    n_blocks, rows, block, channels = pair.shape
    n = n_blocks * block
    inner = w_o.shape[0]
    row_spec = pl.BlockSpec((n_blocks, 1, block, channels), lambda i: (0, i, 0, 0))

    def whole(a):
        return pl.BlockSpec(a.shape, lambda i: (0,) * len(a.shape))

    chunk = jax.ShapeDtypeStruct((n_blocks, heads * block // 2, 128), BF16)
    flops = 2 * 6 * rows * n * n * inner
    return pl.pallas_call(
        lambda *refs: attention_kernel(heads, *refs),
        grid=(rows,),
        in_specs=[row_spec, row_spec]
        + [whole(a) for a in (gain, shift_row, w_n, w_t, w_o, *bias)],
        out_specs=[row_spec, row_spec] + [whole(chunk)] * 8,
        out_shape=[
            jax.ShapeDtypeStruct(pair.shape, BF16),
            jax.ShapeDtypeStruct(pair.shape, BF16),
        ]
        + [chunk] * 8,
        scratch_shapes=[
            pltpu.VMEM((heads, n, n), F32),
            pltpu.VMEM((heads, n, n), F32),
            pltpu.VMEM((n, n), F32),
            pltpu.VMEM((n, n), F32),
            pltpu.VMEM((n, n), BF16),
            pltpu.VMEM((n, n), BF16),
            pltpu.VMEM((inner, n), BF16),
            pltpu.VMEM((inner, n), BF16),
            pltpu.VMEM((inner, n), BF16),
            pltpu.VMEM((inner, n), BF16),
            pltpu.VMEM((inner, n), F32),
            pltpu.VMEM((inner, n), F32),
            pltpu.VMEM((n, inner), F32),
            pltpu.VMEM((n, inner), F32),
        ],
        compiler_params=pltpu.CompilerParams(vmem_limit_bytes=48 * 1024 * 1024),
        cost_estimate=pl.CostEstimate(
            flops=flops, bytes_accessed=8 * 2**20, transcendentals=rows * n * n * heads
        ),
    )(pair, cot, gain, shift_row, w_n, w_t, w_o, *bias)


def shards(
    pair,
    cotangent,
    norm_gain,
    norm_shift,
    query_weight,
    key_weight,
    value_weight,
    gate_weight,
    bias_weight,
    out_weight,
):
    rows_i, rows_j, channels = pair.shape
    heads = bias_weight.shape[1]
    n_ja = lax.axis_size(JA)
    own_i = rows_i // n_ja
    sub = rows_j // 2
    gain = norm_gain.reshape(1, channels)
    shift_row = norm_shift.reshape(1, channels)
    head_of = jnp.tile(jnp.repeat(jnp.arange(heads), sub), 2)
    w_spread = bias_weight[:, head_of]

    pair_rows = lax.all_to_all(
        pair.reshape(n_ja, own_i, rows_j, channels), JA, 0, 0, tiled=True
    )
    cot_rows = lax.all_to_all(
        cotangent.reshape(n_ja, own_i, rows_j, channels), JA, 0, 0, tiled=True
    )

    mine, theirs = prep(pair, gain, shift_row, w_spread)
    tile = assemble(mine, cross(theirs, 1), cross(mine, 2), cross(theirs, 3))
    near = jnp.stack([tile] + [shift(tile, "y", d) for d in (1, 2, 3)])
    near = jnp.stack([near, lax.ppermute(near, "xl", [(0, 1), (1, 0)])])
    prev, after = shift(near, "z", 1), shift(near, "z", 3)
    opp0, opp1 = shift(prev[0], "z", 1), shift(after[1], "z", 3)
    bias = [near, prev, after, opp0, opp1]
    bias = bias + [swap(a) for a in bias]

    w_n = jnp.concatenate([query_weight, key_weight, value_weight], axis=1)
    w_t = jnp.concatenate([query_weight.T, gate_weight.T, key_weight.T, value_weight.T], axis=0)

    update_rows, dn_rows, *gb = attention(
        heads, pair_rows, cot_rows, gain, shift_row, w_n, w_t, out_weight, bias
    )

    def joined(a, b):
        return a.astype(F32) + b.astype(F32)

    opp = joined(gb[3], swap(gb[7])).astype(BF16)
    half = n_ja // 2
    via_next = shift(opp[:half], "z", 1)
    via_prev = shift(opp[half:], "z", 3)
    ahead = joined(gb[1], swap(gb[5]))
    back = joined(gb[2], swap(gb[6]))
    own = joined(gb[0], swap(gb[4]))
    zeros = jnp.zeros_like(via_next)
    ahead = ahead + jnp.concatenate([via_next, zeros], axis=0).astype(F32)
    back = back + jnp.concatenate([zeros, via_prev], axis=0).astype(F32)
    own = own + joined(shift(ahead.astype(BF16), "z", 1), shift(back.astype(BF16), "z", 3))
    own = own.astype(BF16).reshape((4, 2) + own.shape[1:])
    y = lax.axis_index("y")
    xl = lax.axis_index("xl")

    def pick(a, at):
        return lax.dynamic_index_in_dim(a, at, 0, keepdims=False)

    near = pick(own, y).astype(F32)
    for d in (1, 2, 3):
        near = near + shift(pick(own, (y + d) % 4), "y", d).astype(F32)
    near = near.astype(BF16)
    tile = joined(pick(near, xl), lax.ppermute(pick(near, 1 - xl), "xl", [(0, 1), (1, 0)]))
    tile = tile.T.astype(BF16).reshape(4, rows_i, -1)
    me = lax.axis_index("xh") * 2 + lax.axis_index("core")
    tiles = [pick(tile, me)] + [cross(pick(tile, me ^ bits), bits) for bits in (1, 2, 3)]

    update = lax.all_to_all(update_rows, JA, 0, 0, tiled=True).reshape(pair.shape)
    dn = lax.all_to_all(dn_rows, JA, 0, 0, tiled=True).reshape(pair.shape)
    pair_grad = final(pair, dn, gain, shift_row, w_spread.T, tiles)
    return (update, pair_grad)


def solution(mesh):
    fine = Mesh(mesh.devices.reshape(4, 2, 2, 4, 2), IA + JA)
    spec = P(IA, JA, None)
    in_specs = (spec, spec) + (P(),) * 8
    return jax.shard_map(
        shards, mesh=fine, in_specs=in_specs, out_specs=(spec, spec), check_vma=False
    )
```

```python
import math

import jax
import jax.numpy as jnp
from jax import lax
from jax.experimental import pallas as pl
from jax.experimental.pallas import tpu as pltpu
from jax.sharding import Mesh, PartitionSpec as P

EPSILON = 1e-05
LOG2E = math.log2(math.e)
IA = ("z", "xh", "core")
JA = ("y", "xl")
F32 = jnp.float32
BF16 = jnp.bfloat16
LANES = 128
PARAMS = pltpu.CompilerParams(vmem_limit_bytes=48 * 1024 * 1024)


def normalize(values, norm_gain, norm_shift):
    mean_val = jnp.mean(values, axis=-1, keepdims=True)
    centred = values - mean_val
    variance = jnp.mean(centred * centred, axis=-1, keepdims=True)
    return centred * lax.rsqrt(variance + EPSILON) * norm_gain + norm_shift


def mm(a, b):
    return lax.dot_general(a, b, (((1,), (0,)), ((), ())), preferred_element_type=F32)


def mm_nt(a, b):
    return lax.dot_general(a, b, (((1,), (1,)), ((), ())), preferred_element_type=F32)


def mm_tn(a, b):
    return lax.dot_general(a, b, (((0,), (0,)), ((), ())), preferred_element_type=F32)


def swap(a):
    return lax.ppermute(a, "core", [(0, 1), (1, 0)])


def cross(a, bits):
    return lax.ppermute(a, ("xh", "xl"), [(s, s ^ bits) for s in range(4)])


def shift(a, axis, by):
    size = lax.axis_size(axis)
    return lax.ppermute(a, axis, [(s, (s + by) % size) for s in range(size)])


def whole(a):
    return pl.BlockSpec(a.shape, lambda *_: (0,) * len(a.shape))


def line_mask(block, width):
    lane = lax.broadcasted_iota(jnp.int32, (block, width), 1)
    return lax.broadcasted_iota(jnp.int32, (block, width), 0) == lane % block


def prep_kernel(pair_ref, gain_ref, shift_ref, w_ref, tile_ref):
    rows, block, channels = pair_ref.shape
    x = pair_ref[...].reshape(rows * block, channels).astype(F32)
    normed = normalize(x, gain_ref[...], shift_ref[...]).astype(BF16)
    every = mm(normed, w_ref[...])
    keep = line_mask(block, every.shape[1])
    lines = []
    for i in range(rows):
        part = jnp.where(keep, every[i * block : (i + 1) * block], 0.0)
        lines.append(jnp.sum(part, axis=0, keepdims=True))
    tile_ref[...] = jnp.concatenate(lines, axis=0).astype(BF16)


def prep(pair, gain, shift_row, w_spread):
    return pl.pallas_call(
        prep_kernel,
        out_shape=jax.ShapeDtypeStruct((pair.shape[0], w_spread.shape[1]), BF16),
        compiler_params=PARAMS,
        cost_estimate=pl.CostEstimate(
            flops=2**27, bytes_accessed=2**19, transcendentals=2**12
        ),
    )(pair, gain, shift_row, w_spread)


def project_kernel(
    rows_ref, gain_ref, shift_ref, w_n_ref, w_t_ref, w_o_ref, out_n_ref, out_t_ref, out_f_ref
):
    n_blocks, _, _, block, channels = rows_ref.shape
    n = n_blocks * block
    inner = w_o_ref.shape[0]
    x = rows_ref[:, 0].reshape(n, channels).astype(F32)
    normed = normalize(x, gain_ref[...], shift_ref[...]).astype(BF16)
    out_n_ref[0, :, : 3 * inner] = mm(normed, w_n_ref[...]).astype(BF16)
    proj_t = mm_nt(w_t_ref[...], normed)
    gate = jax.nn.sigmoid(proj_t[inner : 2 * inner])
    d_gated = mm_nt(w_o_ref[...], rows_ref[:, 1].reshape(n, channels))
    d_att = (d_gated * gate).astype(BF16)
    out_t_ref[0, :inner] = proj_t[:inner].astype(BF16)
    out_t_ref[0, inner : 3 * inner] = proj_t[2 * inner :].astype(BF16)
    out_t_ref[0, 3 * inner :] = d_att
    out_n_ref[0, :, 3 * inner :] = d_att.T
    out_f_ref[0, :inner] = gate
    out_f_ref[0, inner:] = d_gated


def project(both, gain, shift_row, w_n, w_t, w_o):
    n_blocks, kinds, rows, block, channels = both.shape
    n = n_blocks * block
    inner = w_o.shape[0]
    out_n = jax.ShapeDtypeStruct((rows, n, 4 * inner), BF16)
    out_t = jax.ShapeDtypeStruct((rows, 4 * inner, n), BF16)
    out_f = jax.ShapeDtypeStruct((rows, 2 * inner, n), F32)
    return pl.pallas_call(
        project_kernel,
        grid=(rows,),
        in_specs=[
            pl.BlockSpec((n_blocks, kinds, 1, block, channels), lambda i: (0, 0, i, 0, 0))
        ]
        + [whole(a) for a in (gain, shift_row, w_n, w_t, w_o)],
        out_specs=[
            pl.BlockSpec((1,) + a.shape[1:], lambda i: (i, 0, 0)) for a in (out_n, out_t, out_f)
        ],
        out_shape=[out_n, out_t, out_f],
        compiler_params=PARAMS,
        cost_estimate=pl.CostEstimate(
            flops=2**31, bytes_accessed=8 * 2**20, transcendentals=2**18
        ),
    )(both, gain, shift_row, w_n, w_t, w_o)


def z_lanes(ahead):
    at = lax.rem(lax.axis_index("z") + ahead, lax.axis_size("z"))
    return pl.ds(pl.multiple_of(at * LANES, LANES), LANES)


def attend_kernel(heads, aheads, n_own, *refs):
    n_ref, t_ref = refs[:2]
    bias_refs = refs[2 : 2 + n_own * 2]
    refs = refs[2 + n_own * 2 :]
    count = len(aheads)
    att_refs = refs[:count]
    dq_refs = refs[count : 2 * count]
    dk_ref, dv_ref = refs[2 * count : 2 * count + 2]
    mine_refs = refs[2 * count + 2 : 3 * count + 2]
    theirs_refs = refs[3 * count + 2 : 4 * count + 2]
    bias_s, gb_s, s_s, dp_s, p_s, ds_s, tile_s, line_s = refs[4 * count + 2 :]
    row = pl.program_id(0)
    n = n_ref.shape[1]
    inner = n_ref.shape[2] // 4
    head_dim = inner // heads
    scale = 1.0 / math.sqrt(head_dim)
    n_ja, _, lines = tile_s.shape
    block = n // n_ja
    rows_i = LANES // 4
    pairs = heads // 2
    core = lax.axis_index("core")
    xh = lax.axis_index("xh")
    xl = lax.axis_index("xl")
    y = lax.axis_index("y")

    @pl.when(row == 0)
    def _():
        gb_s[...] = jnp.zeros_like(gb_s)
        parts = n_own // count
        for c in range(count):
            for which in range(2):
                base = which * n_own + c * parts
                d = 0
                for ref in bias_refs[base : base + parts]:
                    for e in range(ref.shape[0]):
                        for bits in range(4):
                            owner = lax.rem(y + 4 - d, 4) * 2 + (xl ^ (bits & 1))
                            at = (xh ^ (bits >> 1)) * 2 + (core ^ which)
                            at = pl.ds(pl.multiple_of(at * rows_i, rows_i), rows_i)
                            tile_s[owner, at, :] = ref[e, bits]
                        d += 1
            for owner in range(n_ja):
                for p in range(pairs):
                    t = tile_s[owner, :, p * LANES : (p + 1) * LANES].astype(F32).T * LOG2E
                    for e in range(2):
                        h = p * 2 + e
                        bias_s[
                            c, owner * block : (owner + 1) * block, h * LANES : (h + 1) * LANES
                        ] = t[e * block : (e + 1) * block]

    k_n = n_ref[0, :, inner : 2 * inner]
    v_n = n_ref[0, :, 2 * inner : 3 * inner]
    row_head = lax.broadcasted_iota(jnp.int32, (inner, LANES), 0) // head_dim
    lane_head = lax.broadcasted_iota(jnp.int32, (LANES, inner), 1) // head_dim
    nil = jnp.zeros((), BF16)
    step = 16
    wide = heads * LANES
    for c, ahead in enumerate(aheads):
        at = z_lanes(ahead)
        q_t = t_ref[0, :inner, at]
        a_t = t_ref[0, 3 * inner :, at]
        q_n = n_ref[0, at, :inner]
        a_n = n_ref[0, at, 3 * inner :]
        q_blk = jnp.concatenate([jnp.where(row_head == h, q_t, nil) for h in range(heads)], 1)
        a_blk = jnp.concatenate([jnp.where(row_head == h, a_t, nil) for h in range(heads)], 1)
        q_row = jnp.concatenate([jnp.where(lane_head == h, q_n, nil) for h in range(heads)], 0)
        a_row = jnp.concatenate([jnp.where(lane_head == h, a_n, nil) for h in range(heads)], 0)
        s_s[...] = mm(k_n, q_blk)
        top = jnp.full((8, wide), -jnp.inf, F32)
        for k in range(0, n, step):
            t = s_s[k : k + step, :] * (scale * LOG2E) + bias_s[c, k : k + step, :]
            s_s[k : k + step, :] = t
            top = jnp.maximum(top, jnp.maximum(t[:8], t[8:]))
        top = jnp.max(top, axis=0, keepdims=True)
        total = jnp.zeros((8, wide), F32)
        for k in range(0, n, step):
            p = jnp.exp2(s_s[k : k + step, :] - top)
            s_s[k : k + step, :] = p
            total = total + (p[:8] + p[8:])
        inv = 1.0 / jnp.sum(total, axis=0, keepdims=True)
        for k in range(0, n, step):
            p_s[k : k + step, :] = (s_s[k : k + step, :] * inv).astype(BF16)
        diag = []
        for p in range(pairs):
            rows = slice(p * 2 * head_dim, (p + 1) * 2 * head_dim)
            cols = slice(p * 2 * LANES, (p + 1) * 2 * LANES)
            att = mm(t_ref[0, 2 * inner + rows.start : 2 * inner + rows.stop, :], p_s[:, cols])
            diag.append(
                jnp.sum(a_blk[rows, cols].astype(F32) * att, axis=0, keepdims=True)
            )
            for e in range(2):
                h = p * 2 + e
                att_refs[c][0, h * head_dim : (h + 1) * head_dim, :] = att[
                    e * head_dim : (e + 1) * head_dim, e * LANES : (e + 1) * LANES
                ]
        diag = jnp.concatenate(diag, axis=1)
        dp_s[...] = mm(v_n, a_blk)
        for k in range(0, n, step):
            ds = (s_s[k : k + step, :] * inv) * (dp_s[k : k + step, :] - diag)
            gb_s[c, k : k + step, :] += ds
            ds_s[k : k + step, :] = ds.astype(BF16)
        for p in range(pairs):
            cols = slice(p * 2 * LANES, (p + 1) * 2 * LANES)
            first = inner + p * 2 * head_dim
            dq = mm(t_ref[0, first : first + 2 * head_dim, :], ds_s[:, cols]) * scale
            for e in range(2):
                h = p * 2 + e
                dq_refs[c][0, h * head_dim : (h + 1) * head_dim, :] = dq[
                    e * head_dim : (e + 1) * head_dim, e * LANES : (e + 1) * LANES
                ].astype(BF16)
        dk_c = mm(ds_s[...], q_row)
        dv_c = mm(p_s[...], a_row)
        dk = dk_c if c == 0 else dk + dk_c
        dv = dv_c if c == 0 else dv + dv_c
    dk_ref[0] = (dk * scale).astype(BF16)
    dv_ref[0] = dv.astype(BF16)

    @pl.when(row == pl.num_programs(0) - 1)
    def _():
        for c in range(count):
            for owner in range(n_ja):
                for p in range(pairs):
                    t = jnp.concatenate(
                        [
                            gb_s[
                                c,
                                owner * block : (owner + 1) * block,
                                h * LANES : (h + 1) * LANES,
                            ]
                            for h in (2 * p, 2 * p + 1)
                        ],
                        axis=0,
                    )
                    line_s[:, p * LANES : (p + 1) * LANES] = t.T.astype(BF16)
                for far in range(2):
                    for ref, which in ((mine_refs[c], core), (theirs_refs[c], 1 - core)):
                        at = pl.multiple_of((far * 2 + which) * rows_i, rows_i)
                        ref[far, owner] = line_s[pl.ds(at, rows_i), :]


def attend(heads, aheads, by_n, by_t, own, other):
    rows, n, wide = by_n.shape
    inner = wide // 4
    count = len(aheads)
    rows_i, lines = own[0].shape[2:]
    n_ja = n // (lines // heads)
    att = jax.ShapeDtypeStruct((rows, inner, LANES), F32)
    dq = jax.ShapeDtypeStruct((rows, inner, LANES), BF16)
    grad = jax.ShapeDtypeStruct((rows, n, inner), BF16)
    gb = jax.ShapeDtypeStruct((2, n_ja, rows_i, lines), BF16)

    def by_row(a):
        return pl.BlockSpec((1,) + a.shape[1:], lambda i: (i, 0, 0))

    out_shape = [att] * count + [dq] * count + [grad] * 2 + [gb] * (2 * count)
    out = pl.pallas_call(
        lambda *refs: attend_kernel(heads, aheads, len(own), *refs),
        grid=(rows,),
        in_specs=[by_row(by_n), by_row(by_t)] + [whole(a) for a in (*own, *other)],
        out_specs=[by_row(a) for a in out_shape[: 2 * count + 2]] + [whole(gb)] * (2 * count),
        out_shape=out_shape,
        scratch_shapes=[
            pltpu.VMEM((count, n, heads * LANES), F32),
            pltpu.VMEM((count, n, heads * LANES), F32),
            pltpu.VMEM((n, heads * LANES), F32),
            pltpu.VMEM((n, heads * LANES), F32),
            pltpu.VMEM((n, heads * LANES), BF16),
            pltpu.VMEM((n, heads * LANES), BF16),
            pltpu.VMEM((n_ja, LANES, lines), BF16),
            pltpu.VMEM((LANES, lines), BF16),
        ],
        compiler_params=PARAMS,
        cost_estimate=pl.CostEstimate(
            flops=count * 2**32, bytes_accessed=2**23, transcendentals=count * 2**20
        ),
    )(by_n, by_t, *own, *other)
    return (
        out[:count],
        out[count : 2 * count],
        out[2 * count],
        out[2 * count + 1],
        out[2 * count + 2 : 3 * count + 2],
        out[3 * count + 2 :],
    )


def finish_kernel(aheads, n_parts, f_ref, w_t_ref, w_o_ref, *refs):
    count = len(aheads)
    att_refs, dq_refs = refs[:count], refs[count : 2 * count]
    dk_refs = refs[2 * count : 2 * count + n_parts]
    dv_refs = refs[2 * count + n_parts : 2 * count + 2 * n_parts]
    out_ref, att_s, dq_s = refs[2 * count + 2 * n_parts :]
    inner = w_o_ref.shape[0]
    for ahead, att_ref, dq_ref in zip(aheads, att_refs, dq_refs):
        at = z_lanes(ahead)
        att_s[:, at] = att_ref[0]
        dq_s[:, at] = dq_ref[0]
    gate = f_ref[0, :inner]
    d_gated = f_ref[0, inner:]
    att = att_s[...]
    half = (out_ref.shape[0],) + out_ref.shape[2:]
    update = mm_tn((gate * att).astype(BF16), w_o_ref[...])
    out_ref[:, 0] = update.astype(BF16).reshape(half)
    d_gate = (d_gated * att * gate * (1.0 - gate)).astype(BF16)
    left_t = jnp.concatenate([dq_s[...], d_gate], axis=0)
    dk = sum(ref[0].astype(F32) for ref in dk_refs).astype(BF16)
    dv = sum(ref[0].astype(F32) for ref in dv_refs).astype(BF16)
    dn = mm_tn(left_t, w_t_ref[: 2 * inner])
    dn = dn + mm(jnp.concatenate([dk, dv], axis=1), w_t_ref[2 * inner :])
    out_ref[:, 1] = dn.astype(BF16).reshape(half)


def finish(like, aheads, by_f, w_t, w_o, att, dq, dk, dv):
    n_blocks, kinds, rows, block, channels = like.shape
    inner = w_o.shape[0]
    arrays = (*att, *dq, *dk, *dv)

    def by_row(a):
        return pl.BlockSpec((1,) + a.shape[1:], lambda i: (i, 0, 0))

    return pl.pallas_call(
        lambda *refs: finish_kernel(aheads, len(dk), *refs),
        grid=(rows,),
        in_specs=[by_row(by_f), whole(w_t), whole(w_o)] + [by_row(a) for a in arrays],
        out_specs=pl.BlockSpec(
            (n_blocks, kinds, 1, block, channels), lambda i: (0, 0, i, 0, 0)
        ),
        out_shape=jax.ShapeDtypeStruct(like.shape, BF16),
        scratch_shapes=[
            pltpu.VMEM((inner, n_blocks * block), F32),
            pltpu.VMEM((inner, n_blocks * block), BF16),
        ],
        compiler_params=PARAMS,
        cost_estimate=pl.CostEstimate(flops=2**31, bytes_accessed=2**23, transcendentals=0),
    )(by_f, w_t, w_o, *arrays)


def final_kernel(pair_ref, both_ref, gain_ref, shift_ref, w_ref, gb_ref, out_ref):
    rows, block, channels = pair_ref.shape
    tile = jnp.sum(gb_ref[...].astype(F32), axis=0).astype(BF16).astype(F32)
    keep = line_mask(block, tile.shape[1])
    spread = jnp.concatenate(
        [
            jnp.where(keep, jnp.broadcast_to(tile[i : i + 1], keep.shape), 0.0).astype(BF16)
            for i in range(rows)
        ],
        axis=0,
    )
    dn = both_ref[:, 1].reshape(rows * block, channels).astype(F32) + mm(spread, w_ref[...])
    x = pair_ref[...].reshape(rows * block, channels).astype(F32)
    centred = x - jnp.mean(x, axis=-1, keepdims=True)
    rstd = lax.rsqrt(jnp.mean(centred * centred, axis=-1, keepdims=True) + EPSILON)
    unit = centred * rstd
    push = dn * gain_ref[...]
    along = jnp.mean(push * unit, axis=-1, keepdims=True)
    level = jnp.mean(push, axis=-1, keepdims=True)
    out_ref[...] = ((push - level - unit * along) * rstd).reshape(out_ref.shape)


def final(pair, both, gain, shift_row, w_spread, gb):
    return pl.pallas_call(
        final_kernel,
        out_shape=jax.ShapeDtypeStruct(pair.shape, F32),
        compiler_params=PARAMS,
        cost_estimate=pl.CostEstimate(
            flops=2**27, bytes_accessed=2**21, transcendentals=2**12
        ),
    )(pair, both, gain, shift_row, w_spread, gb)


def shards(
    pair,
    cotangent,
    norm_gain,
    norm_shift,
    query_weight,
    key_weight,
    value_weight,
    gate_weight,
    bias_weight,
    out_weight,
):
    rows_i, rows_j, channels = pair.shape
    heads = bias_weight.shape[1]
    n_ja = lax.axis_size(JA)
    own_i = rows_i // n_ja
    gain = norm_gain.reshape(1, channels)
    shift_row = norm_shift.reshape(1, channels)
    w_spread = jnp.repeat(bias_weight, rows_j, axis=1)
    w_n = jnp.concatenate([query_weight, key_weight, value_weight], axis=1)
    w_t = jnp.concatenate([query_weight.T, gate_weight.T, key_weight.T, value_weight.T], axis=0)

    parts = (n_ja, 1, own_i, rows_j, channels)
    both = jnp.concatenate([pair.reshape(parts), cotangent.reshape(parts)], axis=1)
    both = lax.all_to_all(both, JA, 0, 0, tiled=True)

    tile = prep(pair, gain, shift_row, w_spread)
    near = jnp.stack([tile] + [cross(tile, bits) for bits in (1, 2, 3)])
    near = jnp.stack([near] + [shift(near, "y", d) for d in (1, 2, 3)])
    prev, after = shift(near, "z", 1), shift(near, "z", 3)
    opp0, opp1 = shift(prev[:2], "z", 1), shift(after[2:], "z", 3)

    by_n, by_t, by_f = project(both, gain, shift_row, w_n, w_t, out_weight)
    att0, dq0, dk0, dv0, mine0, theirs0 = attend(
        heads, (0,), by_n, by_t, [near], [swap(near)]
    )
    att1, dq1, dk1, dv1, mine1, theirs1 = attend(
        heads, (3, 1), by_n, by_t, [prev, after], [swap(prev), swap(after)]
    )
    att2, dq2, dk2, dv2, mine2, theirs2 = attend(
        heads, (2,), by_n, by_t, [opp0, opp1], [swap(opp0), swap(opp1)]
    )
    done = finish(
        both,
        (0, 3, 1, 2),
        by_f,
        w_t,
        out_weight,
        (*att0, *att1, *att2),
        (*dq0, *dq1, *dq2),
        (dk0, dk1, dk2),
        (dv0, dv1, dv2),
    )

    def joined(a, b):
        return (a.astype(F32) + b.astype(F32)).astype(BF16)

    own = joined(mine0[0], swap(theirs0[0]))
    back = shift(joined(mine1[0], swap(theirs1[0])), "z", 3)
    ahead = shift(joined(mine1[1], swap(theirs1[1])), "z", 1)
    opp = shift(joined(mine2[0], swap(theirs2[0])), "z", 2)
    gb = (own.astype(F32) + back.astype(F32) + ahead.astype(F32) + opp.astype(F32)).astype(BF16)
    gb = lax.all_to_all(
        gb.reshape((2 * n_ja,) + gb.shape[2:]), ("xh",) + JA, 0, 0, tiled=True
    )

    done = lax.all_to_all(done, JA, 0, 0, tiled=True)
    update = done[:, 0].reshape(pair.shape)
    pair_grad = final(pair, done, gain, shift_row, w_spread.T, gb)
    return (update, pair_grad)


def solution(mesh):
    fine = Mesh(mesh.devices.reshape(4, 2, 2, 4, 2), IA + JA)
    spec = P(IA, JA, None)
    in_specs = (spec, spec) + (P(),) * 8
    return jax.shard_map(
        shards, mesh=fine, in_specs=in_specs, out_specs=(spec, spec), check_vma=False
    )
```

```python
import math

import jax
import jax.numpy as jnp
from jax import lax
from jax.experimental import pallas as pl
from jax.experimental.pallas import tpu as pltpu
from jax.sharding import Mesh, PartitionSpec as P

EPSILON = 1e-05
LOG2E = math.log2(math.e)
IA = ("z", "xh", "core")
JA = ("y", "xl")
F32 = jnp.float32
BF16 = jnp.bfloat16
LANES = 128
PARAMS = pltpu.CompilerParams(vmem_limit_bytes=48 * 1024 * 1024)


def normalize(values, norm_gain, norm_shift):
    mean_val = jnp.mean(values, axis=-1, keepdims=True)
    centred = values - mean_val
    variance = jnp.mean(centred * centred, axis=-1, keepdims=True)
    return centred * lax.rsqrt(variance + EPSILON) * norm_gain + norm_shift


def mm(a, b):
    return lax.dot_general(a, b, (((1,), (0,)), ((), ())), preferred_element_type=F32)


def mm_nt(a, b):
    return lax.dot_general(a, b, (((1,), (1,)), ((), ())), preferred_element_type=F32)


def mm_tn(a, b):
    return lax.dot_general(a, b, (((0,), (0,)), ((), ())), preferred_element_type=F32)


def swap(a):
    return lax.ppermute(a, "core", [(0, 1), (1, 0)])


def cross(a, bits):
    return lax.ppermute(a, ("xh", "xl"), [(s, s ^ bits) for s in range(4)])


def shift(a, axis, by):
    size = lax.axis_size(axis)
    return lax.ppermute(a, axis, [(s, (s + by) % size) for s in range(size)])


def whole(a):
    return pl.BlockSpec(a.shape, lambda *_: (0,) * len(a.shape))


def line_mask(block, width):
    lane = lax.broadcasted_iota(jnp.int32, (block, width), 1)
    return lax.broadcasted_iota(jnp.int32, (block, width), 0) == lane % block


def prep_kernel(pair_ref, cot_ref, gain_ref, shift_ref, w_ref, out_ref):
    rows, block, channels = pair_ref.shape
    n_ja = out_ref.shape[0]
    own = rows // n_ja
    split = (n_ja, own, block, channels)
    out_ref[:, :own] = pair_ref[...].reshape(split)
    out_ref[:, own : 2 * own] = cot_ref[...].reshape(split)
    x = pair_ref[...].reshape(rows * block, channels).astype(F32)
    normed = normalize(x, gain_ref[...], shift_ref[...]).astype(BF16)
    every = mm(normed, w_ref[...])
    width = every.shape[1]
    keep = line_mask(block, width)
    lines = []
    for i in range(rows):
        part = jnp.where(keep, every[i * block : (i + 1) * block], 0.0)
        lines.append(jnp.sum(part, axis=0, keepdims=True))
    tile = jnp.concatenate(lines, axis=0).astype(BF16)
    tile = jnp.concatenate([tile[:, :LANES], tile[:, LANES:]], axis=0)
    for d in range(n_ja):
        out_ref[d, 2 * own] = tile


def prep(pair, cot, gain, shift_row, w_spread, n_ja):
    rows, block, channels = pair.shape
    out = jax.ShapeDtypeStruct((n_ja, 2 * rows // n_ja + 1, block, channels), BF16)
    return pl.pallas_call(
        prep_kernel,
        out_shape=out,
        compiler_params=PARAMS,
        cost_estimate=pl.CostEstimate(
            flops=2**27, bytes_accessed=2**21, transcendentals=2**12
        ),
    )(pair, cot, gain, shift_row, w_spread)


def project_kernel(
    pair_ref, cot_ref, gain_ref, shift_ref, w_n_ref, w_t_ref, w_o_ref, out_n_ref, out_t_ref, out_f_ref
):
    n_blocks, _, block, channels = pair_ref.shape
    n = n_blocks * block
    inner = w_o_ref.shape[0]
    x = pair_ref[...].reshape(n, channels).astype(F32)
    normed = normalize(x, gain_ref[...], shift_ref[...]).astype(BF16)
    out_n_ref[0, :, : 3 * inner] = mm(normed, w_n_ref[...]).astype(BF16)
    proj_t = mm_nt(w_t_ref[...], normed)
    gate = jax.nn.sigmoid(proj_t[inner : 2 * inner])
    d_gated = mm_nt(w_o_ref[...], cot_ref[...].reshape(n, channels))
    d_att = (d_gated * gate).astype(BF16)
    out_t_ref[0, :inner] = proj_t[:inner].astype(BF16)
    out_t_ref[0, inner : 3 * inner] = proj_t[2 * inner :].astype(BF16)
    out_t_ref[0, 3 * inner :] = d_att
    out_n_ref[0, :, 3 * inner :] = d_att.T
    out_f_ref[0, :inner] = gate
    out_f_ref[0, inner:] = d_gated


def project(both, gain, shift_row, w_n, w_t, w_o):
    n_blocks, slabs, block, channels = both.shape
    rows = slabs // 2
    n = n_blocks * block
    inner = w_o.shape[0]
    out_n = jax.ShapeDtypeStruct((rows, n, 4 * inner), BF16)
    out_t = jax.ShapeDtypeStruct((rows, 4 * inner, n), BF16)
    out_f = jax.ShapeDtypeStruct((rows, 2 * inner, n), F32)
    return pl.pallas_call(
        project_kernel,
        grid=(rows,),
        in_specs=[
            pl.BlockSpec((n_blocks, 1, block, channels), lambda i: (0, i, 0, 0)),
            pl.BlockSpec((n_blocks, 1, block, channels), lambda i: (0, rows + i, 0, 0)),
        ]
        + [whole(a) for a in (gain, shift_row, w_n, w_t, w_o)],
        out_specs=[
            pl.BlockSpec((1,) + a.shape[1:], lambda i: (i, 0, 0)) for a in (out_n, out_t, out_f)
        ],
        out_shape=[out_n, out_t, out_f],
        compiler_params=PARAMS,
        cost_estimate=pl.CostEstimate(
            flops=2**31, bytes_accessed=8 * 2**20, transcendentals=2**18
        ),
    )(both, both, gain, shift_row, w_n, w_t, w_o)


def z_lanes(ahead):
    at = lax.rem(lax.axis_index("z") + ahead, lax.axis_size("z"))
    return pl.ds(pl.multiple_of(at * LANES, LANES), LANES)


def attend_kernel(heads, aheads, n_own, *refs):
    n_ref, t_ref = refs[:2]
    bias_refs = refs[2 : 2 + n_own * 2]
    refs = refs[2 + n_own * 2 :]
    count = len(aheads)
    att_refs = refs[:count]
    dq_refs = refs[count : 2 * count]
    dk_ref, dv_ref = refs[2 * count : 2 * count + 2]
    mine_refs = refs[2 * count + 2 : 3 * count + 2]
    theirs_refs = refs[3 * count + 2 : 4 * count + 2]
    bias_s, gb_s, s_s, dp_s, p_s, ds_s, tile_s, line_s = refs[4 * count + 2 :]
    row = pl.program_id(0)
    n = n_ref.shape[1]
    inner = n_ref.shape[2] // 4
    head_dim = inner // heads
    scale = 1.0 / math.sqrt(head_dim)
    n_ja, _, lines = tile_s.shape
    block = n // n_ja
    rows_i = LANES // 4
    pairs = heads // 2
    core = lax.axis_index("core")
    xh = lax.axis_index("xh")

    @pl.when(row == 0)
    def _():
        gb_s[...] = jnp.zeros_like(gb_s)
        parts = n_own // count
        for c in range(count):
            for which in range(2):
                base = which * n_own + c * parts
                far = 0
                for ref in bias_refs[base : base + parts]:
                    for e in range(ref.shape[0]):
                        at = (xh ^ far) * 2 + (core ^ which)
                        at = pl.ds(pl.multiple_of(at * rows_i, rows_i), rows_i)
                        for owner in range(n_ja):
                            for p in range(pairs):
                                tile_s[owner, at, p * LANES : (p + 1) * LANES] = ref[
                                    e, owner, p * rows_i : (p + 1) * rows_i, :
                                ]
                        far += 1
            for owner in range(n_ja):
                for p in range(pairs):
                    t = tile_s[owner, :, p * LANES : (p + 1) * LANES].astype(F32).T * LOG2E
                    for e in range(2):
                        h = p * 2 + e
                        bias_s[
                            c, owner * block : (owner + 1) * block, h * LANES : (h + 1) * LANES
                        ] = t[e * block : (e + 1) * block]

    k_n = n_ref[0, :, inner : 2 * inner]
    v_n = n_ref[0, :, 2 * inner : 3 * inner]
    row_head = lax.broadcasted_iota(jnp.int32, (inner, LANES), 0) // head_dim
    lane_head = lax.broadcasted_iota(jnp.int32, (LANES, inner), 1) // head_dim
    nil = jnp.zeros((), BF16)
    step = 16
    wide = heads * LANES
    for c, ahead in enumerate(aheads):
        at = z_lanes(ahead)
        q_t = t_ref[0, :inner, at]
        a_t = t_ref[0, 3 * inner :, at]
        q_n = n_ref[0, at, :inner]
        a_n = n_ref[0, at, 3 * inner :]
        q_blk = jnp.concatenate([jnp.where(row_head == h, q_t, nil) for h in range(heads)], 1)
        a_blk = jnp.concatenate([jnp.where(row_head == h, a_t, nil) for h in range(heads)], 1)
        q_row = jnp.concatenate([jnp.where(lane_head == h, q_n, nil) for h in range(heads)], 0)
        a_row = jnp.concatenate([jnp.where(lane_head == h, a_n, nil) for h in range(heads)], 0)
        s_s[...] = mm(k_n, q_blk)
        top = jnp.full((8, wide), -jnp.inf, F32)
        for k in range(0, n, step):
            t = s_s[k : k + step, :] * (scale * LOG2E) + bias_s[c, k : k + step, :]
            s_s[k : k + step, :] = t
            top = jnp.maximum(top, jnp.maximum(t[:8], t[8:]))
        top = jnp.max(top, axis=0, keepdims=True)
        total = jnp.zeros((8, wide), F32)
        for k in range(0, n, step):
            p = jnp.exp2(s_s[k : k + step, :] - top)
            s_s[k : k + step, :] = p
            total = total + (p[:8] + p[8:])
        inv = 1.0 / jnp.sum(total, axis=0, keepdims=True)
        for k in range(0, n, step):
            p_s[k : k + step, :] = (s_s[k : k + step, :] * inv).astype(BF16)
        diag = []
        for p in range(pairs):
            rows = slice(p * 2 * head_dim, (p + 1) * 2 * head_dim)
            cols = slice(p * 2 * LANES, (p + 1) * 2 * LANES)
            att = mm(t_ref[0, 2 * inner + rows.start : 2 * inner + rows.stop, :], p_s[:, cols])
            diag.append(
                jnp.sum(a_blk[rows, cols].astype(F32) * att, axis=0, keepdims=True)
            )
            for e in range(2):
                h = p * 2 + e
                att_refs[c][0, h * head_dim : (h + 1) * head_dim, :] = att[
                    e * head_dim : (e + 1) * head_dim, e * LANES : (e + 1) * LANES
                ]
        diag = jnp.concatenate(diag, axis=1)
        dp_s[...] = mm(v_n, a_blk)
        for k in range(0, n, step):
            ds = (s_s[k : k + step, :] * inv) * (dp_s[k : k + step, :] - diag)
            gb_s[c, k : k + step, :] += ds
            ds_s[k : k + step, :] = ds.astype(BF16)
        for p in range(pairs):
            cols = slice(p * 2 * LANES, (p + 1) * 2 * LANES)
            first = inner + p * 2 * head_dim
            dq = mm(t_ref[0, first : first + 2 * head_dim, :], ds_s[:, cols]) * scale
            for e in range(2):
                h = p * 2 + e
                dq_refs[c][0, h * head_dim : (h + 1) * head_dim, :] = dq[
                    e * head_dim : (e + 1) * head_dim, e * LANES : (e + 1) * LANES
                ].astype(BF16)
        dk_c = mm(ds_s[...], q_row)
        dv_c = mm(p_s[...], a_row)
        dk = dk_c if c == 0 else dk + dk_c
        dv = dv_c if c == 0 else dv + dv_c
    dk_ref[0] = (dk * scale).astype(BF16)
    dv_ref[0] = dv.astype(BF16)

    @pl.when(row == pl.num_programs(0) - 1)
    def _():
        for c in range(count):
            for owner in range(n_ja):
                for p in range(pairs):
                    t = jnp.concatenate(
                        [
                            gb_s[
                                c,
                                owner * block : (owner + 1) * block,
                                h * LANES : (h + 1) * LANES,
                            ]
                            for h in (2 * p, 2 * p + 1)
                        ],
                        axis=0,
                    )
                    line_s[:, p * LANES : (p + 1) * LANES] = t.T.astype(BF16)
                for far in range(2):
                    for ref, which in ((mine_refs[c], core), (theirs_refs[c], 1 - core)):
                        at = pl.multiple_of((far * 2 + which) * rows_i, rows_i)
                        for p in range(pairs):
                            ref[far, owner, p * rows_i : (p + 1) * rows_i, :] = line_s[
                                pl.ds(at, rows_i), p * LANES : (p + 1) * LANES
                            ]


def attend(heads, aheads, by_n, by_t, own, other):
    rows, n, wide = by_n.shape
    inner = wide // 4
    count = len(aheads)
    n_ja, slab, _ = own[0].shape[1:]
    lines = heads * n // n_ja
    att = jax.ShapeDtypeStruct((rows, inner, LANES), F32)
    dq = jax.ShapeDtypeStruct((rows, inner, LANES), BF16)
    grad = jax.ShapeDtypeStruct((rows, n, inner), BF16)
    gb = jax.ShapeDtypeStruct((2, n_ja, slab, LANES), BF16)

    def by_row(a):
        return pl.BlockSpec((1,) + a.shape[1:], lambda i: (i, 0, 0))

    out_shape = [att] * count + [dq] * count + [grad] * 2 + [gb] * (2 * count)
    out = pl.pallas_call(
        lambda *refs: attend_kernel(heads, aheads, len(own), *refs),
        grid=(rows,),
        in_specs=[by_row(by_n), by_row(by_t)] + [whole(a) for a in (*own, *other)],
        out_specs=[by_row(a) for a in out_shape[: 2 * count + 2]] + [whole(gb)] * (2 * count),
        out_shape=out_shape,
        scratch_shapes=[
            pltpu.VMEM((count, n, heads * LANES), F32),
            pltpu.VMEM((count, n, heads * LANES), F32),
            pltpu.VMEM((n, heads * LANES), F32),
            pltpu.VMEM((n, heads * LANES), F32),
            pltpu.VMEM((n, heads * LANES), BF16),
            pltpu.VMEM((n, heads * LANES), BF16),
            pltpu.VMEM((n_ja, LANES, lines), BF16),
            pltpu.VMEM((LANES, lines), BF16),
        ],
        compiler_params=PARAMS,
        cost_estimate=pl.CostEstimate(
            flops=count * 2**32, bytes_accessed=2**23, transcendentals=count * 2**20
        ),
    )(by_n, by_t, *own, *other)
    return (
        out[:count],
        out[count : 2 * count],
        out[2 * count],
        out[2 * count + 1],
        out[2 * count + 2 : 3 * count + 2],
        out[3 * count + 2 :],
    )


def finish_kernel(aheads, n_parts, f_ref, w_t_ref, w_o_ref, *refs):
    count = len(aheads)
    att_refs, dq_refs = refs[:count], refs[count : 2 * count]
    dk_refs = refs[2 * count : 2 * count + n_parts]
    dv_refs = refs[2 * count + n_parts : 2 * count + 2 * n_parts]
    out_ref, att_s, dq_s = refs[2 * count + 2 * n_parts :]
    inner = w_o_ref.shape[0]
    for ahead, att_ref, dq_ref in zip(aheads, att_refs, dq_refs):
        at = z_lanes(ahead)
        att_s[:, at] = att_ref[0]
        dq_s[:, at] = dq_ref[0]
    gate = f_ref[0, :inner]
    d_gated = f_ref[0, inner:]
    att = att_s[...]
    half = (out_ref.shape[0],) + out_ref.shape[2:]
    update = mm_tn((gate * att).astype(BF16), w_o_ref[...])
    out_ref[:, 0] = update.astype(BF16).reshape(half)
    d_gate = (d_gated * att * gate * (1.0 - gate)).astype(BF16)
    left_t = jnp.concatenate([dq_s[...], d_gate], axis=0)
    dk = sum(ref[0].astype(F32) for ref in dk_refs).astype(BF16)
    dv = sum(ref[0].astype(F32) for ref in dv_refs).astype(BF16)
    dn = mm_tn(left_t, w_t_ref[: 2 * inner])
    dn = dn + mm(jnp.concatenate([dk, dv], axis=1), w_t_ref[2 * inner :])
    out_ref[:, 1] = dn.astype(BF16).reshape(half)


def finish(block, aheads, by_f, w_t, w_o, att, dq, dk, dv):
    rows, _, n = by_f.shape
    inner, channels = w_o.shape
    n_blocks = n // block
    arrays = (*att, *dq, *dk, *dv)

    def by_row(a):
        return pl.BlockSpec((1,) + a.shape[1:], lambda i: (i, 0, 0))

    return pl.pallas_call(
        lambda *refs: finish_kernel(aheads, len(dk), *refs),
        grid=(rows,),
        in_specs=[by_row(by_f), whole(w_t), whole(w_o)] + [by_row(a) for a in arrays],
        out_specs=pl.BlockSpec(
            (n_blocks, 2, 1, block, channels), lambda i: (0, 0, i, 0, 0)
        ),
        out_shape=jax.ShapeDtypeStruct((n_blocks, 2, rows, block, channels), BF16),
        scratch_shapes=[
            pltpu.VMEM((inner, n_blocks * block), F32),
            pltpu.VMEM((inner, n_blocks * block), BF16),
        ],
        compiler_params=PARAMS,
        cost_estimate=pl.CostEstimate(flops=2**31, bytes_accessed=2**23, transcendentals=0),
    )(by_f, w_t, w_o, *arrays)


def arrange_x_kernel(*refs):
    ins, outs = refs[:4], refs[4:]
    xh = lax.axis_index("xh")
    xl = lax.axis_index("xl")
    for bits, out in enumerate(outs):
        for y in range(out.shape[0]):
            at = (xh ^ (bits >> 1), y * 2 + (xl ^ (bits & 1)))
            out[y] = sum(ref[at].astype(F32) for ref in ins).astype(BF16)


def arrange_y_kernel(*refs):
    ins, outs = refs[:4], refs[4:]
    size = ins[0].shape[0]
    y = lax.axis_index("y")
    for ahead, out in enumerate(outs):
        at = lax.rem(y + ahead, size)
        out[...] = sum(ref[at].astype(F32) for ref in ins).astype(BF16)


def arrange(kernel, arrays, shape):
    out = jax.ShapeDtypeStruct(shape, BF16)
    return pl.pallas_call(
        kernel,
        out_shape=[out] * 4,
        cost_estimate=pl.CostEstimate(flops=2**18, bytes_accessed=2**20, transcendentals=0),
    )(*arrays)


def final_kernel(
    pair_ref, both_ref, gain_ref, shift_ref, w_ref, g0_ref, g1_ref, g2_ref, g3_ref, out_ref
):
    rows, block, channels = pair_ref.shape
    tile = sum(ref[...].astype(F32) for ref in (g0_ref, g1_ref, g2_ref, g3_ref))
    tile = jnp.concatenate([tile[:rows], tile[rows:]], axis=1).astype(BF16).astype(F32)
    keep = line_mask(block, tile.shape[1])
    spread = jnp.concatenate(
        [
            jnp.where(keep, jnp.broadcast_to(tile[i : i + 1], keep.shape), 0.0).astype(BF16)
            for i in range(rows)
        ],
        axis=0,
    )
    dn = both_ref[:, 1].reshape(rows * block, channels).astype(F32) + mm(spread, w_ref[...])
    x = pair_ref[...].reshape(rows * block, channels).astype(F32)
    centred = x - jnp.mean(x, axis=-1, keepdims=True)
    rstd = lax.rsqrt(jnp.mean(centred * centred, axis=-1, keepdims=True) + EPSILON)
    unit = centred * rstd
    push = dn * gain_ref[...]
    along = jnp.mean(push * unit, axis=-1, keepdims=True)
    level = jnp.mean(push, axis=-1, keepdims=True)
    out_ref[...] = ((push - level - unit * along) * rstd).reshape(out_ref.shape)


def final(pair, both, gain, shift_row, w_spread, gb):
    return pl.pallas_call(
        final_kernel,
        out_shape=jax.ShapeDtypeStruct(pair.shape, F32),
        compiler_params=PARAMS,
        cost_estimate=pl.CostEstimate(
            flops=2**27, bytes_accessed=2**21, transcendentals=2**12
        ),
    )(pair, both, gain, shift_row, w_spread, *gb)


def shards(
    pair,
    cotangent,
    norm_gain,
    norm_shift,
    query_weight,
    key_weight,
    value_weight,
    gate_weight,
    bias_weight,
    out_weight,
):
    rows_i, rows_j, channels = pair.shape
    heads = bias_weight.shape[1]
    n_ja = lax.axis_size(JA)
    own_i = rows_i // n_ja
    gain = norm_gain.reshape(1, channels)
    shift_row = norm_shift.reshape(1, channels)
    w_spread = jnp.repeat(bias_weight, rows_j, axis=1)
    w_n = jnp.concatenate([query_weight, key_weight, value_weight], axis=1)
    w_t = jnp.concatenate([query_weight.T, gate_weight.T, key_weight.T, value_weight.T], axis=0)

    both = prep(pair, cotangent, gain, shift_row, w_spread, n_ja)
    both = lax.all_to_all(both, JA, 0, 0, tiled=True)

    near = both[:, 2 * own_i]
    near = jnp.stack([near, lax.ppermute(near, "xh", [(0, 1), (1, 0)])])
    prev, after = shift(near, "z", 1), shift(near, "z", 3)
    opp0, opp1 = shift(prev[0], "z", 1)[None], shift(after[1], "z", 3)[None]

    by_n, by_t, by_f = project(both, gain, shift_row, w_n, w_t, out_weight)
    slices = (
        (0, [near], [swap(near)]),
        (3, [prev], [swap(prev)]),
        (1, [after], [swap(after)]),
        (2, [opp0, opp1], [swap(opp0), swap(opp1)]),
    )
    att, dq, dk, dv, total = [], [], [], [], []
    for ahead, own, other in slices:
        if dk:
            own, other, dk[-1] = lax.optimization_barrier((own, other, dk[-1]))
        att_a, dq_a, dk_a, dv_a, mine, theirs = attend(
            heads, (ahead,), by_n, by_t, own, other
        )
        att += att_a
        dq += dq_a
        dk.append(dk_a)
        dv.append(dv_a)
        part = (mine[0].astype(F32) + swap(theirs[0]).astype(F32)).astype(BF16)
        if ahead == 2:
            part, dk[-1] = lax.optimization_barrier((part, dk[-1]))
        total.append(shift(part, "z", ahead) if ahead else part)
    done = finish(rows_j, (0, 3, 1, 2), by_f, w_t, out_weight, att, dq, dk, dv)
    done = lax.all_to_all(done, JA, 0, 0, tiled=True)

    slab = total[0].shape[2:]
    by_x = arrange(arrange_x_kernel, total, (lax.axis_size("y"),) + slab)
    by_x = [by_x[0]] + [cross(by_x[bits], bits) for bits in (1, 2, 3)]
    by_y = arrange(arrange_y_kernel, by_x, slab)
    by_y = [by_y[0]] + [shift(by_y[d], "y", d) for d in (1, 2, 3)]

    update = done[:, 0].reshape(pair.shape)
    pair_grad = final(pair, done, gain, shift_row, w_spread.T, by_y)
    return (update, pair_grad)


def solution(mesh):
    fine = Mesh(mesh.devices.reshape(4, 2, 2, 4, 2), IA + JA)
    spec = P(IA, JA, None)
    in_specs = (spec, spec) + (P(),) * 8
    return jax.shard_map(
        shards, mesh=fine, in_specs=in_specs, out_specs=(spec, spec), check_vma=False
    )
```

```python
import math

import jax
import jax.numpy as jnp
from jax import lax
from jax.experimental import pallas as pl
from jax.experimental.pallas import tpu as pltpu
from jax.sharding import Mesh, PartitionSpec as P

EPSILON = 1e-05
LOG2E = math.log2(math.e)
IA = ("z", "xh", "core")
JA = ("y", "xl")
F32 = jnp.float32
BF16 = jnp.bfloat16
LANES = 128
PARAMS = pltpu.CompilerParams(vmem_limit_bytes=48 * 1024 * 1024)


def normalize(values, norm_gain, norm_shift):
    mean_val = jnp.mean(values, axis=-1, keepdims=True)
    centred = values - mean_val
    variance = jnp.mean(centred * centred, axis=-1, keepdims=True)
    return centred * lax.rsqrt(variance + EPSILON) * norm_gain + norm_shift


def mm(a, b):
    return lax.dot_general(a, b, (((1,), (0,)), ((), ())), preferred_element_type=F32)


def mm_nt(a, b):
    return lax.dot_general(a, b, (((1,), (1,)), ((), ())), preferred_element_type=F32)


def mm_tn(a, b):
    return lax.dot_general(a, b, (((0,), (0,)), ((), ())), preferred_element_type=F32)


def swap(a):
    return lax.ppermute(a, "core", [(0, 1), (1, 0)])


def cross(a, bits):
    return lax.ppermute(a, ("xh", "xl"), [(s, s ^ bits) for s in range(4)])


def shift(a, axis, by):
    size = lax.axis_size(axis)
    return lax.ppermute(a, axis, [(s, (s + by) % size) for s in range(size)])


def whole(a):
    return pl.BlockSpec(a.shape, lambda *_: (0,) * len(a.shape))


def line_mask(block, width):
    lane = lax.broadcasted_iota(jnp.int32, (block, width), 1)
    return lax.broadcasted_iota(jnp.int32, (block, width), 0) == lane % block


def spread_heads(w_ref, block):
    w = w_ref[...].astype(F32)
    shape = (w.shape[0], block)
    cols = [jnp.broadcast_to(w[:, h : h + 1], shape) for h in range(w.shape[1])]
    return jnp.concatenate(cols, axis=1).astype(BF16)


def prep_kernel(pair_ref, gain_ref, shift_ref, w_ref, out_ref):
    rows, block, channels = pair_ref.shape
    n_ja = out_ref.shape[0]
    own = rows // n_ja
    split = (n_ja, own, block, channels)
    out_ref[:, :own] = pair_ref[...].reshape(split)
    x = pair_ref[...].reshape(rows * block, channels).astype(F32)
    normed = normalize(x, gain_ref[...], shift_ref[...]).astype(BF16)
    every = mm(normed, spread_heads(w_ref, block))
    width = every.shape[1]
    keep = line_mask(block, width)
    lines = []
    for i in range(rows):
        part = jnp.where(keep, every[i * block : (i + 1) * block], 0.0)
        lines.append(jnp.sum(part, axis=0, keepdims=True))
    tile = jnp.concatenate(lines, axis=0).astype(BF16)
    tile = jnp.concatenate([tile[:, :LANES], tile[:, LANES:]], axis=0)
    for d in range(n_ja):
        out_ref[d, own] = tile


def prep(pair, gain, shift_row, bias_weight, n_ja):
    rows, block, channels = pair.shape
    out = jax.ShapeDtypeStruct((n_ja, rows // n_ja + 1, block, channels), BF16)
    return pl.pallas_call(
        prep_kernel,
        out_shape=out,
        compiler_params=PARAMS,
        cost_estimate=pl.CostEstimate(
            flops=2**27, bytes_accessed=2**21, transcendentals=2**12
        ),
    )(pair, gain, shift_row, bias_weight)


def project_kernel(
    pair_ref, gain_ref, shift_ref, w_q_ref, w_k_ref, w_v_ref, w_g_ref, out_n_ref, out_t_ref, gate_ref
):
    n_blocks, _, block, channels = pair_ref.shape
    n = n_blocks * block
    inner = w_q_ref.shape[1]
    x = pair_ref[...].reshape(n, channels).astype(F32)
    normed = normalize(x, gain_ref[...], shift_ref[...]).astype(BF16)
    weights = [ref[...] for ref in (w_q_ref, w_k_ref, w_v_ref, w_g_ref)]
    out_n_ref[0] = mm(normed, jnp.concatenate(weights[:3], axis=1)).astype(BF16)
    proj_t = mm_nt(jnp.concatenate([w.T for w in weights], axis=0), normed)
    out_t_ref[0] = proj_t[: 3 * inner].astype(BF16)
    gate_ref[0] = jax.nn.sigmoid(proj_t[3 * inner :])


def project(both, gain, shift_row, weights):
    n_blocks, slabs, block, channels = both.shape
    rows = slabs - 1
    n = n_blocks * block
    inner = weights[0].shape[1]
    out_n = jax.ShapeDtypeStruct((rows, n, 3 * inner), BF16)
    out_t = jax.ShapeDtypeStruct((rows, 3 * inner, n), BF16)
    gate = jax.ShapeDtypeStruct((rows, inner, n), F32)
    return pl.pallas_call(
        project_kernel,
        grid=(rows,),
        in_specs=[pl.BlockSpec((n_blocks, 1, block, channels), lambda i: (0, i, 0, 0))]
        + [whole(a) for a in (gain, shift_row, *weights)],
        out_specs=[
            pl.BlockSpec((1,) + a.shape[1:], lambda i: (i, 0, 0)) for a in (out_n, out_t, gate)
        ],
        out_shape=[out_n, out_t, gate],
        compiler_params=PARAMS,
        cost_estimate=pl.CostEstimate(
            flops=2**31, bytes_accessed=8 * 2**20, transcendentals=2**18
        ),
    )(both, gain, shift_row, *weights)


def z_lanes(ahead):
    at = lax.rem(lax.axis_index("z") + ahead, lax.axis_size("z"))
    return pl.ds(pl.multiple_of(at * LANES, LANES), LANES)


def attend_kernel(
    heads,
    ahead,
    n_own,
    n_ref,
    t_ref,
    gate_ref,
    cot_ref,
    w_o_ref,
    *refs,
):
    bias_refs = refs[: n_own * 2]
    att_ref, dq_ref, dk_ref, dv_ref, mine_ref, theirs_ref = refs[n_own * 2 : n_own * 2 + 6]
    bias_s, gb_s, s_s, p_s, ds_s, tile_s, line_s = refs[n_own * 2 + 6 :]
    row = pl.program_id(0)
    n = n_ref.shape[1]
    inner = n_ref.shape[2] // 3
    head_dim = inner // heads
    scale = 1.0 / math.sqrt(head_dim)
    n_ja = tile_s.shape[0]
    block = n // n_ja
    rows_i = LANES // 4
    pairs = heads // 2
    core = lax.axis_index("core")
    xh = lax.axis_index("xh")

    @pl.when(row == 0)
    def _():
        for which in range(2):
            far = 0
            for ref in bias_refs[which * n_own : (which + 1) * n_own]:
                for e in range(ref.shape[0]):
                    at = (xh ^ far) * 2 + (core ^ which)
                    at = pl.ds(pl.multiple_of(at * rows_i, rows_i), rows_i)
                    for owner in range(n_ja):
                        for p in range(pairs):
                            tile_s[owner, at, p * LANES : (p + 1) * LANES] = ref[
                                e, owner, p * rows_i : (p + 1) * rows_i, :
                            ]
                    far += 1
        for owner in range(n_ja):
            for p in range(pairs):
                t = tile_s[owner, :, p * LANES : (p + 1) * LANES].astype(F32).T * LOG2E
                for e in range(2):
                    h = p * 2 + e
                    bias_s[
                        owner * block : (owner + 1) * block, h * LANES : (h + 1) * LANES
                    ] = t[e * block : (e + 1) * block]
        gb_s[...] = jnp.zeros_like(gb_s)

    at = z_lanes(ahead)
    nil = jnp.zeros((), BF16)
    row_head = lax.broadcasted_iota(jnp.int32, (inner, LANES), 0) // head_dim
    lane_head = lax.broadcasted_iota(jnp.int32, (LANES, inner), 1) // head_dim
    q_t = t_ref[0, :inner, at]
    q_n = n_ref[0, at, :inner]
    z = lax.rem(lax.axis_index("z") + ahead, lax.axis_size("z"))
    span = LANES // block
    cot = cot_ref[pl.ds(z * span, span), 0].reshape(LANES, cot_ref.shape[3])
    d_att = mm_nt(w_o_ref[...], cot) * gate_ref[0, :, at]
    q_row = jnp.concatenate([jnp.where(lane_head == h, q_n, nil) for h in range(heads)], 0)
    step = 16
    chunk = 128
    wide = 2 * LANES
    a_rows = []
    invs = []
    for p in range(pairs):
        cols = slice(p * wide, (p + 1) * wide)
        q_blk = jnp.concatenate(
            [jnp.where(row_head == h, q_t, nil) for h in (2 * p, 2 * p + 1)], axis=1
        )
        top = jnp.full((8, wide), -jnp.inf, F32)
        for k in range(0, n, chunk):
            t = mm(n_ref[0, k : k + chunk, inner : 2 * inner], q_blk) * (scale * LOG2E)
            t = t + bias_s[k : k + chunk, cols]
            s_s[k : k + chunk, cols] = t
            for e in range(0, chunk, 8):
                top = jnp.maximum(top, t[e : e + 8])
        top = jnp.max(top, axis=0, keepdims=True)
        total = jnp.zeros((8, wide), F32)
        for k in range(0, n, step):
            e = jnp.exp2(s_s[k : k + step, cols] - top)
            s_s[k : k + step, cols] = e
            p_s[k : k + step, cols] = e.astype(BF16)
            total = total + (e[:8] + e[8:])
        invs.append(1.0 / jnp.sum(total, axis=0, keepdims=True))
    for p in range(pairs):
        cols = slice(p * wide, (p + 1) * wide)
        first = 2 * p * head_dim
        rows = slice(first, first + 2 * head_dim)
        inv = invs[p]
        att = mm(t_ref[0, 2 * inner + first : 2 * inner + first + 2 * head_dim, :], p_s[:, cols])
        att = att * inv
        a_two = jnp.concatenate([d_att[rows], d_att[rows]], axis=1) * inv
        lane = lax.broadcasted_iota(jnp.int32, a_two.shape, 1) // LANES
        sub = lax.broadcasted_iota(jnp.int32, a_two.shape, 0) // head_dim
        a_two = jnp.where(lane == sub, a_two, 0.0).astype(BF16)
        diag = jnp.sum(a_two.astype(F32) * att, axis=0, keepdims=True)
        for e in range(2):
            h = 2 * p + e
            own = slice(h * head_dim, (h + 1) * head_dim)
            att_ref[0, own, :] = att[
                e * head_dim : (e + 1) * head_dim, e * LANES : (e + 1) * LANES
            ]
        lead = [jnp.zeros((first, wide), BF16)] if p else []
        tail = [jnp.zeros((inner - first - 2 * head_dim, wide), BF16)] if p + 1 < pairs else []
        a_blk = jnp.concatenate(lead + [a_two] + tail, axis=0)
        a_rows.append(a_blk.T)
        for k in range(0, n, chunk):
            dp = mm(n_ref[0, k : k + chunk, 2 * inner :], a_blk)
            ds = s_s[k : k + chunk, cols] * (dp - diag)
            gb_s[k : k + chunk, cols] += ds
            ds_s[k : k + chunk, cols] = ds.astype(BF16)
        dq = mm(t_ref[0, inner + first : inner + first + 2 * head_dim, :], ds_s[:, cols]) * scale
        for e in range(2):
            h = 2 * p + e
            dq_ref[0, h * head_dim : (h + 1) * head_dim, :] = dq[
                e * head_dim : (e + 1) * head_dim, e * LANES : (e + 1) * LANES
            ].astype(BF16)
    dk_ref[0] = (mm(ds_s[...], q_row) * scale).astype(BF16)
    dv_ref[0] = mm(p_s[...], jnp.concatenate(a_rows, axis=0)).astype(BF16)

    @pl.when(row == pl.num_programs(0) - 1)
    def _():
        for owner in range(n_ja):
            for p in range(pairs):
                t = jnp.concatenate(
                    [
                        gb_s[owner * block : (owner + 1) * block, h * LANES : (h + 1) * LANES]
                        for h in (2 * p, 2 * p + 1)
                    ],
                    axis=0,
                )
                line_s[:, p * LANES : (p + 1) * LANES] = t.T.astype(BF16)
            for far in range(2):
                for ref, which in ((mine_ref, core), (theirs_ref, 1 - core)):
                    at = pl.multiple_of((far * 2 + which) * rows_i, rows_i)
                    for p in range(pairs):
                        ref[far, owner, p * rows_i : (p + 1) * rows_i, :] = line_s[
                            pl.ds(at, rows_i), p * LANES : (p + 1) * LANES
                        ]


def attend(heads, ahead, by_n, by_t, gate, cot, w_o, own, other):
    rows, n, _ = by_n.shape
    inner = gate.shape[1]
    n_ja, slab, _ = own[0].shape[1:]
    lines = heads * n // n_ja
    att = jax.ShapeDtypeStruct((rows, inner, LANES), F32)
    dq = jax.ShapeDtypeStruct((rows, inner, LANES), BF16)
    grad = jax.ShapeDtypeStruct((rows, n, inner), BF16)
    gb = jax.ShapeDtypeStruct((2, n_ja, slab, LANES), BF16)

    def by_row(a):
        return pl.BlockSpec((1,) + a.shape[1:], lambda i: (i, 0, 0))

    cot_spec = pl.BlockSpec((cot.shape[0], 1) + cot.shape[2:], lambda i: (0, i, 0, 0))
    return pl.pallas_call(
        lambda *refs: attend_kernel(heads, ahead, len(own), *refs),
        grid=(rows,),
        in_specs=[by_row(by_n), by_row(by_t), by_row(gate), cot_spec, whole(w_o)]
        + [whole(a) for a in (*own, *other)],
        out_specs=[by_row(a) for a in (att, dq, grad, grad)] + [whole(gb)] * 2,
        out_shape=[att, dq, grad, grad, gb, gb],
        scratch_shapes=[
            pltpu.VMEM((n, heads * LANES), F32),
            pltpu.VMEM((n, heads * LANES), F32),
            pltpu.VMEM((n, heads * LANES), F32),
            pltpu.VMEM((n, heads * LANES), BF16),
            pltpu.VMEM((n, heads * LANES), BF16),
            pltpu.VMEM((n_ja, LANES, lines), BF16),
            pltpu.VMEM((LANES, lines), BF16),
        ],
        compiler_params=PARAMS,
        cost_estimate=pl.CostEstimate(
            flops=2**32, bytes_accessed=2**23, transcendentals=2**20
        ),
    )(by_n, by_t, gate, cot, w_o, *own, *other)


def finish_kernel(aheads, gate_ref, cot_ref, w_o_ref, w_q_ref, w_k_ref, w_v_ref, w_g_ref, *refs):
    count = len(aheads)
    att_refs, dq_refs = refs[:count], refs[count : 2 * count]
    dk_refs, dv_refs = refs[2 * count : 3 * count], refs[3 * count : 4 * count]
    out_ref, att_s, dq_s = refs[4 * count :]
    for ahead, att_ref, dq_ref in zip(aheads, att_refs, dq_refs):
        at = z_lanes(ahead)
        att_s[:, at] = att_ref[0]
        dq_s[:, at] = dq_ref[0]
    half = (out_ref.shape[0],) + out_ref.shape[2:]
    gate = gate_ref[0]
    cot = cot_ref[...].reshape(gate.shape[1], cot_ref.shape[3])
    d_gated = mm_nt(w_o_ref[...], cot)
    att = att_s[...]
    update = mm_tn((gate * att).astype(BF16), w_o_ref[...])
    out_ref[:, 0] = update.astype(BF16).reshape(half)
    d_gate = (d_gated * att * gate * (1.0 - gate)).astype(BF16)
    left_t = jnp.concatenate([dq_s[...], d_gate], axis=0)
    dk = sum(ref[0].astype(F32) for ref in dk_refs).astype(BF16)
    dv = sum(ref[0].astype(F32) for ref in dv_refs).astype(BF16)
    dn = mm_tn(left_t, jnp.concatenate([w_q_ref[...].T, w_g_ref[...].T], axis=0))
    dn = dn + mm(
        jnp.concatenate([dk, dv], axis=1),
        jnp.concatenate([w_k_ref[...].T, w_v_ref[...].T], axis=0),
    )
    out_ref[:, 1] = dn.astype(BF16).reshape(half)


def finish(aheads, gate, cot, w_o, weights, att, dq, dk, dv):
    n_blocks, rows, block, channels = cot.shape
    inner = w_o.shape[0]
    arrays = (*att, *dq, *dk, *dv)

    def by_row(a):
        return pl.BlockSpec((1,) + a.shape[1:], lambda i: (i, 0, 0))

    cot_spec = pl.BlockSpec((n_blocks, 1, block, channels), lambda i: (0, i, 0, 0))
    return pl.pallas_call(
        lambda *refs: finish_kernel(aheads, *refs),
        grid=(rows,),
        in_specs=[by_row(gate), cot_spec, whole(w_o)]
        + [whole(a) for a in weights]
        + [by_row(a) for a in arrays],
        out_specs=pl.BlockSpec(
            (n_blocks, 2, 1, block, channels), lambda i: (0, 0, i, 0, 0)
        ),
        out_shape=jax.ShapeDtypeStruct((n_blocks, 2, rows, block, channels), BF16),
        scratch_shapes=[
            pltpu.VMEM((inner, n_blocks * block), F32),
            pltpu.VMEM((inner, n_blocks * block), BF16),
        ],
        compiler_params=PARAMS,
        cost_estimate=pl.CostEstimate(flops=2**31, bytes_accessed=2**23, transcendentals=0),
    )(gate, cot, w_o, *weights, *arrays)


def arrange_x_kernel(*refs):
    ins, outs = refs[:4], refs[4:]
    xh = lax.axis_index("xh")
    xl = lax.axis_index("xl")
    for bits, out in enumerate(outs):
        for y in range(out.shape[0]):
            at = (xh ^ (bits >> 1), y * 2 + (xl ^ (bits & 1)))
            out[y] = sum(ref[at].astype(F32) for ref in ins).astype(BF16)


def arrange_y_kernel(*refs):
    ins, outs = refs[:4], refs[4:]
    size = ins[0].shape[0]
    y = lax.axis_index("y")
    for ahead, out in enumerate(outs):
        at = lax.rem(y + ahead, size)
        out[...] = sum(ref[at].astype(F32) for ref in ins).astype(BF16)


def arrange(kernel, arrays, shape):
    out = jax.ShapeDtypeStruct(shape, BF16)
    return pl.pallas_call(
        kernel,
        out_shape=[out] * 4,
        cost_estimate=pl.CostEstimate(flops=2**18, bytes_accessed=2**20, transcendentals=0),
    )(*arrays)


def final_kernel(
    pair_ref, both_ref, gain_ref, shift_ref, w_ref, g0_ref, g1_ref, g2_ref, g3_ref, out_ref
):
    rows, block, channels = pair_ref.shape
    tile = sum(ref[...].astype(F32) for ref in (g0_ref, g1_ref, g2_ref, g3_ref))
    tile = jnp.concatenate([tile[:rows], tile[rows:]], axis=1).astype(BF16).astype(F32)
    keep = line_mask(block, tile.shape[1])
    spread = jnp.concatenate(
        [
            jnp.where(keep, jnp.broadcast_to(tile[i : i + 1], keep.shape), 0.0).astype(BF16)
            for i in range(rows)
        ],
        axis=0,
    )
    w_back = spread_heads(w_ref, block)
    dn = both_ref[:, 1].reshape(rows * block, channels).astype(F32) + mm_nt(spread, w_back)
    x = pair_ref[...].reshape(rows * block, channels).astype(F32)
    centred = x - jnp.mean(x, axis=-1, keepdims=True)
    rstd = lax.rsqrt(jnp.mean(centred * centred, axis=-1, keepdims=True) + EPSILON)
    unit = centred * rstd
    push = dn * gain_ref[...]
    along = jnp.mean(push * unit, axis=-1, keepdims=True)
    level = jnp.mean(push, axis=-1, keepdims=True)
    out_ref[...] = ((push - level - unit * along) * rstd).reshape(out_ref.shape)


def final(pair, both, gain, shift_row, bias_weight, gb):
    return pl.pallas_call(
        final_kernel,
        out_shape=jax.ShapeDtypeStruct(pair.shape, F32),
        compiler_params=PARAMS,
        cost_estimate=pl.CostEstimate(
            flops=2**27, bytes_accessed=2**21, transcendentals=2**12
        ),
    )(pair, both, gain, shift_row, bias_weight, *gb)


def shards(
    pair,
    cotangent,
    norm_gain,
    norm_shift,
    query_weight,
    key_weight,
    value_weight,
    gate_weight,
    bias_weight,
    out_weight,
):
    rows_i, rows_j, channels = pair.shape
    heads = bias_weight.shape[1]
    n_ja = lax.axis_size(JA)
    own_i = rows_i // n_ja
    gain = norm_gain.reshape(1, channels)
    shift_row = norm_shift.reshape(1, channels)
    weights = (query_weight, key_weight, value_weight, gate_weight)
    tie = lax.optimization_barrier

    both = lax.all_to_all(
        prep(pair, gain, shift_row, bias_weight, n_ja), JA, 0, 0, tiled=True
    )
    cotangent, both = tie((cotangent, both))
    cot = lax.all_to_all(
        cotangent.reshape(n_ja, own_i, rows_j, channels), JA, 0, 0, tiled=True
    )

    near = both[:, own_i]
    far = lax.ppermute(near, "xh", [(0, 1), (1, 0)])
    by_n, by_t, gate = project(both, gain, shift_row, weights)
    far, by_n = tie((far, by_n))
    near = jnp.stack([near, far])
    prev, after = shift(near, "z", 1), shift(near, "z", 3)
    att, dq, dk, dv, total = [], [], [], [], []

    def slice_of(ahead, own, other):
        att_a, dq_a, dk_a, dv_a, mine, theirs = attend(
            heads, ahead, by_n, by_t, gate, cot, out_weight, own, other
        )
        att.append(att_a)
        dq.append(dq_a)
        dk.append(dk_a)
        dv.append(dv_a)
        return mine, swap(theirs)

    def joined(mine, theirs):
        return (mine.astype(F32) + theirs.astype(F32)).astype(BF16)

    mine0, theirs0 = slice_of(0, [near], [swap(near)])
    prev, after, dk[0] = tie((prev, after, dk[0]))
    opp0, opp1 = shift(prev[0], "z", 1)[None], shift(after[1], "z", 3)[None]
    mine1, theirs1 = slice_of(3, [prev], [swap(prev)])
    after_swap = swap(after)
    after, after_swap, opp0, opp1, dk[1] = tie((after, after_swap, opp0, opp1, dk[1]))
    mine2, theirs2 = slice_of(1, [after], [after_swap])
    opp_swap = [swap(opp0), swap(opp1)]
    opp0, opp1, opp_swap, theirs0, theirs1, dk[2] = tie(
        (opp0, opp1, opp_swap, theirs0, theirs1, dk[2])
    )
    part0 = joined(mine0, theirs0)
    part1 = joined(mine1, theirs1)
    opp0, part1 = tie((opp0, part1))
    part1 = shift(part1, "z", 3)
    mine3, theirs3 = slice_of(2, [opp0, opp1], opp_swap)
    part1, theirs2, dk[3] = tie((part1, theirs2, dk[3]))
    part2 = joined(mine2, theirs2)
    part3 = joined(mine3, theirs3)
    part2, part3, dk[3] = tie((part2, part3, dk[3]))
    part2, part3 = shift(part2, "z", 1), shift(part3, "z", 2)
    done = finish((0, 3, 1, 2), gate, cot, out_weight, weights, att, dq, dk, dv)
    part2, part3, done = tie((part2, part3, done))
    total = [part0, part1, part2, part3]

    slab = total[0].shape[2:]
    by_x = list(arrange(arrange_x_kernel, total, (lax.axis_size("y"),) + slab))
    by_x[1], done = tie((by_x[1], done))
    done = lax.all_to_all(done, JA, 0, 0, tiled=True)
    by_x = [by_x[0]] + [cross(by_x[bits], bits) for bits in (1, 2, 3)]
    by_y = arrange(arrange_y_kernel, by_x, slab)
    by_y = [by_y[0]] + [shift(by_y[d], "y", d) for d in (1, 2, 3)]

    update = done[:, 0].reshape(pair.shape)
    pair_grad = final(pair, done, gain, shift_row, bias_weight, by_y)
    return (update, pair_grad)


def solution(mesh):
    fine = Mesh(mesh.devices.reshape(4, 2, 2, 4, 2), IA + JA)
    spec = P(IA, JA, None)
    in_specs = (spec, spec) + (P(),) * 8
    return jax.shard_map(
        shards, mesh=fine, in_specs=in_specs, out_specs=(spec, spec), check_vma=False
    )
```

```python
import math

import jax
import jax.numpy as jnp
from jax import lax
from jax.experimental import pallas as pl
from jax.experimental.pallas import tpu as pltpu
from jax.sharding import Mesh, PartitionSpec as P

EPSILON = 1e-05
LOG2E = math.log2(math.e)
IA = ("z", "xh", "core")
JA = ("y", "xl")
F32 = jnp.float32
BF16 = jnp.bfloat16
LANES = 128
PARAMS = pltpu.CompilerParams(vmem_limit_bytes=24 * 1024 * 1024)
FIRST = pltpu.CompilerParams(vmem_limit_bytes=60 * 1024 * 1024)


def normalize(values, norm_gain, norm_shift):
    mean_val = jnp.mean(values, axis=-1, keepdims=True)
    centred = values - mean_val
    variance = jnp.mean(centred * centred, axis=-1, keepdims=True)
    return centred * lax.rsqrt(variance + EPSILON) * norm_gain + norm_shift


def mm(a, b):
    return lax.dot_general(a, b, (((1,), (0,)), ((), ())), preferred_element_type=F32)


def mm_nt(a, b):
    return lax.dot_general(a, b, (((1,), (1,)), ((), ())), preferred_element_type=F32)


def mm_tn(a, b):
    return lax.dot_general(a, b, (((0,), (0,)), ((), ())), preferred_element_type=F32)


def swap(a):
    return lax.ppermute(a, "core", [(0, 1), (1, 0)])


def shift(a, axis, by):
    size = lax.axis_size(axis)
    return lax.ppermute(a, axis, [(s, (s + by) % size) for s in range(size)])


def whole(a):
    return pl.BlockSpec(a.shape, lambda *_: (0,) * len(a.shape))


def line_mask(block, width):
    lane = lax.broadcasted_iota(jnp.int32, (block, width), 1)
    return lax.broadcasted_iota(jnp.int32, (block, width), 0) == lane % block


def spread_heads(w_ref, block):
    w = w_ref[...].astype(F32)
    shape = (block, w.shape[1])
    rows = [jnp.broadcast_to(w[h : h + 1], shape) for h in range(w.shape[0])]
    return jnp.concatenate(rows, axis=0).astype(BF16)


def prep_kernel(pair_ref, gain_ref, shift_ref, w_ref, out_ref):
    rows, block, channels = pair_ref.shape
    n_ja = out_ref.shape[0]
    own = rows // n_ja
    split = (n_ja, own, block, channels)
    out_ref[:, :own] = pair_ref[...].reshape(split)
    x = pair_ref[...].reshape(rows * block, channels).astype(F32)
    normed = normalize(x, gain_ref[...], shift_ref[...]).astype(BF16)
    every = mm_nt(normed, spread_heads(w_ref, block))
    width = every.shape[1]
    keep = line_mask(block, width)
    lines = []
    for i in range(rows):
        part = jnp.where(keep, every[i * block : (i + 1) * block], 0.0)
        lines.append(jnp.sum(part, axis=0, keepdims=True))
    tile = jnp.concatenate(lines, axis=0).astype(BF16)
    tile = jnp.concatenate([tile[:, :LANES], tile[:, LANES:]], axis=0)
    for d in range(n_ja):
        out_ref[d, own] = tile


def prep(pair, gain, shift_row, bias_weight, n_ja):
    rows, block, channels = pair.shape
    out = jax.ShapeDtypeStruct((n_ja, rows // n_ja + 1, block, channels), BF16)
    return pl.pallas_call(
        prep_kernel,
        out_shape=out,
        compiler_params=FIRST,
        cost_estimate=pl.CostEstimate(
            flops=2**27, bytes_accessed=2**21, transcendentals=2**12
        ),
    )(pair, gain, shift_row, bias_weight)


def project_kernel(
    pair_ref, gain_ref, shift_ref, w_q_ref, w_k_ref, w_v_ref, w_g_ref, out_n_ref, out_t_ref, gate_ref
):
    n_blocks, _, block, channels = pair_ref.shape
    n = n_blocks * block
    inner = w_q_ref.shape[1]
    x = pair_ref[...].reshape(n, channels).astype(F32)
    normed = normalize(x, gain_ref[...], shift_ref[...]).astype(BF16)
    weights = [ref[...] for ref in (w_q_ref, w_k_ref, w_v_ref, w_g_ref)]
    out_n_ref[0] = mm(normed, jnp.concatenate(weights[:3], axis=1)).astype(BF16)
    proj_t = mm_nt(jnp.concatenate([w.T for w in weights], axis=0), normed)
    out_t_ref[0] = proj_t[: 3 * inner].astype(BF16)
    gate_ref[0] = jax.nn.sigmoid(proj_t[3 * inner :])


def project(both, gain, shift_row, weights):
    n_blocks, slabs, block, channels = both.shape
    rows = slabs - 1
    n = n_blocks * block
    inner = weights[0].shape[1]
    out_n = jax.ShapeDtypeStruct((rows, n, 3 * inner), BF16)
    out_t = jax.ShapeDtypeStruct((rows, 3 * inner, n), BF16)
    gate = jax.ShapeDtypeStruct((rows, inner, n), F32)
    return pl.pallas_call(
        project_kernel,
        grid=(rows,),
        in_specs=[pl.BlockSpec((n_blocks, 1, block, channels), lambda i: (0, i, 0, 0))]
        + [whole(a) for a in (gain, shift_row, *weights)],
        out_specs=[
            pl.BlockSpec((1,) + a.shape[1:], lambda i: (i, 0, 0)) for a in (out_n, out_t, gate)
        ],
        out_shape=[out_n, out_t, gate],
        compiler_params=PARAMS,
        cost_estimate=pl.CostEstimate(
            flops=2**31, bytes_accessed=8 * 2**20, transcendentals=2**18
        ),
    )(both, gain, shift_row, *weights)


def z_lanes(ahead):
    at = lax.rem(lax.axis_index("z") + ahead, lax.axis_size("z"))
    return pl.ds(pl.multiple_of(at * LANES, LANES), LANES)


def attend_kernel(
    heads,
    ahead,
    n_own,
    n_ref,
    t_ref,
    gate_ref,
    cot_ref,
    w_o_ref,
    *refs,
):
    bias_refs = refs[: n_own * 2]
    att_ref, dq_ref, dk_ref, dv_ref, mine_ref, theirs_ref = refs[n_own * 2 : n_own * 2 + 6]
    bias_s, gb_s, s_s, p_s, ds_s, tile_s, line_s = refs[n_own * 2 + 6 :]
    row = pl.program_id(0)
    n = n_ref.shape[1]
    inner = n_ref.shape[2] // 3
    head_dim = inner // heads
    scale = 1.0 / math.sqrt(head_dim)
    n_ja = tile_s.shape[0]
    block = n // n_ja
    rows_i = LANES // 4
    pairs = heads // 2
    core = lax.axis_index("core")
    xh = lax.axis_index("xh")

    @pl.when(row == 0)
    def _():
        for which in range(2):
            far = 0
            for ref in bias_refs[which * n_own : (which + 1) * n_own]:
                for e in range(ref.shape[0]):
                    at = (xh ^ far) * 2 + (core ^ which)
                    at = pl.ds(pl.multiple_of(at * rows_i, rows_i), rows_i)
                    for owner in range(n_ja):
                        for p in range(pairs):
                            tile_s[owner, at, p * LANES : (p + 1) * LANES] = ref[
                                e, owner, p * rows_i : (p + 1) * rows_i, :
                            ]
                    far += 1
        for owner in range(n_ja):
            for p in range(pairs):
                t = tile_s[owner, :, p * LANES : (p + 1) * LANES].astype(F32).T * LOG2E
                for e in range(2):
                    h = p * 2 + e
                    bias_s[
                        owner * block : (owner + 1) * block, h * LANES : (h + 1) * LANES
                    ] = t[e * block : (e + 1) * block]
        gb_s[...] = jnp.zeros_like(gb_s)

    at = z_lanes(ahead)
    nil = jnp.zeros((), BF16)
    row_head = lax.broadcasted_iota(jnp.int32, (inner, LANES), 0) // head_dim
    lane_head = lax.broadcasted_iota(jnp.int32, (LANES, inner), 1) // head_dim
    q_t = t_ref[0, :inner, at]
    q_n = n_ref[0, at, :inner]
    z = lax.rem(lax.axis_index("z") + ahead, lax.axis_size("z"))
    span = LANES // block
    cot = cot_ref[pl.ds(z * span, span), 0].reshape(LANES, cot_ref.shape[3])
    d_att = mm_nt(w_o_ref[...], cot) * gate_ref[0, :, at]
    q_row = jnp.concatenate([jnp.where(lane_head == h, q_n, nil) for h in range(heads)], 0)
    step = 16
    chunk = 128
    wide = 2 * LANES
    a_rows = []
    invs = []
    for p in range(pairs):
        cols = slice(p * wide, (p + 1) * wide)
        q_blk = jnp.concatenate(
            [jnp.where(row_head == h, q_t, nil) for h in (2 * p, 2 * p + 1)], axis=1
        )
        top = jnp.full((8, wide), -jnp.inf, F32)
        for k in range(0, n, chunk):
            t = mm(n_ref[0, k : k + chunk, inner : 2 * inner], q_blk) * (scale * LOG2E)
            t = t + bias_s[k : k + chunk, cols]
            s_s[k : k + chunk, cols] = t
            for e in range(0, chunk, 8):
                top = jnp.maximum(top, t[e : e + 8])
        top = jnp.max(top, axis=0, keepdims=True)
        total = jnp.zeros((8, wide), F32)
        for k in range(0, n, step):
            e = jnp.exp2(s_s[k : k + step, cols] - top)
            s_s[k : k + step, cols] = e
            p_s[k : k + step, cols] = e.astype(BF16)
            total = total + (e[:8] + e[8:])
        invs.append(1.0 / jnp.sum(total, axis=0, keepdims=True))
    for p in range(pairs):
        cols = slice(p * wide, (p + 1) * wide)
        first = 2 * p * head_dim
        rows = slice(first, first + 2 * head_dim)
        inv = invs[p]
        att = mm(t_ref[0, 2 * inner + first : 2 * inner + first + 2 * head_dim, :], p_s[:, cols])
        att = att * inv
        a_two = jnp.concatenate([d_att[rows], d_att[rows]], axis=1) * inv
        lane = lax.broadcasted_iota(jnp.int32, a_two.shape, 1) // LANES
        sub = lax.broadcasted_iota(jnp.int32, a_two.shape, 0) // head_dim
        a_two = jnp.where(lane == sub, a_two, 0.0).astype(BF16)
        diag = jnp.sum(a_two.astype(F32) * att, axis=0, keepdims=True)
        for e in range(2):
            h = 2 * p + e
            own = slice(h * head_dim, (h + 1) * head_dim)
            att_ref[0, own, :] = att[
                e * head_dim : (e + 1) * head_dim, e * LANES : (e + 1) * LANES
            ]
        lead = [jnp.zeros((first, wide), BF16)] if p else []
        tail = [jnp.zeros((inner - first - 2 * head_dim, wide), BF16)] if p + 1 < pairs else []
        a_blk = jnp.concatenate(lead + [a_two] + tail, axis=0)
        a_rows.append(a_blk.T)
        for k in range(0, n, chunk):
            dp = mm(n_ref[0, k : k + chunk, 2 * inner :], a_blk)
            ds = s_s[k : k + chunk, cols] * (dp - diag)
            gb_s[k : k + chunk, cols] += ds
            ds_s[k : k + chunk, cols] = ds.astype(BF16)
        dq = mm(t_ref[0, inner + first : inner + first + 2 * head_dim, :], ds_s[:, cols]) * scale
        for e in range(2):
            h = 2 * p + e
            dq_ref[0, h * head_dim : (h + 1) * head_dim, :] = dq[
                e * head_dim : (e + 1) * head_dim, e * LANES : (e + 1) * LANES
            ].astype(BF16)
    dk_ref[0] = (mm(ds_s[...], q_row) * scale).astype(BF16)
    dv_ref[0] = mm(p_s[...], jnp.concatenate(a_rows, axis=0)).astype(BF16)

    @pl.when(row == pl.num_programs(0) - 1)
    def _():
        for owner in range(n_ja):
            for p in range(pairs):
                t = jnp.concatenate(
                    [
                        gb_s[owner * block : (owner + 1) * block, h * LANES : (h + 1) * LANES]
                        for h in (2 * p, 2 * p + 1)
                    ],
                    axis=0,
                )
                line_s[:, p * LANES : (p + 1) * LANES] = t.T.astype(BF16)
            for far in range(2):
                for ref, which in ((mine_ref, core), (theirs_ref, 1 - core)):
                    at = pl.multiple_of((far * 2 + which) * rows_i, rows_i)
                    for p in range(pairs):
                        ref[far, owner, p * rows_i : (p + 1) * rows_i, :] = line_s[
                            pl.ds(at, rows_i), p * LANES : (p + 1) * LANES
                        ]


def attend(heads, ahead, by_n, by_t, gate, cot, w_o, own, other):
    rows, n, _ = by_n.shape
    inner = gate.shape[1]
    n_ja, slab, _ = own[0].shape[1:]
    lines = heads * n // n_ja
    att = jax.ShapeDtypeStruct((rows, inner, LANES), F32)
    dq = jax.ShapeDtypeStruct((rows, inner, LANES), BF16)
    grad = jax.ShapeDtypeStruct((rows, n, inner), BF16)
    gb = jax.ShapeDtypeStruct((2, n_ja, slab, LANES), BF16)

    def by_row(a):
        return pl.BlockSpec((1,) + a.shape[1:], lambda i: (i, 0, 0))

    cot_spec = pl.BlockSpec((cot.shape[0], 1) + cot.shape[2:], lambda i: (0, i, 0, 0))
    return pl.pallas_call(
        lambda *refs: attend_kernel(heads, ahead, len(own), *refs),
        grid=(rows,),
        in_specs=[by_row(by_n), by_row(by_t), by_row(gate), cot_spec, whole(w_o)]
        + [whole(a) for a in (*own, *other)],
        out_specs=[by_row(a) for a in (att, dq, grad, grad)] + [whole(gb)] * 2,
        out_shape=[att, dq, grad, grad, gb, gb],
        scratch_shapes=[
            pltpu.VMEM((n, heads * LANES), F32),
            pltpu.VMEM((n, heads * LANES), F32),
            pltpu.VMEM((n, heads * LANES), F32),
            pltpu.VMEM((n, heads * LANES), BF16),
            pltpu.VMEM((n, heads * LANES), BF16),
            pltpu.VMEM((n_ja, LANES, lines), BF16),
            pltpu.VMEM((LANES, lines), BF16),
        ],
        compiler_params=PARAMS,
        cost_estimate=pl.CostEstimate(
            flops=2**32, bytes_accessed=2**23, transcendentals=2**20
        ),
    )(by_n, by_t, gate, cot, w_o, *own, *other)


def finish_kernel(aheads, gate_ref, cot_ref, w_o_ref, w_q_ref, w_k_ref, w_v_ref, w_g_ref, *refs):
    count = len(aheads)
    att_refs, dq_refs = refs[:count], refs[count : 2 * count]
    dk_refs, dv_refs = refs[2 * count : 3 * count], refs[3 * count : 4 * count]
    out_ref, att_s, dq_s = refs[4 * count :]
    for ahead, att_ref, dq_ref in zip(aheads, att_refs, dq_refs):
        at = z_lanes(ahead)
        att_s[:, at] = att_ref[0]
        dq_s[:, at] = dq_ref[0]
    half = (out_ref.shape[0],) + out_ref.shape[2:]
    gate = gate_ref[0]
    cot = cot_ref[...].reshape(gate.shape[1], cot_ref.shape[3])
    d_gated = mm_nt(w_o_ref[...], cot)
    att = att_s[...]
    update = mm_tn((gate * att).astype(BF16), w_o_ref[...])
    out_ref[:, 0] = update.astype(BF16).reshape(half)
    d_gate = (d_gated * att * gate * (1.0 - gate)).astype(BF16)
    left_t = jnp.concatenate([dq_s[...], d_gate], axis=0)
    dk = sum(ref[0].astype(F32) for ref in dk_refs).astype(BF16)
    dv = sum(ref[0].astype(F32) for ref in dv_refs).astype(BF16)
    dn = mm_tn(left_t, jnp.concatenate([w_q_ref[...].T, w_g_ref[...].T], axis=0))
    dn = dn + mm(
        jnp.concatenate([dk, dv], axis=1),
        jnp.concatenate([w_k_ref[...].T, w_v_ref[...].T], axis=0),
    )
    out_ref[:, 1] = dn.astype(BF16).reshape(half)


def finish(aheads, gate, cot, w_o, weights, att, dq, dk, dv):
    n_blocks, rows, block, channels = cot.shape
    inner = w_o.shape[0]
    arrays = (*att, *dq, *dk, *dv)

    def by_row(a):
        return pl.BlockSpec((1,) + a.shape[1:], lambda i: (i, 0, 0))

    cot_spec = pl.BlockSpec((n_blocks, 1, block, channels), lambda i: (0, i, 0, 0))
    return pl.pallas_call(
        lambda *refs: finish_kernel(aheads, *refs),
        grid=(rows,),
        in_specs=[by_row(gate), cot_spec, whole(w_o)]
        + [whole(a) for a in weights]
        + [by_row(a) for a in arrays],
        out_specs=pl.BlockSpec(
            (n_blocks, 2, 1, block, channels), lambda i: (0, 0, i, 0, 0)
        ),
        out_shape=jax.ShapeDtypeStruct((n_blocks, 2, rows, block, channels), BF16),
        scratch_shapes=[
            pltpu.VMEM((inner, n_blocks * block), F32),
            pltpu.VMEM((inner, n_blocks * block), BF16),
        ],
        compiler_params=PARAMS,
        cost_estimate=pl.CostEstimate(flops=2**31, bytes_accessed=2**23, transcendentals=0),
    )(gate, cot, w_o, *weights, *arrays)


def join_kernel(mine_ref, theirs_ref, back_ref, ahead_ref, opp_ref, keep_ref, send_ref):
    xh = lax.axis_index("xh")
    refs = (mine_ref, theirs_ref, back_ref, ahead_ref, opp_ref)
    for far, out in ((0, keep_ref), (1, send_ref)):
        out[...] = sum(ref[xh ^ far].astype(F32) for ref in refs).astype(BF16)


def join(arrays):
    out = jax.ShapeDtypeStruct(arrays[0].shape[1:], BF16)
    return pl.pallas_call(
        join_kernel,
        out_shape=[out] * 2,
        compiler_params=PARAMS,
        cost_estimate=pl.CostEstimate(flops=2**18, bytes_accessed=2**20, transcendentals=0),
    )(*arrays)


def final_kernel(
    pair_ref, both_ref, gain_ref, shift_ref, w_ref, gb_ref, out_ref
):
    rows, block, channels = pair_ref.shape
    tile = jnp.sum(gb_ref[...].astype(F32), axis=0)
    tile = jnp.concatenate([tile[:rows], tile[rows:]], axis=1).astype(BF16).astype(F32)
    keep = line_mask(block, tile.shape[1])
    spread = jnp.concatenate(
        [
            jnp.where(keep, jnp.broadcast_to(tile[i : i + 1], keep.shape), 0.0).astype(BF16)
            for i in range(rows)
        ],
        axis=0,
    )
    w_back = spread_heads(w_ref, block)
    dn = both_ref[:, 1].reshape(rows * block, channels).astype(F32) + mm(spread, w_back)
    x = pair_ref[...].reshape(rows * block, channels).astype(F32)
    centred = x - jnp.mean(x, axis=-1, keepdims=True)
    rstd = lax.rsqrt(jnp.mean(centred * centred, axis=-1, keepdims=True) + EPSILON)
    unit = centred * rstd
    push = dn * gain_ref[...]
    along = jnp.mean(push * unit, axis=-1, keepdims=True)
    level = jnp.mean(push, axis=-1, keepdims=True)
    out_ref[...] = ((push - level - unit * along) * rstd).reshape(out_ref.shape)


def final(pair, both, gain, shift_row, bias_weight, gb):
    return pl.pallas_call(
        final_kernel,
        out_shape=jax.ShapeDtypeStruct(pair.shape, F32),
        compiler_params=PARAMS,
        cost_estimate=pl.CostEstimate(
            flops=2**27, bytes_accessed=2**21, transcendentals=2**12
        ),
    )(pair, both, gain, shift_row, bias_weight, gb)


def shards(
    pair,
    cotangent,
    norm_gain,
    norm_shift,
    query_weight,
    key_weight,
    value_weight,
    gate_weight,
    bias_weight,
    out_weight,
):
    rows_i, rows_j, channels = pair.shape
    heads = bias_weight.shape[1]
    n_ja = lax.axis_size(JA)
    own_i = rows_i // n_ja
    gain = norm_gain.reshape(1, channels)
    shift_row = norm_shift.reshape(1, channels)
    bias_rows = bias_weight.T
    weights = (query_weight, key_weight, value_weight, gate_weight)
    tie = lax.optimization_barrier

    both = lax.all_to_all(
        prep(pair, gain, shift_row, bias_rows, n_ja), JA, 0, 0, tiled=True
    )
    cotangent, both = tie((cotangent, both))
    cot = lax.all_to_all(
        cotangent.reshape(n_ja, own_i, rows_j, channels), JA, 0, 0, tiled=True
    )

    near = both[:, own_i]
    far = lax.ppermute(near, "xh", [(0, 1), (1, 0)])
    by_n, by_t, gate = project(both, gain, shift_row, weights)
    far, by_n = tie((far, by_n))
    near = jnp.stack([near, far])
    prev, after = shift(near, "z", 1), shift(near, "z", 3)
    att, dq, dk, dv, total = [], [], [], [], []

    def slice_of(ahead, own, other):
        att_a, dq_a, dk_a, dv_a, mine, theirs = attend(
            heads, ahead, by_n, by_t, gate, cot, out_weight, own, other
        )
        att.append(att_a)
        dq.append(dq_a)
        dk.append(dk_a)
        dv.append(dv_a)
        return mine, swap(theirs)

    def joined(mine, theirs):
        return (mine.astype(F32) + theirs.astype(F32)).astype(BF16)

    mine0, theirs0 = slice_of(0, [near], [swap(near)])
    prev, after, dk[0] = tie((prev, after, dk[0]))
    opp0, opp1 = shift(prev[0], "z", 1)[None], shift(after[1], "z", 3)[None]
    mine1, theirs1 = slice_of(3, [prev], [swap(prev)])
    after_swap = swap(after)
    after, after_swap, opp0, opp1, dk[1] = tie((after, after_swap, opp0, opp1, dk[1]))
    mine2, theirs2 = slice_of(1, [after], [after_swap])
    opp_swap = [swap(opp0), swap(opp1)]
    opp0, opp1, opp_swap, theirs0, theirs1, dk[2] = tie(
        (opp0, opp1, opp_swap, theirs0, theirs1, dk[2])
    )
    part1 = joined(mine1, theirs1)
    opp0, part1 = tie((opp0, part1))
    part1 = shift(part1, "z", 3)
    mine3, theirs3 = slice_of(2, [opp0, opp1], opp_swap)
    part1, theirs2, dk[3] = tie((part1, theirs2, dk[3]))
    part2 = joined(mine2, theirs2)
    done = finish((0, 3, 1, 2), gate, cot, out_weight, weights, att, dq, dk, dv)
    theirs3, done = tie((theirs3, done))
    part3 = joined(mine3, theirs3)
    part2, part3, done = tie((part2, part3, done))
    part2, part3 = shift(part2, "z", 1), shift(part3, "z", 2)

    keep, send = join([mine0, theirs0, part1, part2, part3])
    done = lax.all_to_all(done, JA, 0, 0, tiled=True)
    gb = joined(keep, lax.ppermute(send, "xh", [(0, 1), (1, 0)]))
    gb = lax.all_to_all(gb, JA, 0, 0, tiled=True)

    update = done[:, 0].reshape(pair.shape)
    pair_grad = final(pair, done, gain, shift_row, bias_rows, gb)
    return (update, pair_grad)


def solution(mesh):
    fine = Mesh(mesh.devices.reshape(4, 2, 2, 4, 2), IA + JA)
    spec = P(IA, JA, None)
    in_specs = (spec, spec) + (P(),) * 8
    return jax.shard_map(
        shards, mesh=fine, in_specs=in_specs, out_specs=(spec, spec), check_vma=False
    )
```

```python
import math

import jax
import jax.numpy as jnp
from jax import lax
from jax.experimental import pallas as pl
from jax.experimental.pallas import tpu as pltpu
from jax.sharding import Mesh, PartitionSpec as P

EPSILON = 1e-05
LOG2E = math.log2(math.e)
IA = ("z", "xh", "core")
JA = ("y", "xl")
F32 = jnp.float32
BF16 = jnp.bfloat16
LANES = 128
PARAMS = pltpu.CompilerParams(vmem_limit_bytes=24 * 1024 * 1024)
FIRST = pltpu.CompilerParams(vmem_limit_bytes=60 * 1024 * 1024)


def normalize(values, norm_gain, norm_shift):
    mean_val = jnp.mean(values, axis=-1, keepdims=True)
    centred = values - mean_val
    variance = jnp.mean(centred * centred, axis=-1, keepdims=True)
    return centred * lax.rsqrt(variance + EPSILON) * norm_gain + norm_shift


def mm(a, b):
    return lax.dot_general(a, b, (((1,), (0,)), ((), ())), preferred_element_type=F32)


def mm_nt(a, b):
    return lax.dot_general(a, b, (((1,), (1,)), ((), ())), preferred_element_type=F32)


def mm_tn(a, b):
    return lax.dot_general(a, b, (((0,), (0,)), ((), ())), preferred_element_type=F32)


def swap(a):
    return lax.ppermute(a, "core", [(0, 1), (1, 0)])


def shift(a, axis, by):
    size = lax.axis_size(axis)
    return lax.ppermute(a, axis, [(s, (s + by) % size) for s in range(size)])


def in_hbm(*arrays):
    return [pltpu.with_memory_space_constraint(a, pltpu.HBM) for a in arrays]


def whole(a):
    return pl.BlockSpec(a.shape, lambda *_: (0,) * len(a.shape))


def line_mask(block, width):
    lane = lax.broadcasted_iota(jnp.int32, (block, width), 1)
    return lax.broadcasted_iota(jnp.int32, (block, width), 0) == lane % block


def spread_heads(w_ref, block):
    w = w_ref[...].astype(F32)
    shape = (block, w.shape[1])
    rows = [jnp.broadcast_to(w[h : h + 1], shape) for h in range(w.shape[0])]
    return jnp.concatenate(rows, axis=0).astype(BF16)


def prep_kernel(pair_ref, cot_ref, gain_ref, shift_ref, w_ref, out_ref):
    rows, block, channels = pair_ref.shape
    n_ja = out_ref.shape[0]
    own = rows // n_ja
    split = (n_ja, own, block, channels)
    out_ref[:, :own] = pair_ref[...].reshape(split)
    out_ref[:, own : 2 * own] = cot_ref[...].reshape(split)
    x = pair_ref[...].reshape(rows * block, channels).astype(F32)
    normed = normalize(x, gain_ref[...], shift_ref[...]).astype(BF16)
    every = mm_nt(normed, spread_heads(w_ref, block))
    width = every.shape[1]
    keep = line_mask(block, width)
    lines = []
    for i in range(rows):
        part = jnp.where(keep, every[i * block : (i + 1) * block], 0.0)
        lines.append(jnp.sum(part, axis=0, keepdims=True))
    tile = jnp.concatenate(lines, axis=0).astype(BF16)
    tile = jnp.concatenate([tile[:, :LANES], tile[:, LANES:]], axis=0)
    for d in range(n_ja):
        out_ref[d, 2 * own] = tile


def prep(pair, cot, gain, shift_row, bias_weight, n_ja):
    rows, block, channels = pair.shape
    out = jax.ShapeDtypeStruct((n_ja, 2 * rows // n_ja + 1, block, channels), BF16)
    return pl.pallas_call(
        prep_kernel,
        out_shape=out,
        compiler_params=FIRST,
        cost_estimate=pl.CostEstimate(
            flops=2**27, bytes_accessed=2**21, transcendentals=2**12
        ),
    )(pair, cot, gain, shift_row, bias_weight)


def project_kernel(
    pair_ref,
    cot_ref,
    gain_ref,
    shift_ref,
    w_o_ref,
    w_q_ref,
    w_k_ref,
    w_v_ref,
    w_g_ref,
    kv_n_ref,
    kv_t_ref,
    q_n_ref,
    q_t_ref,
    d_att_ref,
    gate_ref,
):
    n_blocks, _, block, channels = pair_ref.shape
    n = n_blocks * block
    inner = w_q_ref.shape[1]
    x = pair_ref[...].reshape(n, channels).astype(F32)
    normed = normalize(x, gain_ref[...], shift_ref[...]).astype(BF16)
    weights = [ref[...] for ref in (w_q_ref, w_k_ref, w_v_ref, w_g_ref)]
    proj = mm(normed, jnp.concatenate(weights[:3], axis=1)).astype(BF16)
    kv_n_ref[0] = proj[:, inner:]
    proj_t = mm_nt(jnp.concatenate([w.T for w in weights], axis=0), normed)
    kv_t_ref[0] = proj_t[inner : 3 * inner].astype(BF16)
    gate = jax.nn.sigmoid(proj_t[3 * inner :])
    gate_ref[0] = gate
    d_att = mm_nt(w_o_ref[...], cot_ref[...].reshape(n, channels)) * gate
    size = lax.axis_size("z")
    z = lax.axis_index("z")
    for owner in range(n // LANES):
        at = slice(owner * LANES, (owner + 1) * LANES)
        ahead = lax.rem(owner + size - z, size)
        q_n_ref[ahead, 0] = proj[at, :inner]
        q_t_ref[ahead, 0] = proj_t[:inner, at].astype(BF16)
        d_att_ref[ahead, 0] = d_att[:, at]


def project(both, gain, shift_row, w_o, weights):
    n_blocks, slabs, block, channels = both.shape
    rows = slabs // 2
    n = n_blocks * block
    inner = w_o.shape[0]
    kv_n = pltpu.HBM((rows, n, 2 * inner), BF16)
    kv_t = pltpu.HBM((rows, 2 * inner, n), BF16)
    gate = pltpu.HBM((rows, inner, n), F32)
    q_n = pltpu.HBM((n // LANES, rows, LANES, inner), BF16)
    q_t = pltpu.HBM((n // LANES, rows, inner, LANES), BF16)
    d_att = pltpu.HBM((n // LANES, rows, inner, LANES), F32)

    def by_row(a):
        return pl.BlockSpec((1,) + a.shape[1:], lambda i: (i, 0, 0))

    def sliced(a):
        return pl.BlockSpec((a.shape[0], 1) + a.shape[2:], lambda i: (0, i, 0, 0))

    return pl.pallas_call(
        project_kernel,
        grid=(rows,),
        in_specs=[
            pl.BlockSpec((n_blocks, 1, block, channels), lambda i: (0, i, 0, 0)),
            pl.BlockSpec((n_blocks, 1, block, channels), lambda i: (0, rows + i, 0, 0)),
        ]
        + [whole(a) for a in (gain, shift_row, w_o, *weights)],
        out_specs=[by_row(kv_n), by_row(kv_t)]
        + [sliced(a) for a in (q_n, q_t, d_att)]
        + [by_row(gate)],
        out_shape=[kv_n, kv_t, q_n, q_t, d_att, gate],
        compiler_params=PARAMS,
        cost_estimate=pl.CostEstimate(
            flops=2**31, bytes_accessed=8 * 2**20, transcendentals=2**18
        ),
    )(both, both, gain, shift_row, w_o, *weights)


def z_lanes(ahead):
    at = lax.rem(lax.axis_index("z") + ahead, lax.axis_size("z"))
    return pl.ds(pl.multiple_of(at * LANES, LANES), LANES)


def attend_kernel(
    heads,
    n_own,
    n_ref,
    t_ref,
    q_n_ref,
    q_t_ref,
    d_att_ref,
    *refs,
):
    bias_refs = refs[: n_own * 2]
    att_ref, dq_ref, dk_ref, dv_ref, mine_ref, theirs_ref = refs[n_own * 2 : n_own * 2 + 6]
    bias_s, gb_s, s_s, p_s, ds_s, tile_s, line_s = refs[n_own * 2 + 6 :]
    row = pl.program_id(0)
    n = n_ref.shape[1]
    inner = n_ref.shape[2] // 2
    head_dim = inner // heads
    scale = 1.0 / math.sqrt(head_dim)
    n_ja = tile_s.shape[0]
    block = n // n_ja
    rows_i = LANES // 4
    pairs = heads // 2
    core = lax.axis_index("core")
    xh = lax.axis_index("xh")

    @pl.when(row == 0)
    def _():
        for which in range(2):
            views = []
            for ref in bias_refs[which * n_own : (which + 1) * n_own]:
                views += [ref] if len(ref.shape) == 3 else [ref.at[e] for e in range(2)]
            for far, ref in enumerate(views):
                at = (xh ^ far) * 2 + (core ^ which)
                at = pl.ds(pl.multiple_of(at * rows_i, rows_i), rows_i)
                for owner in range(n_ja):
                    for p in range(pairs):
                        tile_s[owner, at, p * LANES : (p + 1) * LANES] = ref[
                            owner, p * rows_i : (p + 1) * rows_i, :
                        ]
        for owner in range(n_ja):
            for p in range(pairs):
                t = tile_s[owner, :, p * LANES : (p + 1) * LANES].astype(F32).T * LOG2E
                for e in range(2):
                    h = p * 2 + e
                    bias_s[
                        owner * block : (owner + 1) * block, h * LANES : (h + 1) * LANES
                    ] = t[e * block : (e + 1) * block]
        gb_s[...] = jnp.zeros_like(gb_s)

    nil = jnp.zeros((), BF16)
    row_head = lax.broadcasted_iota(jnp.int32, (inner, LANES), 0) // head_dim
    lane_head = lax.broadcasted_iota(jnp.int32, (LANES, inner), 1) // head_dim
    q_n = q_n_ref[0, 0]
    q_t = q_t_ref[0, 0]
    d_att = d_att_ref[0, 0]
    q_row = jnp.concatenate([jnp.where(lane_head == h, q_n, nil) for h in range(heads)], 0)
    step = 16
    chunk = 128
    wide = 2 * LANES
    a_rows = []
    invs = []
    for p in range(pairs):
        cols = slice(p * wide, (p + 1) * wide)
        q_blk = jnp.concatenate(
            [jnp.where(row_head == h, q_t, nil) for h in (2 * p, 2 * p + 1)], axis=1
        )
        top = jnp.full((8, wide), -jnp.inf, F32)
        for k in range(0, n, chunk):
            t = mm(n_ref[0, k : k + chunk, :inner], q_blk) * (scale * LOG2E)
            t = t + bias_s[k : k + chunk, cols]
            s_s[k : k + chunk, cols] = t
            for e in range(0, chunk, 8):
                top = jnp.maximum(top, t[e : e + 8])
        top = jnp.max(top, axis=0, keepdims=True)
        total = jnp.zeros((8, wide), F32)
        for k in range(0, n, step):
            e = jnp.exp2(s_s[k : k + step, cols] - top)
            s_s[k : k + step, cols] = e
            p_s[k : k + step, cols] = e.astype(BF16)
            total = total + (e[:8] + e[8:])
        invs.append(1.0 / jnp.sum(total, axis=0, keepdims=True))
    for p in range(pairs):
        cols = slice(p * wide, (p + 1) * wide)
        first = 2 * p * head_dim
        rows = slice(first, first + 2 * head_dim)
        inv = invs[p]
        att = mm(t_ref[0, inner + first : inner + first + 2 * head_dim, :], p_s[:, cols])
        att = att * inv
        a_two = jnp.concatenate([d_att[rows], d_att[rows]], axis=1) * inv
        lane = lax.broadcasted_iota(jnp.int32, a_two.shape, 1) // LANES
        sub = lax.broadcasted_iota(jnp.int32, a_two.shape, 0) // head_dim
        a_two = jnp.where(lane == sub, a_two, 0.0).astype(BF16)
        diag = jnp.sum(a_two.astype(F32) * att, axis=0, keepdims=True)
        for e in range(2):
            h = 2 * p + e
            own = slice(h * head_dim, (h + 1) * head_dim)
            att_ref[0, own, :] = att[
                e * head_dim : (e + 1) * head_dim, e * LANES : (e + 1) * LANES
            ]
        lead = [jnp.zeros((first, wide), BF16)] if p else []
        tail = [jnp.zeros((inner - first - 2 * head_dim, wide), BF16)] if p + 1 < pairs else []
        a_blk = jnp.concatenate(lead + [a_two] + tail, axis=0)
        a_rows.append(a_blk.T)
        for k in range(0, n, chunk):
            dp = mm(n_ref[0, k : k + chunk, inner:], a_blk)
            ds = s_s[k : k + chunk, cols] * (dp - diag)
            gb_s[k : k + chunk, cols] += ds
            ds_s[k : k + chunk, cols] = ds.astype(BF16)
        dq = mm(t_ref[0, first : first + 2 * head_dim, :], ds_s[:, cols]) * scale
        for e in range(2):
            h = 2 * p + e
            dq_ref[0, h * head_dim : (h + 1) * head_dim, :] = dq[
                e * head_dim : (e + 1) * head_dim, e * LANES : (e + 1) * LANES
            ].astype(BF16)
    dk_ref[0] = (mm(ds_s[...], q_row) * scale).astype(BF16)
    dv_ref[0] = mm(p_s[...], jnp.concatenate(a_rows, axis=0)).astype(BF16)

    @pl.when(row == pl.num_programs(0) - 1)
    def _():
        for owner in range(n_ja):
            for p in range(pairs):
                t = jnp.concatenate(
                    [
                        gb_s[owner * block : (owner + 1) * block, h * LANES : (h + 1) * LANES]
                        for h in (2 * p, 2 * p + 1)
                    ],
                    axis=0,
                )
                line_s[:, p * LANES : (p + 1) * LANES] = t.T.astype(BF16)
            for far in range(2):
                for ref, which in ((mine_ref, core), (theirs_ref, 1 - core)):
                    at = pl.multiple_of((far * 2 + which) * rows_i, rows_i)
                    for p in range(pairs):
                        ref[far, owner, p * rows_i : (p + 1) * rows_i, :] = line_s[
                            pl.ds(at, rows_i), p * LANES : (p + 1) * LANES
                        ]


def attend(heads, ahead, projected, own, other):
    rows, n, inner = projected[0].shape
    inner = inner // 2
    n_ja, slab, _ = own[0].shape[-3:]
    lines = heads * n // n_ja
    att = jax.ShapeDtypeStruct((rows, inner, LANES), F32)
    dq = jax.ShapeDtypeStruct((rows, inner, LANES), BF16)
    grad = jax.ShapeDtypeStruct((rows, n, inner), BF16)
    gb = jax.ShapeDtypeStruct((2, n_ja, slab, LANES), BF16)

    def by_row(a):
        return pl.BlockSpec((1,) + a.shape[1:], lambda i: (i, 0, 0))

    def sliced(a):
        return pl.BlockSpec((1, 1) + a.shape[2:], lambda i: (ahead, i, 0, 0))

    return pl.pallas_call(
        lambda *refs: attend_kernel(heads, len(own), *refs),
        grid=(rows,),
        in_specs=[by_row(a) for a in projected[:2]]
        + [sliced(a) for a in projected[2:]]
        + [whole(a) for a in (*own, *other)],
        out_specs=[by_row(a) for a in (att, dq, grad, grad)] + [whole(gb)] * 2,
        out_shape=[att, dq, grad, grad, gb, gb],
        scratch_shapes=[
            pltpu.VMEM((n, heads * LANES), F32),
            pltpu.VMEM((n, heads * LANES), F32),
            pltpu.VMEM((n, heads * LANES), F32),
            pltpu.VMEM((n, heads * LANES), BF16),
            pltpu.VMEM((n, heads * LANES), BF16),
            pltpu.VMEM((n_ja, LANES, lines), BF16),
            pltpu.VMEM((LANES, lines), BF16),
        ],
        compiler_params=PARAMS,
        cost_estimate=pl.CostEstimate(
            flops=2**32, bytes_accessed=2**23, transcendentals=2**20
        ),
    )(*in_hbm(*projected), *own, *other)


def finish_kernel(aheads, gate_ref, cot_ref, w_o_ref, w_q_ref, w_k_ref, w_v_ref, w_g_ref, *refs):
    count = len(aheads)
    att_refs, dq_refs = refs[:count], refs[count : 2 * count]
    dk_refs, dv_refs = refs[2 * count : 3 * count], refs[3 * count : 4 * count]
    out_ref, att_s, dq_s = refs[4 * count :]
    for ahead, att_ref, dq_ref in zip(aheads, att_refs, dq_refs):
        at = z_lanes(ahead)
        att_s[:, at] = att_ref[0]
        dq_s[:, at] = dq_ref[0]
    half = (out_ref.shape[0],) + out_ref.shape[2:]
    gate = gate_ref[0]
    cot = cot_ref[...].reshape(gate.shape[1], cot_ref.shape[3])
    d_gated = mm_nt(w_o_ref[...], cot)
    att = att_s[...]
    update = mm_tn((gate * att).astype(BF16), w_o_ref[...])
    out_ref[:, 0] = update.astype(BF16).reshape(half)
    d_gate = (d_gated * att * gate * (1.0 - gate)).astype(BF16)
    left_t = jnp.concatenate([dq_s[...], d_gate], axis=0)
    dk = sum(ref[0].astype(F32) for ref in dk_refs).astype(BF16)
    dv = sum(ref[0].astype(F32) for ref in dv_refs).astype(BF16)
    dn = mm_tn(left_t, jnp.concatenate([w_q_ref[...].T, w_g_ref[...].T], axis=0))
    dn = dn + mm(
        jnp.concatenate([dk, dv], axis=1),
        jnp.concatenate([w_k_ref[...].T, w_v_ref[...].T], axis=0),
    )
    out_ref[:, 1] = dn.astype(BF16).reshape(half)


def finish(aheads, gate, both, w_o, weights, att, dq, dk, dv):
    n_blocks, _, block, channels = both.shape
    rows, inner, _ = gate.shape
    arrays = (*att, *dq, *dk, *dv)

    def by_row(a):
        return pl.BlockSpec((1,) + a.shape[1:], lambda i: (i, 0, 0))

    cot_spec = pl.BlockSpec((n_blocks, 1, block, channels), lambda i: (0, rows + i, 0, 0))
    return pl.pallas_call(
        lambda *refs: finish_kernel(aheads, *refs),
        grid=(rows,),
        in_specs=[by_row(gate), cot_spec, whole(w_o)]
        + [whole(a) for a in weights]
        + [by_row(a) for a in arrays],
        out_specs=pl.BlockSpec((n_blocks, 2, block, channels), lambda i: (0, i, 0, 0)),
        out_shape=jax.ShapeDtypeStruct((n_blocks, 2 * rows + 1, block, channels), BF16),
        scratch_shapes=[
            pltpu.VMEM((inner, n_blocks * block), F32),
            pltpu.VMEM((inner, n_blocks * block), BF16),
        ],
        compiler_params=PARAMS,
        cost_estimate=pl.CostEstimate(flops=2**31, bytes_accessed=2**23, transcendentals=0),
    )(*in_hbm(gate), both, w_o, *weights, *arrays)


def halves_kernel(parts, *refs):
    xh = lax.axis_index("xh")
    keep_ref, send_ref = refs[parts:]
    for far, out in ((0, keep_ref), (1, send_ref)):
        out[...] = sum(ref[xh ^ far].astype(F32) for ref in refs[:parts]).astype(BF16)


def halves(*arrays):
    out = jax.ShapeDtypeStruct(arrays[0].shape[1:], BF16)
    return pl.pallas_call(
        lambda *refs: halves_kernel(len(arrays), *refs),
        out_shape=[out] * 2,
        compiler_params=PARAMS,
        cost_estimate=pl.CostEstimate(flops=2**18, bytes_accessed=2**20, transcendentals=0),
    )(*arrays)


def fill_kernel(done_ref, a_ref, b_ref, c_ref, d_ref, out_ref):
    del done_ref
    total = sum(ref[...].astype(F32) for ref in (a_ref, b_ref, c_ref, d_ref))
    out_ref[:, 0] = total.astype(BF16)


def fill(done, *parts):
    n_ja, slabs, block, channels = done.shape
    spec = pl.BlockSpec((n_ja, 1, block, channels), lambda i: (0, slabs - 1, 0, 0))
    return pl.pallas_call(
        fill_kernel,
        grid=(1,),
        in_specs=[pl.BlockSpec(memory_space=pl.ANY)] + [whole(a) for a in parts],
        out_specs=spec,
        out_shape=jax.ShapeDtypeStruct(done.shape, BF16),
        input_output_aliases={0: 0},
        compiler_params=PARAMS,
        cost_estimate=pl.CostEstimate(flops=2**18, bytes_accessed=2**20, transcendentals=0),
    )(done, *parts)


def final_kernel(
    pair_ref, both_ref, gain_ref, shift_ref, w_ref, out_ref
):
    rows, block, channels = pair_ref.shape
    n_ja = both_ref.shape[0]
    own = rows // n_ja
    tile = jnp.sum(both_ref[:, 2 * own].astype(F32), axis=0)
    tile = jnp.concatenate([tile[:rows], tile[rows:]], axis=1).astype(BF16).astype(F32)
    keep = line_mask(block, tile.shape[1])
    spread = jnp.concatenate(
        [
            jnp.where(keep, jnp.broadcast_to(tile[i : i + 1], keep.shape), 0.0).astype(BF16)
            for i in range(rows)
        ],
        axis=0,
    )
    w_back = spread_heads(w_ref, block)
    dn = [both_ref[:, 2 * i + 1][:, None] for i in range(own)]
    dn = jnp.concatenate(dn, axis=1).reshape(rows * block, channels).astype(F32)
    dn = dn + mm(spread, w_back)
    x = pair_ref[...].reshape(rows * block, channels).astype(F32)
    centred = x - jnp.mean(x, axis=-1, keepdims=True)
    rstd = lax.rsqrt(jnp.mean(centred * centred, axis=-1, keepdims=True) + EPSILON)
    unit = centred * rstd
    push = dn * gain_ref[...]
    along = jnp.mean(push * unit, axis=-1, keepdims=True)
    level = jnp.mean(push, axis=-1, keepdims=True)
    out_ref[...] = ((push - level - unit * along) * rstd).reshape(out_ref.shape)


def final(pair, both, gain, shift_row, bias_weight):
    return pl.pallas_call(
        final_kernel,
        out_shape=jax.ShapeDtypeStruct(pair.shape, F32),
        compiler_params=PARAMS,
        cost_estimate=pl.CostEstimate(
            flops=2**27, bytes_accessed=2**21, transcendentals=2**12
        ),
    )(pair, both, gain, shift_row, bias_weight)


def shards(
    pair,
    cotangent,
    norm_gain,
    norm_shift,
    query_weight,
    key_weight,
    value_weight,
    gate_weight,
    bias_weight,
    out_weight,
):
    rows_i, rows_j, channels = pair.shape
    heads = bias_weight.shape[1]
    n_ja = lax.axis_size(JA)
    own_i = rows_i // n_ja
    gain = norm_gain.reshape(1, channels)
    shift_row = norm_shift.reshape(1, channels)
    bias_rows = bias_weight.T
    weights = (query_weight, key_weight, value_weight, gate_weight)
    tie = lax.optimization_barrier

    both = lax.all_to_all(
        prep(pair, cotangent, gain, shift_row, bias_rows, n_ja), JA, 0, 0, tiled=True
    )

    def cross(a, bits):
        return lax.ppermute(a, ("xh", "core"), [(s, s ^ bits) for s in range(4)])

    own = both[:, 2 * own_i]
    far, own_swap, far_swap = cross(own, 2), cross(own, 1), cross(own, 3)
    projected = project(both, gain, shift_row, out_weight, weights)
    far, own_swap, far_swap, projected = tie((far, own_swap, far_swap, projected))
    *projected, gate = projected
    near = jnp.stack([own, far])
    prev, after = shift(near, "z", 1), shift(near, "z", 3)

    def slice_of(ahead, own, other):
        return attend(heads, ahead, projected, own, other)

    def joined(out, theirs):
        return (out[4].astype(F32) + theirs.astype(F32)).astype(BF16)

    out0 = slice_of(0, [own, far], [own_swap, far_swap])
    out0, prev, after = tie((out0, prev, after))
    opp0, opp1 = shift(prev[0], "z", 1), shift(after[1], "z", 3)
    prev_swap, after_swap, theirs0 = swap(prev), swap(after), swap(out0[5])
    out0, prev, prev_swap = tie((out0, prev, prev_swap))
    out1 = slice_of(3, [prev], [prev_swap])
    out1, opp0, opp1, after_swap, theirs0 = tie((out1, opp0, opp1, after_swap, theirs0))
    opp0_swap, opp1_swap, theirs1 = swap(opp0), swap(opp1), swap(out1[5])
    out2 = slice_of(1, [after], [after_swap])
    out2, opp0_swap, opp1_swap, theirs1 = tie((out2, opp0_swap, opp1_swap, theirs1))
    theirs2 = swap(out2[5])
    part1 = joined(out1, theirs1)
    theirs2, part1, opp0 = tie((theirs2, part1, opp0))
    part2 = joined(out2, theirs2)
    part2, opp0 = tie((part2, opp0))
    part1, part2 = shift(part1, "z", 3), shift(part2, "z", 1)
    out3 = slice_of(2, [opp0, opp1], [opp0_swap, opp1_swap])
    out3, part1, part2 = tie((out3, part1, part2))
    theirs3 = swap(out3[5])
    keep, send = halves(out0[4], theirs0, part1, part2)
    theirs3, keep, send = tie((theirs3, keep, send))
    opp_keep, opp_send = halves(out3[4], theirs3)
    flips = [(s, s ^ 5) for s in range(8)]
    opp_keep = shift(opp_keep, "z", 2)
    opp_send = lax.ppermute(opp_send, ("z", "xh"), flips)
    send = lax.ppermute(send, "xh", [(0, 1), (1, 0)])
    att, dq, dk, dv = zip(out0[:4], out1[:4], out2[:4], out3[:4])
    done = finish((0, 3, 1, 2), gate, both, out_weight, weights, att, dq, dk, dv)
    done, opp_keep, opp_send, send = tie((done, opp_keep, opp_send, send))
    done = fill(done, keep, send, opp_keep, opp_send)
    done = lax.all_to_all(done, JA, 0, 0, tiled=True)
    update = jnp.stack([done[:, 2 * i] for i in range(own_i)], axis=1).reshape(pair.shape)
    pair_grad = final(pair, done, gain, shift_row, bias_rows)
    return (update, pair_grad)


def solution(mesh):
    fine = Mesh(mesh.devices.reshape(4, 2, 2, 4, 2), IA + JA)
    spec = P(IA, JA, None)
    in_specs = (spec, spec) + (P(),) * 8
    return jax.shard_map(
        shards, mesh=fine, in_specs=in_specs, out_specs=(spec, spec), check_vma=False
    )
```

```python
import math

import jax
import jax.numpy as jnp
from jax import lax
from jax.experimental import pallas as pl
from jax.experimental.pallas import tpu as pltpu
from jax.sharding import Mesh, PartitionSpec as P

EPSILON = 1e-05
LOG2E = math.log2(math.e)
IA = ("z", "xh", "core")
JA = ("y", "xl")
F32 = jnp.float32
BF16 = jnp.bfloat16
LANES = 128
PARAMS = pltpu.CompilerParams(vmem_limit_bytes=24 * 1024 * 1024)
WIDE = pltpu.CompilerParams(vmem_limit_bytes=36 * 1024 * 1024)
FIRST = pltpu.CompilerParams(vmem_limit_bytes=60 * 1024 * 1024)


def normalize(values, norm_gain, norm_shift):
    mean_val = jnp.mean(values, axis=-1, keepdims=True)
    centred = values - mean_val
    variance = jnp.mean(centred * centred, axis=-1, keepdims=True)
    return centred * lax.rsqrt(variance + EPSILON) * norm_gain + norm_shift


def mm(a, b):
    return lax.dot_general(a, b, (((1,), (0,)), ((), ())), preferred_element_type=F32)


def mm_nt(a, b):
    return lax.dot_general(a, b, (((1,), (1,)), ((), ())), preferred_element_type=F32)


def mm_tn(a, b):
    return lax.dot_general(a, b, (((0,), (0,)), ((), ())), preferred_element_type=F32)


def swap(a):
    return lax.ppermute(a, "core", [(0, 1), (1, 0)])


def shift(a, axis, by):
    size = lax.axis_size(axis)
    return lax.ppermute(a, axis, [(s, (s + by) % size) for s in range(size)])


def in_hbm(*arrays):
    return [pltpu.with_memory_space_constraint(a, pltpu.HBM) for a in arrays]


def whole(a):
    return pl.BlockSpec(a.shape, lambda *_: (0,) * len(a.shape))


def line_mask(block, width):
    lane = lax.broadcasted_iota(jnp.int32, (block, width), 1)
    return lax.broadcasted_iota(jnp.int32, (block, width), 0) == lane % block


def spread_heads(w_ref, block):
    w = w_ref[...].astype(F32)
    shape = (block, w.shape[1])
    rows = [jnp.broadcast_to(w[h : h + 1], shape) for h in range(w.shape[0])]
    return jnp.concatenate(rows, axis=0).astype(BF16)


def prep_kernel(pair_ref, cot_ref, gain_ref, shift_ref, w_ref, out_ref):
    rows, block, channels = pair_ref.shape
    n_ja = out_ref.shape[0]
    own = rows // n_ja
    split = (n_ja, own, block, channels)
    out_ref[:, :own] = pair_ref[...].reshape(split)
    out_ref[:, own : 2 * own] = cot_ref[...].reshape(split)
    x = pair_ref[...].reshape(rows * block, channels).astype(F32)
    normed = normalize(x, gain_ref[...], shift_ref[...]).astype(BF16)
    every = mm_nt(normed, spread_heads(w_ref, block))
    width = every.shape[1]
    keep = line_mask(block, width)
    lines = []
    for i in range(rows):
        part = jnp.where(keep, every[i * block : (i + 1) * block], 0.0)
        lines.append(jnp.sum(part, axis=0, keepdims=True))
    tile = jnp.concatenate(lines, axis=0).astype(BF16)
    tile = jnp.concatenate([tile[:, :LANES], tile[:, LANES:]], axis=0)
    for d in range(n_ja):
        out_ref[d, 2 * own] = tile


def prep(pair, cot, gain, shift_row, bias_weight, n_ja):
    rows, block, channels = pair.shape
    out = jax.ShapeDtypeStruct((n_ja, 2 * rows // n_ja + 1, block, channels), BF16)
    return pl.pallas_call(
        prep_kernel,
        out_shape=out,
        compiler_params=FIRST,
        cost_estimate=pl.CostEstimate(
            flops=2**27, bytes_accessed=2**21, transcendentals=2**12
        ),
    )(pair, cot, gain, shift_row, bias_weight)


def project_kernel(
    pair_ref,
    cot_ref,
    gain_ref,
    shift_ref,
    w_o_ref,
    w_q_ref,
    w_k_ref,
    w_v_ref,
    w_g_ref,
    kv_n_ref,
    kv_t_ref,
    q_n_ref,
    q_t_ref,
    d_att_ref,
    gate_ref,
):
    n_blocks, _, block, channels = pair_ref.shape
    n = n_blocks * block
    inner = w_q_ref.shape[1]
    x = pair_ref[...].reshape(n, channels).astype(F32)
    normed = normalize(x, gain_ref[...], shift_ref[...]).astype(BF16)
    weights = [ref[...] for ref in (w_q_ref, w_k_ref, w_v_ref, w_g_ref)]
    proj = mm(normed, jnp.concatenate(weights[:3], axis=1)).astype(BF16)
    kv_n_ref[0] = proj[:, inner:]
    proj_t = mm_nt(jnp.concatenate([w.T for w in weights], axis=0), normed)
    kv_t_ref[0] = proj_t[inner : 3 * inner].astype(BF16)
    gate = jax.nn.sigmoid(proj_t[3 * inner :])
    gate_ref[0] = gate
    d_att = mm_nt(w_o_ref[...], cot_ref[...].reshape(n, channels)) * gate
    size = lax.axis_size("z")
    z = lax.axis_index("z")
    for owner in range(n // LANES):
        at = slice(owner * LANES, (owner + 1) * LANES)
        ahead = lax.rem(owner + size - z, size)
        q_n_ref[ahead, 0] = proj[at, :inner]
        q_t_ref[ahead, 0] = proj_t[:inner, at].astype(BF16)
        d_att_ref[ahead, 0] = d_att[:, at]


def project(both, gain, shift_row, w_o, weights):
    n_blocks, slabs, block, channels = both.shape
    rows = slabs // 2
    n = n_blocks * block
    inner = w_o.shape[0]
    kv_n = pltpu.HBM((rows, n, 2 * inner), BF16)
    kv_t = pltpu.HBM((rows, 2 * inner, n), BF16)
    gate = pltpu.HBM((rows, inner, n), F32)
    q_n = pltpu.HBM((n // LANES, rows, LANES, inner), BF16)
    q_t = pltpu.HBM((n // LANES, rows, inner, LANES), BF16)
    d_att = pltpu.HBM((n // LANES, rows, inner, LANES), F32)

    def by_row(a):
        return pl.BlockSpec((1,) + a.shape[1:], lambda i: (i, 0, 0))

    def sliced(a):
        return pl.BlockSpec((a.shape[0], 1) + a.shape[2:], lambda i: (0, i, 0, 0))

    return pl.pallas_call(
        project_kernel,
        grid=(rows,),
        in_specs=[
            pl.BlockSpec((n_blocks, 1, block, channels), lambda i: (0, i, 0, 0)),
            pl.BlockSpec((n_blocks, 1, block, channels), lambda i: (0, rows + i, 0, 0)),
        ]
        + [whole(a) for a in (gain, shift_row, w_o, *weights)],
        out_specs=[by_row(kv_n), by_row(kv_t)]
        + [sliced(a) for a in (q_n, q_t, d_att)]
        + [by_row(gate)],
        out_shape=[kv_n, kv_t, q_n, q_t, d_att, gate],
        compiler_params=PARAMS,
        cost_estimate=pl.CostEstimate(
            flops=2**31, bytes_accessed=8 * 2**20, transcendentals=2**18
        ),
    )(both, both, gain, shift_row, w_o, *weights)


def z_lanes(ahead):
    at = lax.rem(lax.axis_index("z") + ahead, lax.axis_size("z"))
    return pl.ds(pl.multiple_of(at * LANES, LANES), LANES)


def attend_kernel(heads, count, views, kv_n_hbm, kv_t_hbm, q_n_ref, q_t_ref, d_att_ref, *refs):
    bias_refs = refs[: count * 2 * views]
    refs = refs[count * 2 * views :]
    att_ref, dq_ref, dk_ref, dv_ref, mine_ref, theirs_ref = refs[:6]
    n_ref, t_ref, bias_s, gb_s, s_s, p_s, ds_s, tile_s, line_s, dk_s, dv_s, sems = refs[6:]
    at_slice = pl.program_id(0)
    row_count, n, wide_kv = n_ref.shape
    inner = wide_kv // 2
    head_dim = inner // heads
    scale = 1.0 / math.sqrt(head_dim)
    n_ja = tile_s.shape[0]
    block = n // n_ja
    rows_i = LANES // 4
    pairs = heads // 2
    wide = 2 * LANES
    core = lax.axis_index("core")
    xh = lax.axis_index("xh")
    copies = [
        pltpu.make_async_copy(src, dst, sems.at[e])
        for e, (src, dst) in enumerate(((kv_n_hbm, n_ref), (kv_t_hbm, t_ref)))
    ]

    @pl.when(at_slice == 0)
    def _():
        for copy in copies:
            copy.start()
        if count > 1:
            dk_s[...] = jnp.zeros_like(dk_s)
            dv_s[...] = jnp.zeros_like(dv_s)

    def sort_tiles(c):
        for which in range(2):
            base = (c * 2 + which) * views
            parts = []
            for ref in bias_refs[base : base + views]:
                parts += [ref] if len(ref.shape) == 3 else [ref.at[e] for e in range(2)]
            for far, ref in enumerate(parts):
                at = (xh ^ far) * 2 + (core ^ which)
                at = pl.ds(pl.multiple_of(at * rows_i, rows_i), rows_i)
                for owner in range(n_ja):
                    for p in range(pairs):
                        tile_s[owner, at, p * LANES : (p + 1) * LANES] = ref[
                            owner, p * rows_i : (p + 1) * rows_i, :
                        ]

    for c in range(count):
        pl.when(at_slice == c)(lambda c=c: sort_tiles(c))
    for owner in range(n_ja):
        for p in range(pairs):
            t = tile_s[owner, :, p * LANES : (p + 1) * LANES].astype(F32).T * LOG2E
            for e in range(2):
                h = p * 2 + e
                bias_s[owner * block : (owner + 1) * block, h * LANES : (h + 1) * LANES] = t[
                    e * block : (e + 1) * block
                ]

    @pl.when(at_slice == 0)
    def _():
        for copy in copies:
            copy.wait()

    nil = jnp.zeros((), BF16)
    row_head = lax.broadcasted_iota(jnp.int32, (inner, LANES), 0) // head_dim
    lane_head = lax.broadcasted_iota(jnp.int32, (LANES, inner), 1) // head_dim
    step = 16
    held = {}

    def cols_of(p):
        return slice(p * wide, (p + 1) * wide)

    def scores(r, p):
        q_blk = jnp.concatenate(
            [jnp.where(row_head == h, q_t_ref[0, r], nil) for h in (2 * p, 2 * p + 1)], axis=1
        )
        t = mm(n_ref[r, :, :inner], q_blk) * (scale * LOG2E) + bias_s[:, cols_of(p)]
        s_s[r, :, cols_of(p)] = t
        top = t[:8]
        for e in range(8, n, 8):
            top = jnp.maximum(top, t[e : e + 8])
        held["top", r, p] = jnp.max(top, axis=0, keepdims=True)

    def weights(r, p):
        total = jnp.zeros((8, wide), F32)
        for k in range(0, n, step):
            e = jnp.exp2(s_s[r, k : k + step, cols_of(p)] - held["top", r, p])
            s_s[r, k : k + step, cols_of(p)] = e
            p_s[r, k : k + step, cols_of(p)] = e.astype(BF16)
            total = total + (e[:8] + e[8:])
        held["inv", r, p] = 1.0 / jnp.sum(total, axis=0, keepdims=True)

    def attended(r, p):
        first = 2 * p * head_dim
        rows = slice(first, first + 2 * head_dim)
        inv = held["inv", r, p]
        att = mm(t_ref[r, inner + first : inner + first + 2 * head_dim, :], p_s[r, :, cols_of(p)])
        att = att * inv
        d_att = d_att_ref[0, r, rows, :]
        a_two = jnp.concatenate([d_att, d_att], axis=1) * inv
        lane = lax.broadcasted_iota(jnp.int32, a_two.shape, 1) // LANES
        sub = lax.broadcasted_iota(jnp.int32, a_two.shape, 0) // head_dim
        a_two = jnp.where(lane == sub, a_two, 0.0).astype(BF16)
        held["diag", r, p] = jnp.sum(a_two.astype(F32) * att, axis=0, keepdims=True)
        for e in range(2):
            h = 2 * p + e
            att_ref[0, r, h * head_dim : (h + 1) * head_dim, :] = att[
                e * head_dim : (e + 1) * head_dim, e * LANES : (e + 1) * LANES
            ]
        lead = [jnp.zeros((first, wide), BF16)] if p else []
        tail = [jnp.zeros((inner - first - 2 * head_dim, wide), BF16)] if p + 1 < pairs else []
        held["a", r, p] = jnp.concatenate(lead + [a_two] + tail, axis=0)

    def d_scores(r, p):
        dp = mm(n_ref[r, :, inner:], held["a", r, p])
        for k in range(0, n, step):
            ds = s_s[r, k : k + step, cols_of(p)] * (dp[k : k + step] - held["diag", r, p])
            if r == 0:
                gb_s[k : k + step, cols_of(p)] = ds
            else:
                gb_s[k : k + step, cols_of(p)] += ds
            ds_s[r, k : k + step, cols_of(p)] = ds.astype(BF16)

    def d_query(r, p):
        first = 2 * p * head_dim
        dq = mm(t_ref[r, first : first + 2 * head_dim, :], ds_s[r, :, cols_of(p)]) * scale
        for e in range(2):
            h = 2 * p + e
            dq_ref[0, r, h * head_dim : (h + 1) * head_dim, :] = dq[
                e * head_dim : (e + 1) * head_dim, e * LANES : (e + 1) * LANES
            ].astype(BF16)

    def gather(r, p, name, part, sum_s, out_ref, factor):
        if p:
            part = part + held.pop((name, r))
        if p + 1 < pairs:
            held[name, r] = part
            return
        if count > 1:
            part = part + sum_s[r]
            sum_s[r] = part
        out_ref[r] = (part * factor).astype(BF16)

    def d_key(r, p):
        q_row = jnp.concatenate(
            [jnp.where(lane_head == h, q_n_ref[0, r], nil) for h in (2 * p, 2 * p + 1)], axis=0
        )
        gather(r, p, "dk", mm(ds_s[r, :, cols_of(p)], q_row), dk_s, dk_ref, scale)

    def d_value(r, p):
        part = mm(p_s[r, :, cols_of(p)], held["a", r, p].T)
        gather(r, p, "dv", part, dv_s, dv_ref, 1.0)

    order = [
        (scores, 0),
        (scores, 1),
        (weights, 0),
        (attended, 0),
        (weights, 1),
        (d_scores, 0),
        (attended, 1),
        (d_value, 0),
        (d_scores, 1),
        (d_query, 0),
        (d_key, 0),
        (d_value, 1),
        (d_query, 1),
        (d_key, 1),
    ]
    lag = 5
    for t in range(len(order) + lag * (row_count - 1)):
        for r in range(row_count):
            if 0 <= t - lag * r < len(order):
                phase, p = order[t - lag * r]
                phase(r, p)

    for owner in range(n_ja):
        for p in range(pairs):
            t = jnp.concatenate(
                [
                    gb_s[owner * block : (owner + 1) * block, h * LANES : (h + 1) * LANES]
                    for h in (2 * p, 2 * p + 1)
                ],
                axis=0,
            )
            line_s[:, p * LANES : (p + 1) * LANES] = t.T.astype(BF16)
        for far in range(2):
            for ref, which in ((mine_ref, core), (theirs_ref, 1 - core)):
                at = pl.multiple_of((far * 2 + which) * rows_i, rows_i)
                for p in range(pairs):
                    ref[0, far, owner, p * rows_i : (p + 1) * rows_i, :] = line_s[
                        pl.ds(at, rows_i), p * LANES : (p + 1) * LANES
                    ]


def attend(heads, aheads, projected, bias):
    rows, n, inner = projected[0].shape
    inner = inner // 2
    count = len(aheads)
    leap = aheads[1] - aheads[0] if count > 1 else 0
    views = len(bias[0][0])
    flat = [a for slice_of in bias for side in slice_of for a in side]
    n_ja, slab, _ = flat[0].shape[-3:]
    lines = heads * n // n_ja
    att = jax.ShapeDtypeStruct((count, rows, inner, LANES), F32)
    dq = jax.ShapeDtypeStruct((count, rows, inner, LANES), BF16)
    grad = jax.ShapeDtypeStruct((rows, n, inner), BF16)
    gb = jax.ShapeDtypeStruct((count, 2, n_ja, slab, LANES), BF16)
    sums = (rows, n, inner) if count > 1 else (1, 8, LANES)

    def by_slice(a):
        return pl.BlockSpec((1,) + a.shape[1:], lambda i: (i,) + (0,) * (len(a.shape) - 1))

    def sliced(a):
        return pl.BlockSpec((1,) + a.shape[1:], lambda i: (aheads[0] + leap * i, 0, 0, 0))

    return pl.pallas_call(
        lambda *refs: attend_kernel(heads, count, views, *refs),
        grid=(count,),
        in_specs=[pl.BlockSpec(memory_space=pl.ANY)] * 2
        + [sliced(a) for a in projected[2:]]
        + [whole(a) for a in flat],
        out_specs=[by_slice(att), by_slice(dq), whole(grad), whole(grad)] + [by_slice(gb)] * 2,
        out_shape=[att, dq, grad, grad, gb, gb],
        scratch_shapes=[
            pltpu.VMEM((rows, n, 2 * inner), BF16),
            pltpu.VMEM((rows, 2 * inner, n), BF16),
            pltpu.VMEM((n, heads * LANES), F32),
            pltpu.VMEM((n, heads * LANES), F32),
            pltpu.VMEM((rows, n, heads * LANES), F32),
            pltpu.VMEM((rows, n, heads * LANES), BF16),
            pltpu.VMEM((rows, n, heads * LANES), BF16),
            pltpu.VMEM((n_ja, LANES, lines), BF16),
            pltpu.VMEM((LANES, lines), BF16),
            pltpu.VMEM(sums, F32),
            pltpu.VMEM(sums, F32),
            pltpu.SemaphoreType.DMA((2,)),
        ],
        compiler_params=WIDE,
        cost_estimate=pl.CostEstimate(
            flops=count * 2**32, bytes_accessed=2**23, transcendentals=count * 2**20
        ),
    )(*in_hbm(*projected), *flat)


def finish_kernel(
    aheads, gate_ref, cot_ref, w_o_ref, w_q_ref, w_k_ref, w_v_ref, w_g_ref, *refs
):
    count = len(aheads)
    att_refs, dq_refs = refs[:count], refs[count : 2 * count]
    dk_refs, dv_refs = refs[2 * count : 3 * count], refs[3 * count : 4 * count]
    out_ref, att_s, dq_s = refs[4 * count :]
    for group, att_ref, dq_ref in zip(aheads, att_refs, dq_refs):
        for c, ahead in enumerate(group):
            at = z_lanes(ahead)
            att_s[:, at] = att_ref[c, 0]
            dq_s[:, at] = dq_ref[c, 0]
    half = (out_ref.shape[0],) + out_ref.shape[2:]
    gate = gate_ref[0]
    cot = cot_ref[...].reshape(gate.shape[1], cot_ref.shape[3])
    d_gated = mm_nt(w_o_ref[...], cot)
    att = att_s[...]
    update = mm_tn((gate * att).astype(BF16), w_o_ref[...])
    out_ref[:, 0] = update.astype(BF16).reshape(half)
    d_gate = (d_gated * att * gate * (1.0 - gate)).astype(BF16)
    left_t = jnp.concatenate([dq_s[...], d_gate], axis=0)
    dk = sum(ref[0].astype(F32) for ref in dk_refs).astype(BF16)
    dv = sum(ref[0].astype(F32) for ref in dv_refs).astype(BF16)
    dn = mm_tn(left_t, jnp.concatenate([w_q_ref[...].T, w_g_ref[...].T], axis=0))
    dn = dn + mm(
        jnp.concatenate([dk, dv], axis=1),
        jnp.concatenate([w_k_ref[...].T, w_v_ref[...].T], axis=0),
    )
    out_ref[:, 1] = dn.astype(BF16).reshape(half)


def finish(aheads, gate, both, w_o, weights, att, dq, dk, dv):
    n_blocks, _, block, channels = both.shape
    rows, inner, _ = gate.shape
    arrays = (*att, *dq, *dk, *dv)

    def by_row(a):
        return pl.BlockSpec((1,) + a.shape[1:], lambda i: (i, 0, 0))

    def by_slices(a):
        return pl.BlockSpec((a.shape[0], 1) + a.shape[2:], lambda i: (0, i, 0, 0))

    cot_spec = pl.BlockSpec((n_blocks, 1, block, channels), lambda i: (0, rows + i, 0, 0))
    return pl.pallas_call(
        lambda *refs: finish_kernel(aheads, *refs),
        grid=(rows,),
        in_specs=[by_row(gate), cot_spec, whole(w_o)]
        + [whole(a) for a in weights]
        + [by_slices(a) for a in (*att, *dq)]
        + [by_row(a) for a in (*dk, *dv)],
        out_specs=pl.BlockSpec((n_blocks, 2, block, channels), lambda i: (0, i, 0, 0)),
        out_shape=jax.ShapeDtypeStruct((n_blocks, 2 * rows + 1, block, channels), BF16),
        scratch_shapes=[
            pltpu.VMEM((inner, n_blocks * block), F32),
            pltpu.VMEM((inner, n_blocks * block), BF16),
        ],
        compiler_params=PARAMS,
        cost_estimate=pl.CostEstimate(flops=2**31, bytes_accessed=2**23, transcendentals=0),
    )(*in_hbm(gate), both, w_o, *weights, *arrays)


def halves_kernel(parts, *refs):
    xh = lax.axis_index("xh")
    keep_ref, send_ref = refs[parts:]
    for far, out in ((0, keep_ref), (1, send_ref)):
        out[...] = sum(ref[xh ^ far].astype(F32) for ref in refs[:parts]).astype(BF16)


def halves(*arrays):
    out = jax.ShapeDtypeStruct(arrays[0].shape[1:], BF16)
    return pl.pallas_call(
        lambda *refs: halves_kernel(len(arrays), *refs),
        out_shape=[out] * 2,
        compiler_params=PARAMS,
        cost_estimate=pl.CostEstimate(flops=2**18, bytes_accessed=2**20, transcendentals=0),
    )(*arrays)


def fill_kernel(done_ref, a_ref, b_ref, c_ref, d_ref, out_ref):
    del done_ref
    total = sum(ref[...].astype(F32) for ref in (a_ref, b_ref, c_ref, d_ref))
    out_ref[:, 0] = total.astype(BF16)


def fill(done, *parts):
    n_ja, slabs, block, channels = done.shape
    spec = pl.BlockSpec((n_ja, 1, block, channels), lambda i: (0, slabs - 1, 0, 0))
    return pl.pallas_call(
        fill_kernel,
        grid=(1,),
        in_specs=[pl.BlockSpec(memory_space=pl.ANY)] + [whole(a) for a in parts],
        out_specs=spec,
        out_shape=jax.ShapeDtypeStruct(done.shape, BF16),
        input_output_aliases={0: 0},
        compiler_params=PARAMS,
        cost_estimate=pl.CostEstimate(flops=2**18, bytes_accessed=2**20, transcendentals=0),
    )(done, *parts)


def final_kernel(
    pair_ref, both_ref, gain_ref, shift_ref, w_ref, out_ref
):
    rows, block, channels = pair_ref.shape
    n_ja = both_ref.shape[0]
    own = rows // n_ja
    tile = jnp.sum(both_ref[:, 2 * own].astype(F32), axis=0)
    tile = jnp.concatenate([tile[:rows], tile[rows:]], axis=1).astype(BF16).astype(F32)
    keep = line_mask(block, tile.shape[1])
    spread = jnp.concatenate(
        [
            jnp.where(keep, jnp.broadcast_to(tile[i : i + 1], keep.shape), 0.0).astype(BF16)
            for i in range(rows)
        ],
        axis=0,
    )
    w_back = spread_heads(w_ref, block)
    dn = [both_ref[:, 2 * i + 1][:, None] for i in range(own)]
    dn = jnp.concatenate(dn, axis=1).reshape(rows * block, channels).astype(F32)
    dn = dn + mm(spread, w_back)
    x = pair_ref[...].reshape(rows * block, channels).astype(F32)
    centred = x - jnp.mean(x, axis=-1, keepdims=True)
    rstd = lax.rsqrt(jnp.mean(centred * centred, axis=-1, keepdims=True) + EPSILON)
    unit = centred * rstd
    push = dn * gain_ref[...]
    along = jnp.mean(push * unit, axis=-1, keepdims=True)
    level = jnp.mean(push, axis=-1, keepdims=True)
    out_ref[...] = ((push - level - unit * along) * rstd).reshape(out_ref.shape)


def final(pair, both, gain, shift_row, bias_weight):
    return pl.pallas_call(
        final_kernel,
        out_shape=jax.ShapeDtypeStruct(pair.shape, F32),
        compiler_params=PARAMS,
        cost_estimate=pl.CostEstimate(
            flops=2**27, bytes_accessed=2**21, transcendentals=2**12
        ),
    )(pair, both, gain, shift_row, bias_weight)


def shards(
    pair,
    cotangent,
    norm_gain,
    norm_shift,
    query_weight,
    key_weight,
    value_weight,
    gate_weight,
    bias_weight,
    out_weight,
):
    rows_i, rows_j, channels = pair.shape
    heads = bias_weight.shape[1]
    n_ja = lax.axis_size(JA)
    own_i = rows_i // n_ja
    gain = norm_gain.reshape(1, channels)
    shift_row = norm_shift.reshape(1, channels)
    bias_rows = bias_weight.T
    weights = (query_weight, key_weight, value_weight, gate_weight)
    tie = lax.optimization_barrier

    both = lax.all_to_all(
        prep(pair, cotangent, gain, shift_row, bias_rows, n_ja), JA, 0, 0, tiled=True
    )

    def joined(mine, theirs):
        return (mine.astype(F32) + theirs.astype(F32)).astype(BF16)

    own = both[:, 2 * own_i]
    far = lax.ppermute(own, "xh", [(0, 1), (1, 0)])
    projected = project(both, gain, shift_row, out_weight, weights)
    far, projected = tie((far, projected))
    *projected, gate = projected
    near = jnp.stack([own, far])
    near_swap = swap(near)
    prev, after = shift(near, "z", 1), shift(near, "z", 3)

    groups = ((0,), (3, 1), (2,))
    out0 = attend(heads, groups[0], projected, [([near], [near_swap])])
    out0, prev, after = tie((out0, prev, after))
    prev_swap, after_swap = swap(prev), swap(after)
    opp0, opp1 = shift(prev[0], "z", 1), shift(after[1], "z", 3)
    theirs0 = swap(out0[5])
    out0, prev, prev_swap, after, after_swap = tie((out0, prev, prev_swap, after, after_swap))
    out1 = attend(
        heads, groups[1], projected, [([prev], [prev_swap]), ([after], [after_swap])]
    )
    out1, opp0, opp1, theirs0 = tie((out1, opp0, opp1, theirs0))
    opp0_swap, opp1_swap, theirs1 = swap(opp0), swap(opp1), swap(out1[5])
    theirs1, opp0_swap, opp1_swap = tie((theirs1, opp0_swap, opp1_swap))
    part1 = joined(out1[4], theirs1)
    part1, opp0 = tie((part1, opp0))
    part1, part2 = shift(part1[0], "z", 3), shift(part1[1], "z", 1)
    out3 = attend(heads, groups[2], projected, [([opp0, opp1], [opp0_swap, opp1_swap])])
    out3, part1, part2 = tie((out3, part1, part2))
    theirs3 = swap(out3[5])
    keep, send = halves(out0[4][0], theirs0[0], part1, part2)
    theirs3, keep, send = tie((theirs3, keep, send))
    opp_keep, opp_send = halves(out3[4][0], theirs3[0])
    flips = [(s, s ^ 5) for s in range(8)]
    opp_keep = shift(opp_keep, "z", 2)
    opp_send = lax.ppermute(opp_send, ("z", "xh"), flips)
    send = lax.ppermute(send, "xh", [(0, 1), (1, 0)])
    att, dq, dk, dv = zip(out0[:4], out1[:4], out3[:4])
    done = finish(groups, gate, both, out_weight, weights, att, dq, dk, dv)
    done, opp_keep, opp_send, send = tie((done, opp_keep, opp_send, send))
    done = fill(done, keep, send, opp_keep, opp_send)
    done = lax.all_to_all(done, JA, 0, 0, tiled=True)
    update = jnp.stack([done[:, 2 * i] for i in range(own_i)], axis=1).reshape(pair.shape)
    pair_grad = final(pair, done, gain, shift_row, bias_rows)
    return (update, pair_grad)


def solution(mesh):
    fine = Mesh(mesh.devices.reshape(4, 2, 2, 4, 2), IA + JA)
    spec = P(IA, JA, None)
    in_specs = (spec, spec) + (P(),) * 8
    return jax.shard_map(
        shards, mesh=fine, in_specs=in_specs, out_specs=(spec, spec), check_vma=False
    )
```

```python
import math

import jax
import jax.numpy as jnp
from jax import lax
from jax.experimental import pallas as pl
from jax.experimental.pallas import tpu as pltpu
from jax.sharding import Mesh, PartitionSpec as P

EPSILON = 1e-05
LOG2E = math.log2(math.e)
IA = ("z", "xh", "core")
JA = ("y", "xl")
F32 = jnp.float32
BF16 = jnp.bfloat16
LANES = 128
PARAMS = pltpu.CompilerParams(vmem_limit_bytes=24 * 1024 * 1024)
WIDE = pltpu.CompilerParams(vmem_limit_bytes=36 * 1024 * 1024)
FIRST = pltpu.CompilerParams(vmem_limit_bytes=60 * 1024 * 1024)


def mm(a, b):
    return lax.dot_general(a, b, (((1,), (0,)), ((), ())), preferred_element_type=F32)


def mm_nt(a, b):
    return lax.dot_general(a, b, (((1,), (1,)), ((), ())), preferred_element_type=F32)


def mm_tn(a, b):
    return lax.dot_general(a, b, (((0,), (0,)), ((), ())), preferred_element_type=F32)


def centre(rows):
    channels = rows.shape[1]
    share = jnp.full((channels, channels), 1.0 / channels, BF16)
    centred = rows.astype(F32) - mm(rows, share)
    variance = jnp.mean(centred * centred, axis=-1, keepdims=True)
    return centred, lax.rsqrt(variance + EPSILON)


def normalize(rows, norm_gain, norm_shift):
    centred, rstd = centre(rows)
    return (centred * rstd * norm_gain + norm_shift).astype(BF16)


def swap(a):
    return lax.ppermute(a, "core", [(0, 1), (1, 0)])


def shift(a, axis, by):
    size = lax.axis_size(axis)
    return lax.ppermute(a, axis, [(s, (s + by) % size) for s in range(size)])


def in_hbm(*arrays):
    return [pltpu.with_memory_space_constraint(a, pltpu.HBM) for a in arrays]


def whole(a):
    return pl.BlockSpec(a.shape, lambda *_: (0,) * len(a.shape))


def line_mask(block, width):
    lane = lax.broadcasted_iota(jnp.int32, (block, width), 1)
    return lax.broadcasted_iota(jnp.int32, (block, width), 0) == lane % block


def spread_heads(w_ref, block):
    w = w_ref[...].astype(F32)
    shape = (block, w.shape[1])
    rows = [jnp.broadcast_to(w[h : h + 1], shape) for h in range(w.shape[0])]
    return jnp.concatenate(rows, axis=0).astype(BF16)


def prep_kernel(pair_ref, gain_ref, shift_ref, w_ref, tile_ref):
    rows, block, channels = pair_ref.shape
    x = pair_ref[...].reshape(rows * block, channels)
    normed = normalize(x, gain_ref[...], shift_ref[...])
    every = mm_nt(normed, spread_heads(w_ref, block))
    width = every.shape[1]
    keep = line_mask(block, width)
    lines = []
    for i in range(rows):
        part = jnp.where(keep, every[i * block : (i + 1) * block], 0.0)
        lines.append(jnp.sum(part, axis=0, keepdims=True))
    tile = jnp.concatenate(lines, axis=0).astype(BF16)
    tile = jnp.concatenate([tile[:, :LANES], tile[:, LANES:]], axis=0)
    for d in range(tile_ref.shape[0]):
        tile_ref[d] = tile


def prep(pair, gain, shift_row, bias_weight, copies):
    rows, block, channels = pair.shape
    return pl.pallas_call(
        prep_kernel,
        out_shape=jax.ShapeDtypeStruct((copies, block, channels), BF16),
        compiler_params=FIRST,
        cost_estimate=pl.CostEstimate(
            flops=2**27, bytes_accessed=2**20, transcendentals=2**12
        ),
    )(pair, gain, shift_row, bias_weight)


def pack_kernel(pair_ref, cot_ref, out_ref):
    group, slabs, block, channels = out_ref.shape
    own = slabs // 2
    out_ref[:, :own] = pair_ref[...].reshape(group, own, block, channels)
    out_ref[:, own:] = cot_ref[...].reshape(group, own, block, channels)


def pack(pair, cot, n_ja):
    rows, block, channels = pair.shape
    own = rows // n_ja
    group = n_ja // 2
    part = pl.BlockSpec((group * own, block, channels), lambda d: (d, 0, 0))
    return pl.pallas_call(
        pack_kernel,
        grid=(n_ja // group,),
        in_specs=[part, part],
        out_specs=pl.BlockSpec((group, 2 * own, block, channels), lambda d: (d, 0, 0, 0)),
        out_shape=jax.ShapeDtypeStruct((n_ja, 2 * own, block, channels), BF16),
        compiler_params=FIRST,
        cost_estimate=pl.CostEstimate(flops=2**10, bytes_accessed=2**21, transcendentals=0),
    )(pair, cot)


def project_kernel(
    pair_ref,
    cot_ref,
    gain_ref,
    shift_ref,
    w_o_ref,
    w_q_ref,
    w_k_ref,
    w_v_ref,
    w_g_ref,
    kv_n_ref,
    kv_t_ref,
    q_n_ref,
    q_t_ref,
    d_att_ref,
    gate_ref,
):
    n_blocks, group, block, channels = pair_ref.shape
    n = n_blocks * block
    inner = w_q_ref.shape[1]
    weights = [ref[...] for ref in (w_q_ref, w_k_ref, w_v_ref, w_g_ref)]
    w_n = jnp.concatenate(weights[:3], axis=1)
    w_t = jnp.concatenate([w.T for w in weights], axis=0)
    size = lax.axis_size("z")
    z = lax.axis_index("z")
    for r in range(group):
        normed = normalize(pair_ref[:, r].reshape(n, channels), gain_ref[...], shift_ref[...])
        proj = mm(normed, w_n).astype(BF16)
        kv_n_ref[r] = proj[:, inner:]
        proj_t = mm_nt(w_t, normed)
        kv_t_ref[r] = proj_t[inner : 3 * inner].astype(BF16)
        gate = jax.nn.sigmoid(proj_t[3 * inner :])
        gate_ref[r] = gate
        d_att = mm_nt(w_o_ref[...], cot_ref[:, r].reshape(n, channels)) * gate
        for owner in range(n // LANES):
            at = slice(owner * LANES, (owner + 1) * LANES)
            ahead = lax.rem(owner + size - z, size)
            q_n_ref[ahead, r] = proj[at, :inner]
            q_t_ref[ahead, r] = proj_t[:inner, at].astype(BF16)
            d_att_ref[ahead, r] = d_att[:, at]


def project(both, gain, shift_row, w_o, weights):
    n_blocks, slabs, block, channels = both.shape
    rows = slabs // 2
    group = 2
    n = n_blocks * block
    inner = w_o.shape[0]
    kv_n = pltpu.HBM((rows, n, 2 * inner), BF16)
    kv_t = pltpu.HBM((rows, 2 * inner, n), BF16)
    gate = pltpu.HBM((rows, inner, n), F32)
    q_n = pltpu.HBM((n // LANES, rows, LANES, inner), BF16)
    q_t = pltpu.HBM((n // LANES, rows, inner, LANES), BF16)
    d_att = pltpu.HBM((n // LANES, rows, inner, LANES), F32)

    def by_row(a):
        return pl.BlockSpec((group,) + a.shape[1:], lambda i: (i, 0, 0))

    def sliced(a):
        return pl.BlockSpec((a.shape[0], group) + a.shape[2:], lambda i: (0, i, 0, 0))

    return pl.pallas_call(
        project_kernel,
        grid=(rows // group,),
        in_specs=[
            pl.BlockSpec((n_blocks, group, block, channels), lambda i: (0, i, 0, 0)),
            pl.BlockSpec(
                (n_blocks, group, block, channels), lambda i: (0, rows // group + i, 0, 0)
            ),
        ]
        + [whole(a) for a in (gain, shift_row, w_o, *weights)],
        out_specs=[by_row(kv_n), by_row(kv_t)]
        + [sliced(a) for a in (q_n, q_t, d_att)]
        + [by_row(gate)],
        out_shape=[kv_n, kv_t, q_n, q_t, d_att, gate],
        compiler_params=PARAMS,
        cost_estimate=pl.CostEstimate(
            flops=2**31, bytes_accessed=8 * 2**20, transcendentals=2**18
        ),
    )(both, both, gain, shift_row, w_o, *weights)


def z_lanes(ahead):
    at = lax.rem(lax.axis_index("z") + ahead, lax.axis_size("z"))
    return pl.ds(pl.multiple_of(at * LANES, LANES), LANES)


def attend_kernel(heads, count, views, kv_n_hbm, kv_t_hbm, q_n_ref, q_t_ref, d_att_ref, *refs):
    bias_refs = refs[: count * 2 * views]
    refs = refs[count * 2 * views :]
    att_ref, dq_ref, dk_ref, dv_ref, mine_ref, theirs_ref = refs[:6]
    n_ref, t_ref, bias_s, gb_s, s_s, p_s, ds_s, tile_s, line_s, dk_s, dv_s, sems = refs[6:]
    at_slice = pl.program_id(0)
    row_count, n, wide_kv = n_ref.shape
    inner = wide_kv // 2
    head_dim = inner // heads
    scale = 1.0 / math.sqrt(head_dim)
    n_ja = tile_s.shape[0]
    block = n // n_ja
    rows_i = LANES // 4
    pairs = heads // 2
    wide = 2 * LANES
    core = lax.axis_index("core")
    copies = [
        pltpu.make_async_copy(src, dst, sems.at[e])
        for e, (src, dst) in enumerate(((kv_n_hbm, n_ref), (kv_t_hbm, t_ref)))
    ]

    @pl.when(at_slice == 0)
    def _():
        for copy in copies:
            copy.start()
        if count > 1:
            dk_s[...] = jnp.zeros_like(dk_s)
            dv_s[...] = jnp.zeros_like(dv_s)

    def sort_tiles(c):
        for which in range(2):
            base = (c * 2 + which) * views
            parts = []
            for ref in bias_refs[base : base + views]:
                parts += [ref] if len(ref.shape) == 3 else [ref.at[e] for e in range(2)]
            for far, ref in enumerate(parts):
                at = far * 2 + (core ^ which)
                at = pl.ds(pl.multiple_of(at * rows_i, rows_i), rows_i)
                for owner in range(n_ja):
                    for p in range(pairs):
                        tile_s[owner, at, p * LANES : (p + 1) * LANES] = ref[
                            owner, p * rows_i : (p + 1) * rows_i, :
                        ]

    for c in range(count):
        pl.when(at_slice == c)(lambda c=c: sort_tiles(c))
    for owner in range(n_ja):
        for p in range(pairs):
            t = tile_s[owner, :, p * LANES : (p + 1) * LANES].T.astype(F32) * LOG2E
            for e in range(2):
                h = p * 2 + e
                bias_s[owner * block : (owner + 1) * block, h * LANES : (h + 1) * LANES] = t[
                    e * block : (e + 1) * block
                ]

    @pl.when(at_slice == 0)
    def _():
        for copy in copies:
            copy.wait()

    nil = jnp.zeros((), BF16)
    row_head = lax.broadcasted_iota(jnp.int32, (inner, LANES), 0) // head_dim
    lane_head = lax.broadcasted_iota(jnp.int32, (LANES, inner), 1) // head_dim
    step = 16
    held = {}

    def cols_of(p):
        return slice(p * wide, (p + 1) * wide)

    def scores(r, p):
        q_blk = jnp.concatenate(
            [jnp.where(row_head == h, q_t_ref[0, r], nil) for h in (2 * p, 2 * p + 1)], axis=1
        )
        t = mm(n_ref[r, :, :inner], q_blk) * (scale * LOG2E) + bias_s[:, cols_of(p)]
        s_s[r, :, cols_of(p)] = t
        top = t[:8]
        for e in range(8, n, 8):
            top = jnp.maximum(top, t[e : e + 8])
        held["top", r, p] = jnp.max(top, axis=0, keepdims=True)

    def weights(r, p):
        total = jnp.zeros((8, wide), F32)
        for k in range(0, n, step):
            e = jnp.exp2(s_s[r, k : k + step, cols_of(p)] - held["top", r, p])
            s_s[r, k : k + step, cols_of(p)] = e
            p_s[r, k : k + step, cols_of(p)] = e.astype(BF16)
            total = total + (e[:8] + e[8:])
        held["inv", r, p] = 1.0 / jnp.sum(total, axis=0, keepdims=True)

    def attended(r, p):
        first = 2 * p * head_dim
        rows = slice(first, first + 2 * head_dim)
        inv = held["inv", r, p]
        att = mm(t_ref[r, inner + first : inner + first + 2 * head_dim, :], p_s[r, :, cols_of(p)])
        att = att * inv
        d_att = d_att_ref[0, r, rows, :]
        a_two = jnp.concatenate([d_att, d_att], axis=1) * inv
        lane = lax.broadcasted_iota(jnp.int32, a_two.shape, 1) // LANES
        sub = lax.broadcasted_iota(jnp.int32, a_two.shape, 0) // head_dim
        a_two = jnp.where(lane == sub, a_two, 0.0).astype(BF16)
        held["diag", r, p] = jnp.sum(a_two.astype(F32) * att, axis=0, keepdims=True)
        for e in range(2):
            h = 2 * p + e
            att_ref[0, r, h * head_dim : (h + 1) * head_dim, :] = att[
                e * head_dim : (e + 1) * head_dim, e * LANES : (e + 1) * LANES
            ]
        lead = [jnp.zeros((first, wide), BF16)] if p else []
        tail = [jnp.zeros((inner - first - 2 * head_dim, wide), BF16)] if p + 1 < pairs else []
        held["a", r, p] = jnp.concatenate(lead + [a_two] + tail, axis=0)

    def d_scores(r, p):
        dp = mm(n_ref[r, :, inner:], held["a", r, p])
        for k in range(0, n, step):
            ds = s_s[r, k : k + step, cols_of(p)] * (dp[k : k + step] - held["diag", r, p])
            if r == 0:
                gb_s[k : k + step, cols_of(p)] = ds
            else:
                gb_s[k : k + step, cols_of(p)] += ds
            ds_s[r, k : k + step, cols_of(p)] = ds.astype(BF16)

    def d_query(r, p):
        first = 2 * p * head_dim
        dq = mm(t_ref[r, first : first + 2 * head_dim, :], ds_s[r, :, cols_of(p)]) * scale
        for e in range(2):
            h = 2 * p + e
            dq_ref[0, r, h * head_dim : (h + 1) * head_dim, :] = dq[
                e * head_dim : (e + 1) * head_dim, e * LANES : (e + 1) * LANES
            ].astype(BF16)

    def gather(r, p, name, part, sum_s, out_ref, factor):
        if p:
            part = part + held.pop((name, r))
        if p + 1 < pairs:
            held[name, r] = part
            return
        if count > 1:
            part = part + sum_s[r]
            sum_s[r] = part
        out_ref[r] = (part * factor).astype(BF16)

    def d_key(r, p):
        q_row = jnp.concatenate(
            [jnp.where(lane_head == h, q_n_ref[0, r], nil) for h in (2 * p, 2 * p + 1)], axis=0
        )
        gather(r, p, "dk", mm(ds_s[r, :, cols_of(p)], q_row), dk_s, dk_ref, scale)

    def d_value(r, p):
        part = mm(p_s[r, :, cols_of(p)], held["a", r, p].T)
        gather(r, p, "dv", part, dv_s, dv_ref, 1.0)

    order = [
        (scores, 0),
        (scores, 1),
        (weights, 0),
        (attended, 0),
        (weights, 1),
        (d_scores, 0),
        (attended, 1),
        (d_value, 0),
        (d_scores, 1),
        (d_query, 0),
        (d_key, 0),
        (d_value, 1),
        (d_query, 1),
        (d_key, 1),
    ]
    lag = 5
    for t in range(len(order) + lag * (row_count - 1)):
        for r in range(row_count):
            if 0 <= t - lag * r < len(order):
                phase, p = order[t - lag * r]
                phase(r, p)

    for owner in range(n_ja):
        for p in range(pairs):
            t = jnp.concatenate(
                [
                    gb_s[owner * block : (owner + 1) * block, h * LANES : (h + 1) * LANES]
                    for h in (2 * p, 2 * p + 1)
                ],
                axis=0,
            )
            line_s[:, p * LANES : (p + 1) * LANES] = t.astype(BF16).T
        for far in range(2):
            for ref, which in ((mine_ref, core), (theirs_ref, 1 - core)):
                at = pl.multiple_of((far * 2 + which) * rows_i, rows_i)
                for p in range(pairs):
                    ref[0, far, owner, p * rows_i : (p + 1) * rows_i, :] = line_s[
                        pl.ds(at, rows_i), p * LANES : (p + 1) * LANES
                    ]


def attend(heads, aheads, projected, bias):
    rows, n, inner = projected[0].shape
    inner = inner // 2
    count = len(aheads)
    leap = aheads[1] - aheads[0] if count > 1 else 0
    views = len(bias[0][0])
    flat = [a for slice_of in bias for side in slice_of for a in side]
    n_ja, slab, _ = flat[0].shape[-3:]
    lines = heads * n // n_ja
    att = jax.ShapeDtypeStruct((count, rows, inner, LANES), F32)
    dq = jax.ShapeDtypeStruct((count, rows, inner, LANES), BF16)
    grad = jax.ShapeDtypeStruct((rows, n, inner), BF16)
    gb = jax.ShapeDtypeStruct((count, 2, n_ja, slab, LANES), BF16)
    sums = (rows, n, inner) if count > 1 else (1, 8, LANES)

    def by_slice(a):
        return pl.BlockSpec((1,) + a.shape[1:], lambda i: (i,) + (0,) * (len(a.shape) - 1))

    def sliced(a):
        return pl.BlockSpec((1,) + a.shape[1:], lambda i: (aheads[0] + leap * i, 0, 0, 0))

    return pl.pallas_call(
        lambda *refs: attend_kernel(heads, count, views, *refs),
        grid=(count,),
        in_specs=[pl.BlockSpec(memory_space=pl.ANY)] * 2
        + [sliced(a) for a in projected[2:]]
        + [whole(a) for a in flat],
        out_specs=[by_slice(att), by_slice(dq), whole(grad), whole(grad)] + [by_slice(gb)] * 2,
        out_shape=[att, dq, grad, grad, gb, gb],
        scratch_shapes=[
            pltpu.VMEM((rows, n, 2 * inner), BF16),
            pltpu.VMEM((rows, 2 * inner, n), BF16),
            pltpu.VMEM((n, heads * LANES), F32),
            pltpu.VMEM((n, heads * LANES), F32),
            pltpu.VMEM((rows, n, heads * LANES), F32),
            pltpu.VMEM((rows, n, heads * LANES), BF16),
            pltpu.VMEM((rows, n, heads * LANES), BF16),
            pltpu.VMEM((n_ja, LANES, lines), BF16),
            pltpu.VMEM((LANES, lines), BF16),
            pltpu.VMEM(sums, F32),
            pltpu.VMEM(sums, F32),
            pltpu.SemaphoreType.DMA((2,)),
        ],
        compiler_params=WIDE,
        cost_estimate=pl.CostEstimate(
            flops=count * 2**32, bytes_accessed=2**23, transcendentals=count * 2**20
        ),
    )(*in_hbm(*projected), *flat)


def finish_kernel(
    aheads, gate_ref, cot_ref, w_o_ref, w_q_ref, w_k_ref, w_v_ref, w_g_ref, *refs
):
    count = len(aheads)
    att_refs, dq_refs = refs[:count], refs[count : 2 * count]
    dk_refs, dv_refs = refs[2 * count : 3 * count], refs[3 * count : 4 * count]
    out_ref, att_s, dq_s = refs[4 * count :]
    group, inner, n = gate_ref.shape
    for rows, att_ref, dq_ref in zip(aheads, att_refs, dq_refs):
        for c, ahead in enumerate(rows):
            at = z_lanes(ahead)
            for r in range(group):
                att_s[r, :, at] = att_ref[c, r]
                dq_s[r, :, at] = dq_ref[c, r]
    w_t = jnp.concatenate([w_q_ref[...].T, w_g_ref[...].T], axis=0)
    w_n = jnp.concatenate([w_k_ref[...].T, w_v_ref[...].T], axis=0)
    half = (out_ref.shape[0],) + out_ref.shape[2:]
    for r in range(group):
        gate = gate_ref[r]
        d_gated = mm_nt(w_o_ref[...], cot_ref[:, r].reshape(n, cot_ref.shape[3]))
        att = att_s[r]
        update = mm_tn((gate * att).astype(BF16), w_o_ref[...])
        out_ref[:, 2 * r] = update.astype(BF16).reshape(half)
        d_gate = (d_gated * att * gate * (1.0 - gate)).astype(BF16)
        left_t = jnp.concatenate([dq_s[r], d_gate], axis=0)
        dk = sum(ref[r].astype(F32) for ref in dk_refs).astype(BF16)
        dv = sum(ref[r].astype(F32) for ref in dv_refs).astype(BF16)
        dn = mm_tn(left_t, w_t) + mm(jnp.concatenate([dk, dv], axis=1), w_n)
        out_ref[:, 2 * r + 1] = dn.astype(BF16).reshape(half)


def finish(aheads, gate, both, w_o, weights, att, dq, dk, dv):
    n_blocks, _, block, channels = both.shape
    rows, inner, n = gate.shape
    group = 2
    arrays = (*att, *dq, *dk, *dv)

    def by_row(a):
        return pl.BlockSpec((group,) + a.shape[1:], lambda i: (i, 0, 0))

    def by_slices(a):
        return pl.BlockSpec((a.shape[0], group) + a.shape[2:], lambda i: (0, i, 0, 0))

    return pl.pallas_call(
        lambda *refs: finish_kernel(aheads, *refs),
        grid=(rows // group,),
        in_specs=[
            by_row(gate),
            pl.BlockSpec(
                (n_blocks, group, block, channels), lambda i: (0, rows // group + i, 0, 0)
            ),
            whole(w_o),
        ]
        + [whole(a) for a in weights]
        + [by_slices(a) for a in (*att, *dq)]
        + [by_row(a) for a in (*dk, *dv)],
        out_specs=pl.BlockSpec((n_blocks, 2 * group, block, channels), lambda i: (0, i, 0, 0)),
        out_shape=jax.ShapeDtypeStruct((n_blocks, 2 * rows + 1, block, channels), BF16),
        scratch_shapes=[
            pltpu.VMEM((group, inner, n), F32),
            pltpu.VMEM((group, inner, n), BF16),
        ],
        compiler_params=PARAMS,
        cost_estimate=pl.CostEstimate(flops=2**31, bytes_accessed=2**23, transcendentals=0),
    )(*in_hbm(gate), both, w_o, *weights, *arrays)


def halves_kernel(parts, *refs):
    xh = lax.axis_index("xh")
    keep_ref, send_ref = refs[parts:]
    for far, out in ((0, keep_ref), (1, send_ref)):
        out[...] = sum(ref[xh ^ far].astype(F32) for ref in refs[:parts]).astype(BF16)


def halves(*arrays):
    out = jax.ShapeDtypeStruct(arrays[0].shape[1:], BF16)
    return pl.pallas_call(
        lambda *refs: halves_kernel(len(arrays), *refs),
        out_shape=[out] * 2,
        compiler_params=PARAMS,
        cost_estimate=pl.CostEstimate(flops=2**18, bytes_accessed=2**20, transcendentals=0),
    )(*arrays)


def fill_kernel(done_ref, a_ref, b_ref, out_ref):
    del done_ref
    out_ref[:, 0] = (a_ref[...].astype(F32) + b_ref[...].astype(F32)).astype(BF16)


def fill(done, *parts):
    n_ja, slabs, block, channels = done.shape
    spec = pl.BlockSpec((n_ja, 1, block, channels), lambda i: (0, slabs - 1, 0, 0))
    return pl.pallas_call(
        fill_kernel,
        grid=(1,),
        in_specs=[pl.BlockSpec(memory_space=pl.ANY)] + [whole(a) for a in parts],
        out_specs=spec,
        out_shape=jax.ShapeDtypeStruct(done.shape, BF16),
        input_output_aliases={0: 0},
        compiler_params=PARAMS,
        cost_estimate=pl.CostEstimate(flops=2**18, bytes_accessed=2**20, transcendentals=0),
    )(done, *parts)


def final_kernel(
    pair_ref, both_ref, gb_ref, gain_ref, shift_ref, w_ref, update_ref, out_ref, tile_s
):
    rows, block, channels = pair_ref.shape
    group, slabs = both_ref.shape[:2]
    own = slabs // 2
    step = pl.program_id(0)

    @pl.when(step == 0)
    def _():
        tile = jnp.sum(gb_ref[:, 0].astype(F32), axis=0)
        half = tile.shape[0] // 2
        tile = jnp.concatenate([tile[:half], tile[half:]], axis=1).astype(BF16).astype(F32)
        for e in range(tile_s.shape[0]):
            tile_s[e] = tile[e * rows : (e + 1) * rows]

    tile = tile_s[step]
    keep = line_mask(block, tile.shape[1])
    spread = jnp.concatenate(
        [
            jnp.where(keep, jnp.broadcast_to(tile[i : i + 1], keep.shape), 0.0).astype(BF16)
            for i in range(rows)
        ],
        axis=0,
    )
    back = mm(spread, spread_heads(w_ref, block))
    dn = [both_ref[d, 2 * i + 1] for d in range(group) for i in range(own)]
    dn = jnp.concatenate(dn, axis=0).astype(F32) + back
    for d in range(group):
        for i in range(own):
            update_ref[d * own + i] = both_ref[d, 2 * i]
    centred, rstd = centre(pair_ref[...].reshape(rows * block, channels))
    unit = centred * rstd
    push = dn * gain_ref[...]
    along = jnp.mean(push * unit, axis=-1, keepdims=True)
    level = jnp.mean(push, axis=-1, keepdims=True)
    out_ref[...] = ((push - level - unit * along) * rstd).reshape(out_ref.shape)


def final(pair, both, gain, shift_row, bias_weight):
    n_ja, slabs, block, channels = both.shape
    group = 2
    steps = n_ja // group
    rows = pair.shape[0] // steps
    by_rows = pl.BlockSpec((rows, block, channels), lambda i: (i, 0, 0))
    return pl.pallas_call(
        final_kernel,
        grid=(steps,),
        in_specs=[
            by_rows,
            pl.BlockSpec((group, slabs, block, channels), lambda i: (i, 0, 0, 0)),
            pl.BlockSpec((n_ja, 1, block, channels), lambda i: (0, slabs - 1, 0, 0)),
        ]
        + [whole(a) for a in (gain, shift_row, bias_weight)],
        out_specs=[by_rows, by_rows],
        out_shape=[
            jax.ShapeDtypeStruct(pair.shape, BF16),
            jax.ShapeDtypeStruct(pair.shape, F32),
        ],
        scratch_shapes=[pltpu.VMEM((steps, rows, bias_weight.shape[0] * block), F32)],
        compiler_params=PARAMS,
        cost_estimate=pl.CostEstimate(
            flops=2**27, bytes_accessed=2**21, transcendentals=2**12
        ),
    )(pair, both, both, gain, shift_row, bias_weight)


def shards(
    pair,
    cotangent,
    norm_gain,
    norm_shift,
    query_weight,
    key_weight,
    value_weight,
    gate_weight,
    bias_weight,
    out_weight,
):
    rows_i, rows_j, channels = pair.shape
    heads = bias_weight.shape[1]
    n_ja = lax.axis_size(JA)
    own_i = rows_i // n_ja
    gain = norm_gain.reshape(1, channels)
    shift_row = norm_shift.reshape(1, channels)
    bias_rows = bias_weight.T
    weights = (query_weight, key_weight, value_weight, gate_weight)
    tie = lax.optimization_barrier

    n_xh = lax.axis_size("xh")
    tile = prep(pair, gain, shift_row, bias_rows, n_xh * n_ja)
    both = pack(pair, cotangent, n_ja)
    near = lax.all_to_all(tile, ("xh",) + JA, 0, 0, tiled=True)
    near, both = tie((near, both))
    near = near.reshape((n_xh, n_ja) + near.shape[1:])
    both = lax.all_to_all(both, JA, 0, 0, tiled=True)

    def joined(mine, theirs):
        return (mine.astype(F32) + theirs.astype(F32)).astype(BF16)

    slices = [shift(near, "z", 3), shift(near, "z", 2), shift(near, "z", 1)]
    swaps = [swap(a) for a in slices]
    near_swap = swap(near)
    projected = project(both, gain, shift_row, out_weight, weights)
    projected, slices, swaps = tie((projected, slices, swaps))
    *projected, gate = projected

    groups = ((1, 2, 3), (0,))
    out1 = attend(heads, groups[0], projected, [([a], [b]) for a, b in zip(slices, swaps)])
    theirs1 = swap(out1[5])
    theirs1, near = tie((theirs1, near))
    part = joined(out1[4], theirs1)
    part, near = tie((part, near))
    parts = [shift(part[e], "z", e + 1) for e in range(3)]
    out0 = attend(heads, groups[1], projected, [([near], [near_swap])])
    att, dq, dk, dv = zip(out1[:4], out0[:4])
    done = finish(groups, gate, both, out_weight, weights, att, dq, dk, dv)
    theirs0 = swap(out0[5])
    done, parts, theirs0 = tie((done, parts, theirs0))
    keep, send = halves(out0[4][0], theirs0[0], *parts)
    send = lax.ppermute(send, "xh", [(0, 1), (1, 0)])
    done = fill(done, keep, send)
    done = lax.all_to_all(done, JA, 0, 0, tiled=True)
    update, pair_grad = final(pair, done, gain, shift_row, bias_rows)
    return (update, pair_grad)


def solution(mesh):
    fine = Mesh(mesh.devices.reshape(4, 2, 2, 4, 2), IA + JA)
    spec = P(IA, JA, None)
    in_specs = (spec, spec) + (P(),) * 8
    return jax.shard_map(
        shards, mesh=fine, in_specs=in_specs, out_specs=(spec, spec), check_vma=False
    )
```

```python
import math

import jax
import jax.numpy as jnp
from jax import lax
from jax.experimental import pallas as pl
from jax.experimental.pallas import tpu as pltpu
from jax.sharding import Mesh, PartitionSpec as P

EPSILON = 1e-05
LOG2E = math.log2(math.e)
IA = ("z", "xh", "core")
JA = ("y", "xl")
F32 = jnp.float32
BF16 = jnp.bfloat16
LANES = 128
PARAMS = pltpu.CompilerParams(vmem_limit_bytes=24 * 1024 * 1024)
WIDE = pltpu.CompilerParams(vmem_limit_bytes=36 * 1024 * 1024)
FIRST = pltpu.CompilerParams(vmem_limit_bytes=60 * 1024 * 1024)


def mm(a, b):
    return lax.dot_general(a, b, (((1,), (0,)), ((), ())), preferred_element_type=F32)


def mm_nt(a, b):
    return lax.dot_general(a, b, (((1,), (1,)), ((), ())), preferred_element_type=F32)


def mm_tn(a, b):
    return lax.dot_general(a, b, (((0,), (0,)), ((), ())), preferred_element_type=F32)


def centre(rows):
    channels = rows.shape[1]
    share = jnp.full((channels, channels), 1.0 / channels, BF16)
    centred = rows.astype(F32) - mm(rows, share)
    variance = jnp.mean(centred * centred, axis=-1, keepdims=True)
    return centred, lax.rsqrt(variance + EPSILON)


def normalize(rows, norm_gain, norm_shift):
    centred, rstd = centre(rows)
    return (centred * rstd * norm_gain + norm_shift).astype(BF16)


def swap(a):
    return lax.ppermute(a, "core", [(0, 1), (1, 0)])


def shift(a, axis, by):
    size = lax.axis_size(axis)
    return lax.ppermute(a, axis, [(s, (s + by) % size) for s in range(size)])


def in_hbm(*arrays):
    return [pltpu.with_memory_space_constraint(a, pltpu.HBM) for a in arrays]


def whole(a):
    return pl.BlockSpec(a.shape, lambda *_: (0,) * len(a.shape))


def line_mask(block, width):
    lane = lax.broadcasted_iota(jnp.int32, (block, width), 1)
    return lax.broadcasted_iota(jnp.int32, (block, width), 0) == lane % block


def spread_heads(w_ref, block):
    w = w_ref[...].astype(F32)
    shape = (block, w.shape[1])
    rows = [jnp.broadcast_to(w[h : h + 1], shape) for h in range(w.shape[0])]
    return jnp.concatenate(rows, axis=0).astype(BF16)


def prep_kernel(pair_ref, gain_ref, shift_ref, w_ref, tile_ref):
    rows, block, channels = pair_ref.shape
    x = pair_ref[...].reshape(rows * block, channels)
    normed = normalize(x, gain_ref[...], shift_ref[...])
    every = mm_nt(normed, spread_heads(w_ref, block))
    width = every.shape[1]
    keep = line_mask(block, width)
    lines = []
    for i in range(rows):
        part = jnp.where(keep, every[i * block : (i + 1) * block], 0.0)
        lines.append(jnp.sum(part, axis=0, keepdims=True))
    tile = jnp.concatenate(lines, axis=0).astype(BF16)
    tile = jnp.concatenate([tile[:, :LANES], tile[:, LANES:]], axis=0)
    for d in range(tile_ref.shape[0]):
        tile_ref[d] = tile


def prep(pair, gain, shift_row, bias_weight, copies):
    rows, block, channels = pair.shape
    return pl.pallas_call(
        prep_kernel,
        out_shape=jax.ShapeDtypeStruct((copies, block, channels), BF16),
        compiler_params=FIRST,
        cost_estimate=pl.CostEstimate(
            flops=2**27, bytes_accessed=2**20, transcendentals=2**12
        ),
    )(pair, gain, shift_row, bias_weight)


def pack_kernel(pair_ref, cot_ref, out_ref):
    group, slabs, block, channels = out_ref.shape
    own = slabs // 2
    out_ref[:, :own] = pair_ref[...].reshape(group, own, block, channels)
    out_ref[:, own:] = cot_ref[...].reshape(group, own, block, channels)


def pack(pair, cot, n_ja):
    rows, block, channels = pair.shape
    own = rows // n_ja
    group = n_ja // 2
    part = pl.BlockSpec((group * own, block, channels), lambda d: (d, 0, 0))
    return pl.pallas_call(
        pack_kernel,
        grid=(n_ja // group,),
        in_specs=[part, part],
        out_specs=pl.BlockSpec((group, 2 * own, block, channels), lambda d: (d, 0, 0, 0)),
        out_shape=jax.ShapeDtypeStruct((n_ja, 2 * own, block, channels), BF16),
        compiler_params=FIRST,
        cost_estimate=pl.CostEstimate(flops=2**10, bytes_accessed=2**21, transcendentals=0),
    )(pair, cot)


def project_kernel(
    pair_ref,
    cot_ref,
    gain_ref,
    shift_ref,
    w_o_ref,
    w_q_ref,
    w_k_ref,
    w_v_ref,
    w_g_ref,
    kv_n_ref,
    kv_t_ref,
    q_n_ref,
    q_t_ref,
    d_att_ref,
    gate_ref,
):
    n_blocks, group, block, channels = pair_ref.shape
    n = n_blocks * block
    inner = w_q_ref.shape[1]
    weights = [ref[...] for ref in (w_q_ref, w_k_ref, w_v_ref, w_g_ref)]
    w_n = jnp.concatenate(weights[:3], axis=1)
    w_t = jnp.concatenate([w.T for w in weights], axis=0)
    size = lax.axis_size("z")
    z = lax.axis_index("z")
    for r in range(group):
        normed = normalize(pair_ref[:, r].reshape(n, channels), gain_ref[...], shift_ref[...])
        proj = mm(normed, w_n).astype(BF16)
        kv_n_ref[r] = proj[:, inner:]
        proj_t = mm_nt(w_t, normed)
        kv_t_ref[r] = proj_t[inner : 3 * inner].astype(BF16)
        gate = jax.nn.sigmoid(proj_t[3 * inner :])
        gate_ref[r] = gate
        d_att = mm_nt(w_o_ref[...], cot_ref[:, r].reshape(n, channels)) * gate
        for owner in range(n // LANES):
            at = slice(owner * LANES, (owner + 1) * LANES)
            ahead = lax.rem(owner + size - z, size)
            q_n_ref[ahead, r] = proj[at, :inner]
            q_t_ref[ahead, r] = proj_t[:inner, at].astype(BF16)
            d_att_ref[ahead, r] = d_att[:, at].astype(BF16)


def project(both, gain, shift_row, w_o, weights):
    n_blocks, slabs, block, channels = both.shape
    rows = slabs // 2
    group = 2
    n = n_blocks * block
    inner = w_o.shape[0]
    kv_n = pltpu.HBM((rows, n, 2 * inner), BF16)
    kv_t = pltpu.HBM((rows, 2 * inner, n), BF16)
    gate = pltpu.HBM((rows, inner, n), F32)
    q_n = pltpu.HBM((n // LANES, rows, LANES, inner), BF16)
    q_t = pltpu.HBM((n // LANES, rows, inner, LANES), BF16)
    d_att = pltpu.HBM((n // LANES, rows, inner, LANES), BF16)

    def by_row(a):
        return pl.BlockSpec((group,) + a.shape[1:], lambda i: (i, 0, 0))

    def sliced(a):
        return pl.BlockSpec((a.shape[0], group) + a.shape[2:], lambda i: (0, i, 0, 0))

    return pl.pallas_call(
        project_kernel,
        grid=(rows // group,),
        in_specs=[
            pl.BlockSpec((n_blocks, group, block, channels), lambda i: (0, i, 0, 0)),
            pl.BlockSpec(
                (n_blocks, group, block, channels), lambda i: (0, rows // group + i, 0, 0)
            ),
        ]
        + [whole(a) for a in (gain, shift_row, w_o, *weights)],
        out_specs=[by_row(kv_n), by_row(kv_t)]
        + [sliced(a) for a in (q_n, q_t, d_att)]
        + [by_row(gate)],
        out_shape=[kv_n, kv_t, q_n, q_t, d_att, gate],
        compiler_params=PARAMS,
        cost_estimate=pl.CostEstimate(
            flops=2**31, bytes_accessed=8 * 2**20, transcendentals=2**18
        ),
    )(both, both, gain, shift_row, w_o, *weights)


def z_lanes(ahead):
    at = lax.rem(lax.axis_index("z") + ahead, lax.axis_size("z"))
    return pl.ds(pl.multiple_of(at * LANES, LANES), LANES)


def attend_kernel(heads, count, views, kv_n_hbm, kv_t_hbm, q_n_ref, q_t_ref, d_att_ref, *refs):
    bias_refs = refs[: count * 2 * views]
    refs = refs[count * 2 * views :]
    att_ref, dq_ref, dk_ref, dv_ref, mine_ref, theirs_ref = refs[:6]
    n_ref, t_ref, bias_s, gb_s, s_s, p_s, ds_s, tile_s, line_s, dk_s, dv_s, sems = refs[6:]
    at_slice = pl.program_id(0)
    row_count, n, wide_kv = n_ref.shape
    inner = wide_kv // 2
    head_dim = inner // heads
    scale = 1.0 / math.sqrt(head_dim)
    n_ja = tile_s.shape[0]
    block = n // n_ja
    rows_i = LANES // 4
    pairs = heads // 2
    wide = 2 * LANES
    core = lax.axis_index("core")
    copies = [
        pltpu.make_async_copy(src, dst, sems.at[e])
        for e, (src, dst) in enumerate(((kv_n_hbm, n_ref), (kv_t_hbm, t_ref)))
    ]

    @pl.when(at_slice == 0)
    def _():
        for copy in copies:
            copy.start()
        if count > 1:
            dk_s[...] = jnp.zeros_like(dk_s)
            dv_s[...] = jnp.zeros_like(dv_s)

    def sort_tiles(c):
        for which in range(2):
            base = (c * 2 + which) * views
            parts = []
            for ref in bias_refs[base : base + views]:
                parts += [ref] if len(ref.shape) == 3 else [ref.at[e] for e in range(2)]
            for far, ref in enumerate(parts):
                at = far * 2 + (core ^ which)
                at = pl.ds(pl.multiple_of(at * rows_i, rows_i), rows_i)
                for owner in range(n_ja):
                    for p in range(pairs):
                        tile_s[owner, at, p * LANES : (p + 1) * LANES] = ref[
                            owner, p * rows_i : (p + 1) * rows_i, :
                        ]

    for c in range(count):
        pl.when(at_slice == c)(lambda c=c: sort_tiles(c))
    for owner in range(n_ja):
        for p in range(pairs):
            t = tile_s[owner, :, p * LANES : (p + 1) * LANES].T.astype(F32) * LOG2E
            for e in range(2):
                h = p * 2 + e
                bias_s[owner * block : (owner + 1) * block, h * LANES : (h + 1) * LANES] = t[
                    e * block : (e + 1) * block
                ]

    @pl.when(at_slice == 0)
    def _():
        for copy in copies:
            copy.wait()

    nil = jnp.zeros((), BF16)
    row_head = lax.broadcasted_iota(jnp.int32, (inner, LANES), 0) // head_dim
    lane_head = lax.broadcasted_iota(jnp.int32, (LANES, inner), 1) // head_dim
    step = 16
    held = {}

    def cols_of(p):
        return slice(p * wide, (p + 1) * wide)

    def scores(r, p):
        q_blk = jnp.concatenate(
            [jnp.where(row_head == h, q_t_ref[0, r], nil) for h in (2 * p, 2 * p + 1)], axis=1
        )
        t = mm(n_ref[r, :, :inner], q_blk) * (scale * LOG2E) + bias_s[:, cols_of(p)]
        s_s[r, :, cols_of(p)] = t
        top = t[:8]
        for e in range(8, n, 8):
            top = jnp.maximum(top, t[e : e + 8])
        held["top", r, p] = jnp.max(top, axis=0, keepdims=True)

    def weights(r, p):
        total = jnp.zeros((8, wide), F32)
        for k in range(0, n, step):
            e = jnp.exp2(s_s[r, k : k + step, cols_of(p)] - held["top", r, p])
            s_s[r, k : k + step, cols_of(p)] = e
            p_s[r, k : k + step, cols_of(p)] = e.astype(BF16)
            total = total + (e[:8] + e[8:])
        held["inv", r, p] = 1.0 / jnp.sum(total, axis=0, keepdims=True)

    def attended(r, p):
        first = 2 * p * head_dim
        rows = slice(first, first + 2 * head_dim)
        inv = held["inv", r, p]
        att = mm(t_ref[r, inner + first : inner + first + 2 * head_dim, :], p_s[r, :, cols_of(p)])
        att = att * inv
        d_att = d_att_ref[0, r, rows, :].astype(F32)
        a_two = jnp.concatenate([d_att, d_att], axis=1) * inv
        lane = lax.broadcasted_iota(jnp.int32, a_two.shape, 1) // LANES
        sub = lax.broadcasted_iota(jnp.int32, a_two.shape, 0) // head_dim
        a_two = jnp.where(lane == sub, a_two, 0.0).astype(BF16)
        held["diag", r, p] = jnp.sum(a_two.astype(F32) * att, axis=0, keepdims=True)
        for e in range(2):
            h = 2 * p + e
            att_ref[0, r, h * head_dim : (h + 1) * head_dim, :] = att[
                e * head_dim : (e + 1) * head_dim, e * LANES : (e + 1) * LANES
            ]
        lead = [jnp.zeros((first, wide), BF16)] if p else []
        tail = [jnp.zeros((inner - first - 2 * head_dim, wide), BF16)] if p + 1 < pairs else []
        held["a", r, p] = jnp.concatenate(lead + [a_two] + tail, axis=0)

    def d_scores(r, p):
        dp = mm(n_ref[r, :, inner:], held["a", r, p])
        for k in range(0, n, step):
            ds = s_s[r, k : k + step, cols_of(p)] * (dp[k : k + step] - held["diag", r, p])
            if r == 0:
                gb_s[k : k + step, cols_of(p)] = ds
            else:
                gb_s[k : k + step, cols_of(p)] += ds
            ds_s[r, k : k + step, cols_of(p)] = ds.astype(BF16)

    def d_query(r, p):
        first = 2 * p * head_dim
        dq = mm(t_ref[r, first : first + 2 * head_dim, :], ds_s[r, :, cols_of(p)]) * scale
        for e in range(2):
            h = 2 * p + e
            dq_ref[0, r, h * head_dim : (h + 1) * head_dim, :] = dq[
                e * head_dim : (e + 1) * head_dim, e * LANES : (e + 1) * LANES
            ].astype(BF16)

    def gather(r, p, name, part, sum_s, out_ref, factor):
        if p:
            part = part + held.pop((name, r))
        if p + 1 < pairs:
            held[name, r] = part
            return
        if count > 1:
            part = part + sum_s[r]
            sum_s[r] = part
        out_ref[r] = (part * factor).astype(BF16)

    def d_key(r, p):
        q_row = jnp.concatenate(
            [jnp.where(lane_head == h, q_n_ref[0, r], nil) for h in (2 * p, 2 * p + 1)], axis=0
        )
        gather(r, p, "dk", mm(ds_s[r, :, cols_of(p)], q_row), dk_s, dk_ref, scale)

    def d_value(r, p):
        part = mm(p_s[r, :, cols_of(p)], held["a", r, p].T)
        gather(r, p, "dv", part, dv_s, dv_ref, 1.0)

    order = [
        (scores, 0),
        (scores, 1),
        (weights, 0),
        (attended, 0),
        (weights, 1),
        (d_scores, 0),
        (attended, 1),
        (d_value, 0),
        (d_scores, 1),
        (d_query, 0),
        (d_key, 0),
        (d_value, 1),
        (d_query, 1),
        (d_key, 1),
    ]
    lag = 5
    for t in range(len(order) + lag * (row_count - 1)):
        for r in range(row_count):
            if 0 <= t - lag * r < len(order):
                phase, p = order[t - lag * r]
                phase(r, p)

    for owner in range(n_ja):
        for p in range(pairs):
            t = jnp.concatenate(
                [
                    gb_s[owner * block : (owner + 1) * block, h * LANES : (h + 1) * LANES]
                    for h in (2 * p, 2 * p + 1)
                ],
                axis=0,
            )
            line_s[:, p * LANES : (p + 1) * LANES] = t.astype(BF16).T
        for far in range(2):
            for ref, which in ((mine_ref, core), (theirs_ref, 1 - core)):
                at = pl.multiple_of((far * 2 + which) * rows_i, rows_i)
                for p in range(pairs):
                    ref[0, far, owner, p * rows_i : (p + 1) * rows_i, :] = line_s[
                        pl.ds(at, rows_i), p * LANES : (p + 1) * LANES
                    ]


def attend(heads, aheads, projected, bias):
    rows, n, inner = projected[0].shape
    inner = inner // 2
    count = len(aheads)
    leap = aheads[1] - aheads[0] if count > 1 else 0
    views = len(bias[0][0])
    flat = [a for slice_of in bias for side in slice_of for a in side]
    n_ja, slab, _ = flat[0].shape[-3:]
    lines = heads * n // n_ja
    att = jax.ShapeDtypeStruct((count, rows, inner, LANES), F32)
    dq = jax.ShapeDtypeStruct((count, rows, inner, LANES), BF16)
    grad = jax.ShapeDtypeStruct((rows, n, inner), BF16)
    gb = jax.ShapeDtypeStruct((count, 2, n_ja, slab, LANES), BF16)
    sums = (rows, n, inner) if count > 1 else (1, 8, LANES)

    def by_slice(a):
        return pl.BlockSpec((1,) + a.shape[1:], lambda i: (i,) + (0,) * (len(a.shape) - 1))

    def sliced(a):
        return pl.BlockSpec((1,) + a.shape[1:], lambda i: (aheads[0] + leap * i, 0, 0, 0))

    return pl.pallas_call(
        lambda *refs: attend_kernel(heads, count, views, *refs),
        grid=(count,),
        in_specs=[pl.BlockSpec(memory_space=pl.ANY)] * 2
        + [sliced(a) for a in projected[2:]]
        + [whole(a) for a in flat],
        out_specs=[by_slice(att), by_slice(dq), whole(grad), whole(grad)] + [by_slice(gb)] * 2,
        out_shape=[att, dq, grad, grad, gb, gb],
        scratch_shapes=[
            pltpu.VMEM((rows, n, 2 * inner), BF16),
            pltpu.VMEM((rows, 2 * inner, n), BF16),
            pltpu.VMEM((n, heads * LANES), F32),
            pltpu.VMEM((n, heads * LANES), F32),
            pltpu.VMEM((rows, n, heads * LANES), F32),
            pltpu.VMEM((rows, n, heads * LANES), BF16),
            pltpu.VMEM((rows, n, heads * LANES), BF16),
            pltpu.VMEM((n_ja, LANES, lines), BF16),
            pltpu.VMEM((LANES, lines), BF16),
            pltpu.VMEM(sums, F32),
            pltpu.VMEM(sums, F32),
            pltpu.SemaphoreType.DMA((2,)),
        ],
        compiler_params=WIDE,
        cost_estimate=pl.CostEstimate(
            flops=count * 2**32, bytes_accessed=2**23, transcendentals=count * 2**20
        ),
    )(*in_hbm(*projected), *flat)


def finish_kernel(
    aheads, gate_ref, cot_ref, w_o_ref, w_q_ref, w_k_ref, w_v_ref, w_g_ref, *refs
):
    count = len(aheads)
    att_refs, dq_refs = refs[:count], refs[count : 2 * count]
    dk_refs, dv_refs = refs[2 * count : 3 * count], refs[3 * count : 4 * count]
    out_ref, att_s, dq_s = refs[4 * count :]
    group, inner, n = gate_ref.shape
    for rows, att_ref, dq_ref in zip(aheads, att_refs, dq_refs):
        for c, ahead in enumerate(rows):
            at = z_lanes(ahead)
            for r in range(group):
                att_s[r, :, at] = att_ref[c, r]
                dq_s[r, :, at] = dq_ref[c, r]
    w_t = jnp.concatenate([w_q_ref[...].T, w_g_ref[...].T], axis=0)
    w_n = jnp.concatenate([w_k_ref[...].T, w_v_ref[...].T], axis=0)
    half = (out_ref.shape[0],) + out_ref.shape[2:]
    for r in range(group):
        gate = gate_ref[r]
        d_gated = mm_nt(w_o_ref[...], cot_ref[:, r].reshape(n, cot_ref.shape[3]))
        att = att_s[r]
        update = mm_tn((gate * att).astype(BF16), w_o_ref[...])
        out_ref[:, 2 * r] = update.astype(BF16).reshape(half)
        d_gate = (d_gated * att * gate * (1.0 - gate)).astype(BF16)
        left_t = jnp.concatenate([dq_s[r], d_gate], axis=0)
        dk = sum(ref[r].astype(F32) for ref in dk_refs).astype(BF16)
        dv = sum(ref[r].astype(F32) for ref in dv_refs).astype(BF16)
        dn = mm_tn(left_t, w_t) + mm(jnp.concatenate([dk, dv], axis=1), w_n)
        out_ref[:, 2 * r + 1] = dn.astype(BF16).reshape(half)


def finish(aheads, gate, both, w_o, weights, att, dq, dk, dv):
    n_blocks, _, block, channels = both.shape
    rows, inner, n = gate.shape
    group = 2
    arrays = (*att, *dq, *dk, *dv)

    def by_row(a):
        return pl.BlockSpec((group,) + a.shape[1:], lambda i: (i, 0, 0))

    def by_slices(a):
        return pl.BlockSpec((a.shape[0], group) + a.shape[2:], lambda i: (0, i, 0, 0))

    return pl.pallas_call(
        lambda *refs: finish_kernel(aheads, *refs),
        grid=(rows // group,),
        in_specs=[
            by_row(gate),
            pl.BlockSpec(
                (n_blocks, group, block, channels), lambda i: (0, rows // group + i, 0, 0)
            ),
            whole(w_o),
        ]
        + [whole(a) for a in weights]
        + [by_slices(a) for a in (*att, *dq)]
        + [by_row(a) for a in (*dk, *dv)],
        out_specs=pl.BlockSpec((n_blocks, 2 * group, block, channels), lambda i: (0, i, 0, 0)),
        out_shape=jax.ShapeDtypeStruct((n_blocks, 2 * rows + 1, block, channels), BF16),
        scratch_shapes=[
            pltpu.VMEM((group, inner, n), F32),
            pltpu.VMEM((group, inner, n), BF16),
        ],
        compiler_params=PARAMS,
        cost_estimate=pl.CostEstimate(flops=2**31, bytes_accessed=2**23, transcendentals=0),
    )(*in_hbm(gate), both, w_o, *weights, *arrays)


def halves_kernel(parts, *refs):
    xh = lax.axis_index("xh")
    keep_ref, send_ref = refs[parts:]
    for far, out in ((0, keep_ref), (1, send_ref)):
        out[...] = sum(ref[xh ^ far].astype(F32) for ref in refs[:parts]).astype(BF16)


def halves(*arrays):
    out = jax.ShapeDtypeStruct(arrays[0].shape[1:], BF16)
    return pl.pallas_call(
        lambda *refs: halves_kernel(len(arrays), *refs),
        out_shape=[out] * 2,
        compiler_params=PARAMS,
        cost_estimate=pl.CostEstimate(flops=2**18, bytes_accessed=2**20, transcendentals=0),
    )(*arrays)


def fill_kernel(done_ref, a_ref, b_ref, out_ref):
    del done_ref
    out_ref[:, 0] = (a_ref[...].astype(F32) + b_ref[...].astype(F32)).astype(BF16)


def fill(done, *parts):
    n_ja, slabs, block, channels = done.shape
    spec = pl.BlockSpec((n_ja, 1, block, channels), lambda i: (0, slabs - 1, 0, 0))
    return pl.pallas_call(
        fill_kernel,
        grid=(1,),
        in_specs=[pl.BlockSpec(memory_space=pl.ANY)] + [whole(a) for a in parts],
        out_specs=spec,
        out_shape=jax.ShapeDtypeStruct(done.shape, BF16),
        input_output_aliases={0: 0},
        compiler_params=PARAMS,
        cost_estimate=pl.CostEstimate(flops=2**18, bytes_accessed=2**20, transcendentals=0),
    )(done, *parts)


def final_kernel(
    pair_ref, both_ref, gb_ref, gain_ref, shift_ref, w_ref, update_ref, out_ref, tile_s
):
    rows, block, channels = pair_ref.shape
    group, slabs = both_ref.shape[:2]
    own = slabs // 2
    step = pl.program_id(0)

    @pl.when(step == 0)
    def _():
        tile = jnp.sum(gb_ref[:, 0].astype(F32), axis=0)
        half = tile.shape[0] // 2
        tile = jnp.concatenate([tile[:half], tile[half:]], axis=1).astype(BF16).astype(F32)
        for e in range(tile_s.shape[0]):
            tile_s[e] = tile[e * rows : (e + 1) * rows]

    tile = tile_s[step]
    keep = line_mask(block, tile.shape[1])
    spread = jnp.concatenate(
        [
            jnp.where(keep, jnp.broadcast_to(tile[i : i + 1], keep.shape), 0.0).astype(BF16)
            for i in range(rows)
        ],
        axis=0,
    )
    back = mm(spread, spread_heads(w_ref, block))
    dn = [both_ref[d, 2 * i + 1] for d in range(group) for i in range(own)]
    dn = jnp.concatenate(dn, axis=0).astype(F32) + back
    for d in range(group):
        for i in range(own):
            update_ref[d * own + i] = both_ref[d, 2 * i]
    centred, rstd = centre(pair_ref[...].reshape(rows * block, channels))
    unit = centred * rstd
    push = dn * gain_ref[...]
    along = jnp.mean(push * unit, axis=-1, keepdims=True)
    level = jnp.mean(push, axis=-1, keepdims=True)
    out_ref[...] = ((push - level - unit * along) * rstd).reshape(out_ref.shape)


def final(pair, both, gain, shift_row, bias_weight):
    n_ja, slabs, block, channels = both.shape
    group = 2
    steps = n_ja // group
    rows = pair.shape[0] // steps
    by_rows = pl.BlockSpec((rows, block, channels), lambda i: (i, 0, 0))
    return pl.pallas_call(
        final_kernel,
        grid=(steps,),
        in_specs=[
            by_rows,
            pl.BlockSpec((group, slabs, block, channels), lambda i: (i, 0, 0, 0)),
            pl.BlockSpec((n_ja, 1, block, channels), lambda i: (0, slabs - 1, 0, 0)),
        ]
        + [whole(a) for a in (gain, shift_row, bias_weight)],
        out_specs=[by_rows, by_rows],
        out_shape=[
            jax.ShapeDtypeStruct(pair.shape, BF16),
            jax.ShapeDtypeStruct(pair.shape, F32),
        ],
        scratch_shapes=[pltpu.VMEM((steps, rows, bias_weight.shape[0] * block), F32)],
        compiler_params=PARAMS,
        cost_estimate=pl.CostEstimate(
            flops=2**27, bytes_accessed=2**21, transcendentals=2**12
        ),
    )(pair, both, both, gain, shift_row, bias_weight)


def shards(
    pair,
    cotangent,
    norm_gain,
    norm_shift,
    query_weight,
    key_weight,
    value_weight,
    gate_weight,
    bias_weight,
    out_weight,
):
    rows_i, rows_j, channels = pair.shape
    heads = bias_weight.shape[1]
    n_ja = lax.axis_size(JA)
    own_i = rows_i // n_ja
    gain = norm_gain.reshape(1, channels)
    shift_row = norm_shift.reshape(1, channels)
    bias_rows = bias_weight.T
    weights = (query_weight, key_weight, value_weight, gate_weight)
    tie = lax.optimization_barrier

    n_xh = lax.axis_size("xh")
    tile = prep(pair, gain, shift_row, bias_rows, n_xh * n_ja)
    both = pack(pair, cotangent, n_ja)
    near = lax.all_to_all(tile, ("xh",) + JA, 0, 0, tiled=True)
    near, both = tie((near, both))
    near = near.reshape((n_xh, n_ja) + near.shape[1:])
    both = lax.all_to_all(both, JA, 0, 0, tiled=True)

    def joined(mine, theirs):
        return (mine.astype(F32) + theirs.astype(F32)).astype(BF16)

    slices = [shift(near, "z", 3), shift(near, "z", 2), shift(near, "z", 1)]
    swaps = [swap(a) for a in slices]
    near_swap = swap(near)
    projected = project(both, gain, shift_row, out_weight, weights)
    projected, slices, swaps = tie((projected, slices, swaps))
    *projected, gate = projected

    groups = ((1, 2, 3), (0,))
    out1 = attend(heads, groups[0], projected, [([a], [b]) for a, b in zip(slices, swaps)])
    theirs1 = swap(out1[5])
    theirs1, near = tie((theirs1, near))
    part = joined(out1[4], theirs1)
    part, near = tie((part, near))
    parts = [shift(part[e], "z", e + 1) for e in range(3)]
    out0 = attend(heads, groups[1], projected, [([near], [near_swap])])
    att, dq, dk, dv = zip(out1[:4], out0[:4])
    done = finish(groups, gate, both, out_weight, weights, att, dq, dk, dv)
    theirs0 = swap(out0[5])
    done, parts, theirs0 = tie((done, parts, theirs0))
    keep, send = halves(out0[4][0], theirs0[0], *parts)
    send = lax.ppermute(send, "xh", [(0, 1), (1, 0)])
    done = fill(done, keep, send)
    done = lax.all_to_all(done, JA, 0, 0, tiled=True)
    update, pair_grad = final(pair, done, gain, shift_row, bias_rows)
    return (update, pair_grad)


def solution(mesh):
    fine = Mesh(mesh.devices.reshape(4, 2, 2, 4, 2), IA + JA)
    spec = P(IA, JA, None)
    in_specs = (spec, spec) + (P(),) * 8
    return jax.shard_map(
        shards, mesh=fine, in_specs=in_specs, out_specs=(spec, spec), check_vma=False
    )
```

```python
import math

import jax
import jax.numpy as jnp
from jax import lax
from jax.experimental import pallas as pl
from jax.experimental.pallas import tpu as pltpu
from jax.sharding import Mesh, PartitionSpec as P

EPSILON = 1e-05
LOG2E = math.log2(math.e)
IA = ("z", "xh", "core")
JA = ("y", "xl")
F32 = jnp.float32
BF16 = jnp.bfloat16
LANES = 128
PARAMS = pltpu.CompilerParams(vmem_limit_bytes=24 * 1024 * 1024)
WIDE = pltpu.CompilerParams(vmem_limit_bytes=36 * 1024 * 1024)
FIRST = pltpu.CompilerParams(vmem_limit_bytes=60 * 1024 * 1024)


def mm(a, b):
    return lax.dot_general(a, b, (((1,), (0,)), ((), ())), preferred_element_type=F32)


def mm_nt(a, b):
    return lax.dot_general(a, b, (((1,), (1,)), ((), ())), preferred_element_type=F32)


def mm_tn(a, b):
    return lax.dot_general(a, b, (((0,), (0,)), ((), ())), preferred_element_type=F32)


def centre(rows):
    channels = rows.shape[1]
    share = jnp.full((channels, channels), 1.0 / channels, BF16)
    centred = rows.astype(F32) - mm(rows, share)
    variance = jnp.mean(centred * centred, axis=-1, keepdims=True)
    return centred, lax.rsqrt(variance + EPSILON)


def normalize(rows, norm_gain, norm_shift):
    centred, rstd = centre(rows)
    return (centred * rstd * norm_gain + norm_shift).astype(BF16)


def swap(a):
    return lax.ppermute(a, "core", [(0, 1), (1, 0)])


def shift(a, axis, by):
    size = lax.axis_size(axis)
    return lax.ppermute(a, axis, [(s, (s + by) % size) for s in range(size)])


def in_hbm(*arrays):
    return [pltpu.with_memory_space_constraint(a, pltpu.HBM) for a in arrays]


def whole(a):
    return pl.BlockSpec(a.shape, lambda *_: (0,) * len(a.shape))


def line_mask(block, width):
    lane = lax.broadcasted_iota(jnp.int32, (block, width), 1)
    return lax.broadcasted_iota(jnp.int32, (block, width), 0) == lane % block


def spread_heads(w_ref, block):
    w = w_ref[...].astype(F32)
    shape = (block, w.shape[1])
    rows = [jnp.broadcast_to(w[h : h + 1], shape) for h in range(w.shape[0])]
    return jnp.concatenate(rows, axis=0).astype(BF16)


def prep_kernel(pair_ref, gain_ref, shift_ref, w_ref, tile_ref):
    rows, block, channels = pair_ref.shape
    x = pair_ref[...].reshape(rows * block, channels)
    normed = normalize(x, gain_ref[...], shift_ref[...])
    every = mm_nt(normed, spread_heads(w_ref, block))
    width = every.shape[1]
    keep = line_mask(block, width)
    lines = []
    for i in range(rows):
        part = jnp.where(keep, every[i * block : (i + 1) * block], 0.0)
        lines.append(jnp.sum(part, axis=0, keepdims=True))
    tile = jnp.concatenate(lines, axis=0).astype(BF16)
    tile = jnp.concatenate([tile[:, :LANES], tile[:, LANES:]], axis=0)
    for d in range(tile_ref.shape[0]):
        tile_ref[d] = tile


def prep(pair, gain, shift_row, bias_weight, copies):
    rows, block, channels = pair.shape
    return pl.pallas_call(
        prep_kernel,
        out_shape=jax.ShapeDtypeStruct((copies, block, channels), BF16),
        compiler_params=FIRST,
        cost_estimate=pl.CostEstimate(
            flops=2**27, bytes_accessed=2**20, transcendentals=2**12
        ),
    )(pair, gain, shift_row, bias_weight)


def pack_kernel(pair_ref, cot_ref, out_ref):
    group, slabs, block, channels = out_ref.shape
    own = slabs // 2
    out_ref[:, :own] = pair_ref[...].reshape(group, own, block, channels)
    out_ref[:, own:] = cot_ref[...].reshape(group, own, block, channels)


def pack(pair, cot, n_ja):
    rows, block, channels = pair.shape
    own = rows // n_ja
    group = n_ja // 2
    part = pl.BlockSpec((group * own, block, channels), lambda d: (d, 0, 0))
    return pl.pallas_call(
        pack_kernel,
        grid=(n_ja // group,),
        in_specs=[part, part],
        out_specs=pl.BlockSpec((group, 2 * own, block, channels), lambda d: (d, 0, 0, 0)),
        out_shape=jax.ShapeDtypeStruct((n_ja, 2 * own, block, channels), BF16),
        compiler_params=FIRST,
        cost_estimate=pl.CostEstimate(flops=2**10, bytes_accessed=2**21, transcendentals=0),
    )(pair, cot)


def project_kernel(
    pair_ref,
    cot_ref,
    gain_ref,
    shift_ref,
    w_o_ref,
    w_q_ref,
    w_k_ref,
    w_v_ref,
    w_g_ref,
    kv_n_ref,
    kv_t_ref,
    q_n_ref,
    q_t_ref,
    d_att_ref,
    gate_ref,
):
    n_blocks, group, block, channels = pair_ref.shape
    n = n_blocks * block
    inner = w_q_ref.shape[1]
    weights = [ref[...] for ref in (w_q_ref, w_k_ref, w_v_ref, w_g_ref)]
    w_n = jnp.concatenate(weights[:3], axis=1)
    w_t = jnp.concatenate([w.T for w in weights], axis=0)
    size = lax.axis_size("z")
    z = lax.axis_index("z")
    for r in range(group):
        normed = normalize(pair_ref[:, r].reshape(n, channels), gain_ref[...], shift_ref[...])
        proj = mm(normed, w_n).astype(BF16)
        kv_n_ref[r] = proj[:, inner:]
        proj_t = mm_nt(w_t, normed)
        kv_t_ref[r] = proj_t[inner : 3 * inner].astype(BF16)
        gate = jax.nn.sigmoid(proj_t[3 * inner :])
        gate_ref[r] = gate
        d_att = mm_nt(w_o_ref[...], cot_ref[:, r].reshape(n, channels)) * gate
        for owner in range(n // LANES):
            at = slice(owner * LANES, (owner + 1) * LANES)
            ahead = lax.rem(owner + size - z, size)
            q_n_ref[ahead, r] = proj[at, :inner]
            q_t_ref[ahead, r] = proj_t[:inner, at].astype(BF16)
            d_att_ref[ahead, r] = d_att[:, at]


def project(both, gain, shift_row, w_o, weights):
    n_blocks, slabs, block, channels = both.shape
    rows = slabs // 2
    group = 2
    n = n_blocks * block
    inner = w_o.shape[0]
    kv_n = pltpu.HBM((rows, n, 2 * inner), BF16)
    kv_t = pltpu.HBM((rows, 2 * inner, n), BF16)
    gate = pltpu.HBM((rows, inner, n), F32)
    q_n = pltpu.HBM((n // LANES, rows, LANES, inner), BF16)
    q_t = pltpu.HBM((n // LANES, rows, inner, LANES), BF16)
    d_att = pltpu.HBM((n // LANES, rows, inner, LANES), F32)

    def by_row(a):
        return pl.BlockSpec((group,) + a.shape[1:], lambda i: (i, 0, 0))

    def sliced(a):
        return pl.BlockSpec((a.shape[0], group) + a.shape[2:], lambda i: (0, i, 0, 0))

    return pl.pallas_call(
        project_kernel,
        grid=(rows // group,),
        in_specs=[
            pl.BlockSpec((n_blocks, group, block, channels), lambda i: (0, i, 0, 0)),
            pl.BlockSpec(
                (n_blocks, group, block, channels), lambda i: (0, rows // group + i, 0, 0)
            ),
        ]
        + [whole(a) for a in (gain, shift_row, w_o, *weights)],
        out_specs=[by_row(kv_n), by_row(kv_t)]
        + [sliced(a) for a in (q_n, q_t, d_att)]
        + [by_row(gate)],
        out_shape=[kv_n, kv_t, q_n, q_t, d_att, gate],
        compiler_params=PARAMS,
        cost_estimate=pl.CostEstimate(
            flops=2**31, bytes_accessed=8 * 2**20, transcendentals=2**18
        ),
    )(both, both, gain, shift_row, w_o, *weights)


def z_lanes(ahead):
    at = lax.rem(lax.axis_index("z") + ahead, lax.axis_size("z"))
    return pl.ds(pl.multiple_of(at * LANES, LANES), LANES)


def attend_kernel(heads, count, views, kv_n_hbm, kv_t_hbm, q_n_ref, q_t_ref, d_att_ref, *refs):
    bias_refs = refs[: count * 2 * views]
    refs = refs[count * 2 * views :]
    att_ref, dq_ref, dk_ref, dv_ref, mine_ref, theirs_ref = refs[:6]
    n_ref, t_ref, bias_s, gb_s, s_s, p_s, ds_s, tile_s, line_s, dk_s, dv_s, sems = refs[6:]
    at_slice = pl.program_id(0)
    row_count, n, wide_kv = n_ref.shape
    inner = wide_kv // 2
    head_dim = inner // heads
    scale = 1.0 / math.sqrt(head_dim)
    n_ja = tile_s.shape[0]
    block = n // n_ja
    rows_i = LANES // 4
    pairs = heads // 2
    wide = 2 * LANES
    core = lax.axis_index("core")
    copies = [
        pltpu.make_async_copy(src, dst, sems.at[e])
        for e, (src, dst) in enumerate(((kv_n_hbm, n_ref), (kv_t_hbm, t_ref)))
    ]

    @pl.when(at_slice == 0)
    def _():
        for copy in copies:
            copy.start()
        if count > 1:
            dk_s[...] = jnp.zeros_like(dk_s)
            dv_s[...] = jnp.zeros_like(dv_s)

    def sort_tiles(c):
        for which in range(2):
            base = (c * 2 + which) * views
            parts = []
            for ref in bias_refs[base : base + views]:
                parts += [ref] if len(ref.shape) == 3 else [ref.at[e] for e in range(2)]
            for far, ref in enumerate(parts):
                at = far * 2 + (core ^ which)
                at = pl.ds(pl.multiple_of(at * rows_i, rows_i), rows_i)
                for owner in range(n_ja):
                    for p in range(pairs):
                        tile_s[owner, at, p * LANES : (p + 1) * LANES] = ref[
                            owner, p * rows_i : (p + 1) * rows_i, :
                        ]

    for c in range(count):
        pl.when(at_slice == c)(lambda c=c: sort_tiles(c))
    for owner in range(n_ja):
        for p in range(pairs):
            t = tile_s[owner, :, p * LANES : (p + 1) * LANES].T.astype(F32) * LOG2E
            for e in range(2):
                h = p * 2 + e
                bias_s[owner * block : (owner + 1) * block, h * LANES : (h + 1) * LANES] = t[
                    e * block : (e + 1) * block
                ]

    @pl.when(at_slice == 0)
    def _():
        for copy in copies:
            copy.wait()

    nil = jnp.zeros((), BF16)
    row_head = lax.broadcasted_iota(jnp.int32, (inner, LANES), 0) // head_dim
    lane_head = lax.broadcasted_iota(jnp.int32, (LANES, inner), 1) // head_dim
    step = 16
    held = {}

    def cols_of(p):
        return slice(p * wide, (p + 1) * wide)

    def scores(r, p):
        q_blk = jnp.concatenate(
            [jnp.where(row_head == h, q_t_ref[0, r], nil) for h in (2 * p, 2 * p + 1)], axis=1
        )
        t = mm(n_ref[r, :, :inner], q_blk) * (scale * LOG2E) + bias_s[:, cols_of(p)]
        s_s[r, :, cols_of(p)] = t
        top = t[:8]
        for e in range(8, n, 8):
            top = jnp.maximum(top, t[e : e + 8])
        held["top", r, p] = jnp.max(top, axis=0, keepdims=True)

    def weights(r, p):
        total = jnp.zeros((8, wide), F32)
        for k in range(0, n, step):
            e = jnp.exp2(s_s[r, k : k + step, cols_of(p)] - held["top", r, p])
            s_s[r, k : k + step, cols_of(p)] = e
            p_s[r, k : k + step, cols_of(p)] = e.astype(BF16)
            total = total + (e[:8] + e[8:])
        held["inv", r, p] = 1.0 / jnp.sum(total, axis=0, keepdims=True)

    def attended(r, p):
        first = 2 * p * head_dim
        rows = slice(first, first + 2 * head_dim)
        inv = held["inv", r, p]
        att = mm(t_ref[r, inner + first : inner + first + 2 * head_dim, :], p_s[r, :, cols_of(p)])
        att = att * inv
        d_att = d_att_ref[0, r, rows, :]
        a_two = jnp.concatenate([d_att, d_att], axis=1) * inv
        lane = lax.broadcasted_iota(jnp.int32, a_two.shape, 1) // LANES
        sub = lax.broadcasted_iota(jnp.int32, a_two.shape, 0) // head_dim
        a_two = jnp.where(lane == sub, a_two, 0.0).astype(BF16)
        held["diag", r, p] = jnp.sum(a_two.astype(F32) * att, axis=0, keepdims=True)
        for e in range(2):
            h = 2 * p + e
            att_ref[0, r, h * head_dim : (h + 1) * head_dim, :] = att[
                e * head_dim : (e + 1) * head_dim, e * LANES : (e + 1) * LANES
            ]
        lead = [jnp.zeros((first, wide), BF16)] if p else []
        tail = [jnp.zeros((inner - first - 2 * head_dim, wide), BF16)] if p + 1 < pairs else []
        held["a", r, p] = jnp.concatenate(lead + [a_two] + tail, axis=0)

    def d_scores(r, p):
        dp = mm(n_ref[r, :, inner:], held["a", r, p])
        for k in range(0, n, step):
            ds = s_s[r, k : k + step, cols_of(p)] * (dp[k : k + step] - held["diag", r, p])
            if r == 0:
                gb_s[k : k + step, cols_of(p)] = ds
            else:
                gb_s[k : k + step, cols_of(p)] += ds
            ds_s[r, k : k + step, cols_of(p)] = ds.astype(BF16)

    def d_query(r, p):
        first = 2 * p * head_dim
        dq = mm(t_ref[r, first : first + 2 * head_dim, :], ds_s[r, :, cols_of(p)]) * scale
        for e in range(2):
            h = 2 * p + e
            dq_ref[0, r, h * head_dim : (h + 1) * head_dim, :] = dq[
                e * head_dim : (e + 1) * head_dim, e * LANES : (e + 1) * LANES
            ].astype(BF16)

    def gather(r, p, name, part, sum_s, out_ref, factor):
        if p:
            part = part + held.pop((name, r))
        if p + 1 < pairs:
            held[name, r] = part
            return
        if count > 1:
            part = part + sum_s[r]
            sum_s[r] = part
        out_ref[r] = (part * factor).astype(BF16)

    def d_key(r, p):
        q_row = jnp.concatenate(
            [jnp.where(lane_head == h, q_n_ref[0, r], nil) for h in (2 * p, 2 * p + 1)], axis=0
        )
        gather(r, p, "dk", mm(ds_s[r, :, cols_of(p)], q_row), dk_s, dk_ref, scale)

    def d_value(r, p):
        part = mm(p_s[r, :, cols_of(p)], held["a", r, p].T)
        gather(r, p, "dv", part, dv_s, dv_ref, 1.0)

    order = [
        (scores, 0),
        (scores, 1),
        (weights, 0),
        (attended, 0),
        (weights, 1),
        (d_scores, 0),
        (attended, 1),
        (d_value, 0),
        (d_scores, 1),
        (d_query, 0),
        (d_key, 0),
        (d_value, 1),
        (d_query, 1),
        (d_key, 1),
    ]
    lag = 5
    for t in range(len(order) + lag * (row_count - 1)):
        for r in range(row_count):
            if 0 <= t - lag * r < len(order):
                phase, p = order[t - lag * r]
                phase(r, p)

    for owner in range(n_ja):
        for p in range(pairs):
            t = jnp.concatenate(
                [
                    gb_s[owner * block : (owner + 1) * block, h * LANES : (h + 1) * LANES]
                    for h in (2 * p, 2 * p + 1)
                ],
                axis=0,
            )
            line_s[:, p * LANES : (p + 1) * LANES] = t.astype(BF16).T
        for far in range(2):
            for ref, which in ((mine_ref, core), (theirs_ref, 1 - core)):
                at = pl.multiple_of((far * 2 + which) * rows_i, rows_i)
                for p in range(pairs):
                    ref[0, far, owner, p * rows_i : (p + 1) * rows_i, :] = line_s[
                        pl.ds(at, rows_i), p * LANES : (p + 1) * LANES
                    ]


def attend(heads, aheads, projected, bias):
    rows, n, inner = projected[0].shape
    inner = inner // 2
    count = len(aheads)
    leap = aheads[1] - aheads[0] if count > 1 else 0
    views = len(bias[0][0])
    flat = [a for slice_of in bias for side in slice_of for a in side]
    n_ja, slab, _ = flat[0].shape[-3:]
    lines = heads * n // n_ja
    att = jax.ShapeDtypeStruct((count, rows, inner, LANES), F32)
    dq = jax.ShapeDtypeStruct((count, rows, inner, LANES), BF16)
    grad = jax.ShapeDtypeStruct((rows, n, inner), BF16)
    gb = jax.ShapeDtypeStruct((count, 2, n_ja, slab, LANES), BF16)
    sums = (rows, n, inner) if count > 1 else (1, 8, LANES)

    def by_slice(a):
        return pl.BlockSpec((1,) + a.shape[1:], lambda i: (i,) + (0,) * (len(a.shape) - 1))

    def sliced(a):
        return pl.BlockSpec((1,) + a.shape[1:], lambda i: (aheads[0] + leap * i, 0, 0, 0))

    return pl.pallas_call(
        lambda *refs: attend_kernel(heads, count, views, *refs),
        grid=(count,),
        in_specs=[pl.BlockSpec(memory_space=pl.ANY)] * 2
        + [sliced(a) for a in projected[2:]]
        + [whole(a) for a in flat],
        out_specs=[by_slice(att), by_slice(dq), whole(grad), whole(grad)] + [by_slice(gb)] * 2,
        out_shape=[att, dq, grad, grad, gb, gb],
        scratch_shapes=[
            pltpu.VMEM((rows, n, 2 * inner), BF16),
            pltpu.VMEM((rows, 2 * inner, n), BF16),
            pltpu.VMEM((n, heads * LANES), F32),
            pltpu.VMEM((n, heads * LANES), F32),
            pltpu.VMEM((rows, n, heads * LANES), F32),
            pltpu.VMEM((rows, n, heads * LANES), BF16),
            pltpu.VMEM((rows, n, heads * LANES), BF16),
            pltpu.VMEM((n_ja, LANES, lines), BF16),
            pltpu.VMEM((LANES, lines), BF16),
            pltpu.VMEM(sums, F32),
            pltpu.VMEM(sums, F32),
            pltpu.SemaphoreType.DMA((2,)),
        ],
        compiler_params=WIDE,
        cost_estimate=pl.CostEstimate(
            flops=count * 2**32, bytes_accessed=2**23, transcendentals=count * 2**20
        ),
    )(*in_hbm(*projected), *flat)


def finish_kernel(
    aheads, gate_ref, cot_ref, w_o_ref, w_q_ref, w_k_ref, w_v_ref, w_g_ref, *refs
):
    count = len(aheads)
    att_refs, dq_refs = refs[:count], refs[count : 2 * count]
    dk_refs, dv_refs = refs[2 * count : 3 * count], refs[3 * count : 4 * count]
    out_ref, att_s, dq_s = refs[4 * count :]
    group, inner, n = gate_ref.shape
    for rows, att_ref, dq_ref in zip(aheads, att_refs, dq_refs):
        for c, ahead in enumerate(rows):
            at = z_lanes(ahead)
            for r in range(group):
                att_s[r, :, at] = att_ref[c, r]
                dq_s[r, :, at] = dq_ref[c, r]
    w_t = jnp.concatenate([w_q_ref[...].T, w_g_ref[...].T], axis=0)
    w_n = jnp.concatenate([w_k_ref[...].T, w_v_ref[...].T], axis=0)
    half = (out_ref.shape[0],) + out_ref.shape[2:]
    for r in range(group):
        gate = gate_ref[r]
        d_gated = mm_nt(w_o_ref[...], cot_ref[:, r].reshape(n, cot_ref.shape[3]))
        att = att_s[r]
        update = mm_tn((gate * att).astype(BF16), w_o_ref[...])
        out_ref[:, 2 * r] = update.astype(BF16).reshape(half)
        d_gate = (d_gated * att * gate * (1.0 - gate)).astype(BF16)
        left_t = jnp.concatenate([dq_s[r], d_gate], axis=0)
        dk = sum(ref[r].astype(F32) for ref in dk_refs).astype(BF16)
        dv = sum(ref[r].astype(F32) for ref in dv_refs).astype(BF16)
        dn = mm_tn(left_t, w_t) + mm(jnp.concatenate([dk, dv], axis=1), w_n)
        out_ref[:, 2 * r + 1] = dn.astype(BF16).reshape(half)


def finish(aheads, gate, both, w_o, weights, att, dq, dk, dv):
    n_blocks, _, block, channels = both.shape
    rows, inner, n = gate.shape
    group = 2
    arrays = (*att, *dq, *dk, *dv)

    def by_row(a):
        return pl.BlockSpec((group,) + a.shape[1:], lambda i: (i, 0, 0))

    def by_slices(a):
        return pl.BlockSpec((a.shape[0], group) + a.shape[2:], lambda i: (0, i, 0, 0))

    return pl.pallas_call(
        lambda *refs: finish_kernel(aheads, *refs),
        grid=(rows // group,),
        in_specs=[
            by_row(gate),
            pl.BlockSpec(
                (n_blocks, group, block, channels), lambda i: (0, rows // group + i, 0, 0)
            ),
            whole(w_o),
        ]
        + [whole(a) for a in weights]
        + [by_slices(a) for a in (*att, *dq)]
        + [by_row(a) for a in (*dk, *dv)],
        out_specs=pl.BlockSpec((n_blocks, 2 * group, block, channels), lambda i: (0, i, 0, 0)),
        out_shape=jax.ShapeDtypeStruct((n_blocks, 2 * rows + 1, block, channels), BF16),
        scratch_shapes=[
            pltpu.VMEM((group, inner, n), F32),
            pltpu.VMEM((group, inner, n), BF16),
        ],
        compiler_params=PARAMS,
        cost_estimate=pl.CostEstimate(flops=2**31, bytes_accessed=2**23, transcendentals=0),
    )(*in_hbm(gate), both, w_o, *weights, *arrays)


def halves_kernel(parts, *refs):
    xh = lax.axis_index("xh")
    keep_ref, send_ref = refs[parts:]
    for far, out in ((0, keep_ref), (1, send_ref)):
        out[...] = sum(ref[xh ^ far].astype(F32) for ref in refs[:parts]).astype(BF16)


def halves(*arrays):
    out = jax.ShapeDtypeStruct(arrays[0].shape[1:], BF16)
    return pl.pallas_call(
        lambda *refs: halves_kernel(len(arrays), *refs),
        out_shape=[out] * 2,
        compiler_params=PARAMS,
        cost_estimate=pl.CostEstimate(flops=2**18, bytes_accessed=2**20, transcendentals=0),
    )(*arrays)


def fill_kernel(done_ref, a_ref, b_ref, out_ref):
    del done_ref
    out_ref[:, 0] = (a_ref[...].astype(F32) + b_ref[...].astype(F32)).astype(BF16)


def fill(done, *parts):
    n_ja, slabs, block, channels = done.shape
    spec = pl.BlockSpec((n_ja, 1, block, channels), lambda i: (0, slabs - 1, 0, 0))
    return pl.pallas_call(
        fill_kernel,
        grid=(1,),
        in_specs=[pl.BlockSpec(memory_space=pl.ANY)] + [whole(a) for a in parts],
        out_specs=spec,
        out_shape=jax.ShapeDtypeStruct(done.shape, BF16),
        input_output_aliases={0: 0},
        compiler_params=PARAMS,
        cost_estimate=pl.CostEstimate(flops=2**18, bytes_accessed=2**20, transcendentals=0),
    )(done, *parts)


def final_kernel(
    pair_ref, both_ref, gb_ref, gain_ref, shift_ref, w_ref, update_ref, out_ref, tile_s
):
    rows, block, channels = pair_ref.shape
    group, slabs = both_ref.shape[:2]
    own = slabs // 2
    step = pl.program_id(0)

    @pl.when(step == 0)
    def _():
        tile = jnp.sum(gb_ref[:, 0].astype(F32), axis=0)
        half = tile.shape[0] // 2
        tile = jnp.concatenate([tile[:half], tile[half:]], axis=1).astype(BF16).astype(F32)
        for e in range(tile_s.shape[0]):
            tile_s[e] = tile[e * rows : (e + 1) * rows]

    tile = tile_s[step]
    keep = line_mask(block, tile.shape[1])
    spread = jnp.concatenate(
        [
            jnp.where(keep, jnp.broadcast_to(tile[i : i + 1], keep.shape), 0.0).astype(BF16)
            for i in range(rows)
        ],
        axis=0,
    )
    back = mm(spread, spread_heads(w_ref, block))
    dn = [both_ref[d, 2 * i + 1] for d in range(group) for i in range(own)]
    dn = jnp.concatenate(dn, axis=0).astype(F32) + back
    for d in range(group):
        for i in range(own):
            update_ref[d * own + i] = both_ref[d, 2 * i]
    centred, rstd = centre(pair_ref[...].reshape(rows * block, channels))
    unit = centred * rstd
    push = dn * gain_ref[...]
    along = jnp.mean(push * unit, axis=-1, keepdims=True)
    level = jnp.mean(push, axis=-1, keepdims=True)
    out_ref[...] = ((push - level - unit * along) * rstd).reshape(out_ref.shape)


def final(pair, both, gain, shift_row, bias_weight):
    n_ja, slabs, block, channels = both.shape
    group = 4
    steps = n_ja // group
    rows = pair.shape[0] // steps
    by_rows = pl.BlockSpec((rows, block, channels), lambda i: (i, 0, 0))
    return pl.pallas_call(
        final_kernel,
        grid=(steps,),
        in_specs=[
            by_rows,
            pl.BlockSpec((group, slabs, block, channels), lambda i: (i, 0, 0, 0)),
            pl.BlockSpec((n_ja, 1, block, channels), lambda i: (0, slabs - 1, 0, 0)),
        ]
        + [whole(a) for a in (gain, shift_row, bias_weight)],
        out_specs=[by_rows, by_rows],
        out_shape=[
            jax.ShapeDtypeStruct(pair.shape, BF16),
            jax.ShapeDtypeStruct(pair.shape, F32),
        ],
        scratch_shapes=[pltpu.VMEM((steps, rows, bias_weight.shape[0] * block), F32)],
        compiler_params=PARAMS,
        cost_estimate=pl.CostEstimate(
            flops=2**27, bytes_accessed=2**21, transcendentals=2**12
        ),
    )(pair, both, both, gain, shift_row, bias_weight)


def shards(
    pair,
    cotangent,
    norm_gain,
    norm_shift,
    query_weight,
    key_weight,
    value_weight,
    gate_weight,
    bias_weight,
    out_weight,
):
    rows_i, rows_j, channels = pair.shape
    heads = bias_weight.shape[1]
    n_ja = lax.axis_size(JA)
    own_i = rows_i // n_ja
    gain = norm_gain.reshape(1, channels)
    shift_row = norm_shift.reshape(1, channels)
    bias_rows = bias_weight.T
    weights = (query_weight, key_weight, value_weight, gate_weight)
    tie = lax.optimization_barrier

    n_xh = lax.axis_size("xh")
    tile = prep(pair, gain, shift_row, bias_rows, n_xh * n_ja)
    both = pack(pair, cotangent, n_ja)
    near = lax.all_to_all(tile, ("xh",) + JA, 0, 0, tiled=True)
    near, both = tie((near, both))
    near = near.reshape((n_xh, n_ja) + near.shape[1:])
    both = lax.all_to_all(both, JA, 0, 0, tiled=True)

    def joined(mine, theirs):
        return (mine.astype(F32) + theirs.astype(F32)).astype(BF16)

    slices = [shift(near, "z", 3), shift(near, "z", 2), shift(near, "z", 1)]
    swaps = [swap(a) for a in slices]
    near_swap = swap(near)
    projected = project(both, gain, shift_row, out_weight, weights)
    projected, slices, swaps = tie((projected, slices, swaps))
    *projected, gate = projected

    groups = ((1, 2, 3), (0,))
    out1 = attend(heads, groups[0], projected, [([a], [b]) for a, b in zip(slices, swaps)])
    theirs1 = swap(out1[5])
    theirs1, near = tie((theirs1, near))
    part = joined(out1[4], theirs1)
    part, near = tie((part, near))
    parts = [shift(part[e], "z", e + 1) for e in range(3)]
    out0 = attend(heads, groups[1], projected, [([near], [near_swap])])
    att, dq, dk, dv = zip(out1[:4], out0[:4])
    done = finish(groups, gate, both, out_weight, weights, att, dq, dk, dv)
    theirs0 = swap(out0[5])
    done, parts, theirs0 = tie((done, parts, theirs0))
    keep, send = halves(out0[4][0], theirs0[0], *parts)
    send = lax.ppermute(send, "xh", [(0, 1), (1, 0)])
    done = fill(done, keep, send)
    done = lax.all_to_all(done, JA, 0, 0, tiled=True)
    update, pair_grad = final(pair, done, gain, shift_row, bias_rows)
    return (update, pair_grad)


def solution(mesh):
    fine = Mesh(mesh.devices.reshape(4, 2, 2, 4, 2), IA + JA)
    spec = P(IA, JA, None)
    in_specs = (spec, spec) + (P(),) * 8
    return jax.shard_map(
        shards, mesh=fine, in_specs=in_specs, out_specs=(spec, spec), check_vma=False
    )
```
